32 devices in a mesh: dp: 4 (over y, core), fsdp: 8 (over z, x).
Axes of the slice: x: 2, y: 2, z: 4, core: 2. Of those that a mesh axis runs over, the one named last changes fastest.
Arguments:
- patches: bfloat16 [32, 768, 768], P(('dp', 'fsdp')), may hold values from -6 to 6
- positions: int32 [32, 768], P(('dp', 'fsdp')), may hold values from 0 to 198, as said below
- segments: int32 [32, 768], P(('dp', 'fsdp')), may hold values from 0 to 15, as said below
- labels: int32 [32, 15], P(('dp', 'fsdp')), may hold values from 0 to 999
- teacher: int32 [32, 15], P(('dp', 'fsdp')), may hold values from 0 to 999
- layer_master: float32 [2, 1802240], P(None, ('dp', 'fsdp'))
- layer_moment: float32 [2, 1802240], P(None, ('dp', 'fsdp'))
- layer_second: float32 [2, 1802240], P(None, ('dp', 'fsdp'))
- global_master: float32 [1146880], P(('dp', 'fsdp'))
- global_moment: float32 [1146880], P(('dp', 'fsdp'))
- global_second: float32 [1146880], P(('dp', 'fsdp'))
Outputs:
- new_layer_master: float32 [2, 1802240], P(None, ('dp', 'fsdp'))
- new_layer_moment: float32 [2, 1802240], P(None, ('dp', 'fsdp'))
- new_layer_second: float32 [2, 1802240], P(None, ('dp', 'fsdp'))
- new_global_master: float32 [1146880], P(('dp', 'fsdp'))
- new_global_moment: float32 [1146880], P(('dp', 'fsdp'))
- new_global_second: float32 [1146880], P(('dp', 'fsdp'))
- grad_norm: float32 [], replicated
- loss_sum: float32 [], replicated
The draws below stay inside these ranges and needn't reach their ends.
Inputs may be any that keep to these rules, and one draw needn't show every extreme that they name: `positions`: in each sequence 15 images of 51 tokens stand in order, with the remaining tokens as padding before, between or after them; an image's first token has position 196, its second 196 + 1, the others rows of the 14 x 14 table in a 7 x 7 window, row by row; padding has position 198. `segments`: the number of a token's image in its sequence, counting from 0 in order; padding tokens have 15.
All inputs are finite; a program needn't handle non-finite values.
Results may differ from the reference program's by a relative error of at most 0.012.
Values may be sent and summed in bfloat16 or wider, within the bound.
A program may use at most 192 MiB of HBM per device.

```python
import math
import jax
import jax.numpy as jnp
from jax import lax

D = 384
HEADS = 6
HEAD_DIM = 64
FF = 1536
CLASSES = 1000
PATCH = 768
TABLE = 196
LAYERS = 2
IMAGES = 15
IMG_TOKENS = 51
SEQ = 768
STEP = 10
SEQS = 32
PL = 1802240
PG = 1146880


clip_norm = 0.01


vector_state = 0.15


def packing(key):
    key_gap, key_row, key_col = jax.random.split(key, 3)
    spare = SEQ - IMAGES * IMG_TOKENS
    slot_pick = jax.random.randint(key_gap, (SEQS, spare), 0, IMAGES + 1)
    gap_sizes = jnp.sum((slot_pick[:, :, None] == jnp.arange(IMAGES + 1)[None, None, :]).astype(jnp.int32), axis=1)
    pads_before = jnp.cumsum(gap_sizes, axis=1)[:, :IMAGES]
    image_start = jnp.arange(IMAGES, dtype=jnp.int32)[None, :] * IMG_TOKENS + pads_before
    offset = jnp.arange(SEQ, dtype=jnp.int32)[None, :, None] - image_start[:, None, :]
    within = (offset >= 0) & (offset < IMG_TOKENS)
    which_image = jnp.sum(jnp.where(within, jnp.arange(IMAGES, dtype=jnp.int32)[None, None, :], 0), axis=-1)
    any_image = jnp.any(within, axis=-1)
    token_place = jnp.sum(jnp.where(within, offset, 0), axis=-1)
    row_start = jax.random.randint(key_row, (SEQS, IMAGES), 0, 8)
    col_start = jax.random.randint(key_col, (SEQS, IMAGES), 0, 8)
    row_first = jnp.take_along_axis(row_start, which_image, axis=1)
    col_first = jnp.take_along_axis(col_start, which_image, axis=1)
    patch_index = jnp.maximum(token_place - 2, 0)
    grid_pos = (row_first + patch_index // 7) * 14 + col_first + patch_index % 7
    positions = jnp.where(token_place == 0, TABLE, jnp.where(token_place == 1, TABLE + 1, grid_pos))
    positions = jnp.where(any_image, positions, TABLE + 2).astype(jnp.int32)
    segments = jnp.where(any_image, which_image, IMAGES).astype(jnp.int32)
    return (positions, segments)


def draw_positions(key, part):
    return packing(key)[0]


def draw_segments(key, part):
    return packing(key)[1]


def layer_profile():
    return [(3 * D * D, D ** (-0.5), 0.0), (D * D, 4.0 * D ** (-0.5), 0.0), (D * FF, D ** (-0.5), 0.0), (FF * D, FF ** (-0.5), 0.0), (D, 0.1, 1.0), (D, 0.3, 0.0), (D, 0.5, 0.0), (D, 0.3, 0.0), (D, 0.3, 0.0), (D, 0.1, 1.0), (D, 0.3, 0.0), (FF, 0.3, 0.0), (D, 0.3, 0.0)]


def global_profile():
    return [(PATCH * D, PATCH ** (-0.5), 0.0), ((TABLE + 2) * D, 1.0, 0.0), (D, 0.3, 0.0), (D, 0.1, 1.0), (D, 0.3, 0.0), (2 * D * CLASSES, 2.0 * D ** (-0.5), 0.0), (2 * CLASSES, 0.5, 0.0)]


def flat_profile(profile, total):
    used = sum((entries for entries, spread_value, center_value in profile))
    spreads = [jnp.full((entries,), spread_value, jnp.float32) for entries, spread_value, center_value in profile]
    centers = [jnp.full((entries,), center_value, jnp.float32) for entries, spread_value, center_value in profile]
    spreads.append(jnp.ones((total - used,), jnp.float32))
    centers.append(jnp.zeros((total - used,), jnp.float32))
    return (jnp.concatenate(spreads), jnp.concatenate(centers))


def layer_state_scale():
    matrix_entries = 4 * D * D + 2 * D * FF
    vector_entries = 8 * D + FF
    return jnp.concatenate([jnp.ones((matrix_entries,), jnp.float32), jnp.full((vector_entries,), vector_state, jnp.float32), jnp.ones((PL - matrix_entries - vector_entries,), jnp.float32)])


def grad_size():
    return clip_norm / math.sqrt(LAYERS * PL + PG)


def draw_layer_master(key, part):
    key = jax.random.fold_in(key, 11)
    base = jax.random.normal(key, (LAYERS, PL), jnp.float32)
    spreads, centers = flat_profile(layer_profile(), PL)
    return base * spreads[None, :] + centers[None, :]


def draw_global_master(key, part):
    key = jax.random.fold_in(key, 12)
    base = jax.random.normal(key, (PG,), jnp.float32)
    spreads, centers = flat_profile(global_profile(), PG)
    return base * spreads + centers


def draw_layer_moment(key, part):
    key = jax.random.fold_in(key, 13)
    scales = layer_state_scale()[None, :]
    return jax.random.normal(key, (LAYERS, PL), jnp.float32) * (0.111 * grad_size()) * scales


def draw_global_moment(key, part):
    key = jax.random.fold_in(key, 14)
    return jax.random.normal(key, (PG,), jnp.float32) * (0.111 * grad_size())


def draw_layer_second(key, part):
    key = jax.random.fold_in(key, 15)
    logs = jax.random.uniform(key, (LAYERS, PL), jnp.float32, math.log(0.0005), math.log(0.008))
    scales = layer_state_scale()[None, :]
    return jnp.exp(logs) * grad_size() ** 2 * scales * scales


def draw_global_second(key, part):
    key = jax.random.fold_in(key, 16)
    logs = jax.random.uniform(key, (PG,), jnp.float32, math.log(0.0005), math.log(0.008))
    return jnp.exp(logs) * grad_size() ** 2


def place_ends(drawn, own_key, smallest, top_value):
    extent = drawn.shape
    index_at = [jax.random.randint(jax.random.fold_in(own_key, axis), (), 0, extent[axis]) for axis in range(len(extent))]
    drawn = drawn.at[tuple(index_at)].set(smallest)
    longest = extent.index(max(extent))
    index_at[longest] = (index_at[longest] + 1) % extent[longest]
    return drawn.at[tuple(index_at)].set(top_value)


def block_scale(rng, shape, cuts, least, largest):
    def one(position, shards_of):
        steps = jax.random.uniform(jax.random.fold_in(jax.random.fold_in(rng, 6), position), (shards_of,), jnp.float32, least / len(cuts), largest / len(cuts))
        return jnp.repeat(jnp.exp(steps), shape[position] // shards_of).reshape((-1,) + (1,) * (len(shape) - position - 1))

    factor_of = one(*cuts[0])
    for cut in cuts[1:]:
        factor_of = factor_of * one(*cut)
    return factor_of


def bell_draw(own_key, dims, scale, most, cuts=(), kind=jnp.bfloat16):
    level = block_scale(own_key, dims, cuts, -0.22, 0.18) if cuts else 1.0
    array = jax.random.normal(own_key, dims, jnp.float32) * scale * level
    return jnp.minimum(jnp.maximum(array, -most), most).astype(kind)


def setup_inputs(seed: int = 0) -> dict:
    splits = jax.random.split(jax.random.key(seed), 12)
    return {
        "patches": bell_draw(splits[0], (SEQS, SEQ, PATCH), 1.0, 6.0, ((0, 32),)),
        "positions": draw_positions(jax.random.fold_in(splits[11], 71), 0),
        "segments": draw_segments(jax.random.fold_in(splits[11], 71), 0),
        "labels": place_ends(jax.random.randint(splits[3], (SEQS, IMAGES), 0, CLASSES), jax.random.fold_in(splits[3], 1), 0, CLASSES - 1).astype(jnp.int32),
        "teacher": place_ends(jax.random.randint(splits[4], (SEQS, IMAGES), 0, CLASSES), jax.random.fold_in(splits[4], 1), 0, CLASSES - 1).astype(jnp.int32),
        "layer_master": draw_layer_master(jax.random.fold_in(splits[11], 71), 0),
        "layer_moment": draw_layer_moment(jax.random.fold_in(splits[11], 71), 0),
        "layer_second": draw_layer_second(jax.random.fold_in(splits[11], 71), 0),
        "global_master": draw_global_master(jax.random.fold_in(splits[11], 71), 0),
        "global_moment": draw_global_moment(jax.random.fold_in(splits[11], 71), 0),
        "global_second": draw_global_second(jax.random.fold_in(splits[11], 71), 0),
    }


@jax.custom_vjp
def low(v):
    return lax.optimization_barrier(v.astype(jnp.bfloat16)).astype(jnp.float32)

@jax.custom_vjp
def low_back(v):
    return v

def low_keep(v):
    return (low(v), None)

def low_pass(kept, grad):
    return (grad,)

def back_keep(v):
    return (v, None)

def back_low(kept, grad):
    return (low(grad),)
low.defvjp(low_keep, low_pass)
low_back.defvjp(back_keep, back_low)
norm_eps = 1e-06
beta_one = 0.9
beta_two = 0.999
adam_eps = 1e-08
learn_rate = 0.1
weight_decay = 0.05
clip_norm = 0.01
mask_fill = -1000000000.0
highest = lax.Precision.HIGHEST

def layer_plan():
    return [('w_qkv', (D, 3 * D)), ('w_proj', (D, D)), ('w_fc1', (D, FF)), ('w_fc2', (FF, D)), ('pre_gain', (D,)), ('pre_bias', (D,)), ('query_bias', (D,)), ('value_bias', (D,)), ('proj_bias', (D,)), ('mid_gain', (D,)), ('mid_bias', (D,)), ('fc1_bias', (FF,)), ('fc2_bias', (D,))]

def global_plan():
    return [('w_patch', (PATCH, D)), ('pos_table', (TABLE + 2, D)), ('patch_bias', (D,)), ('final_gain', (D,)), ('final_bias', (D,)), ('w_head', (D, 2 * CLASSES)), ('head_bias', (2 * CLASSES,))]

def unpack(flat_rows, plan):
    pieces = {}
    offset = 0
    for label_name, dimensions in plan:
        entries = math.prod(dimensions)
        pieces[label_name] = flat_rows[offset:offset + entries].reshape(dimensions)
        offset += entries
    return pieces

def layer_norm(stream, gain_vec, bias_vec):
    center = stream - lax.optimization_barrier(jnp.mean(stream, axis=-1, keepdims=True))
    spread = lax.optimization_barrier(jnp.mean(center * center, axis=-1, keepdims=True))
    return center * lax.rsqrt(spread + norm_eps) * gain_vec + bias_vec

def matmul(left, right):
    return jnp.dot(left, right, precision=highest, preferred_element_type=jnp.float32)

def layer_forward(stream, weights, same_image):
    normed = low(layer_norm(stream, weights['pre_gain'], weights['pre_bias']))
    zeros_mid = jnp.zeros_like(weights['query_bias'])
    qkv_bias = jnp.concatenate([weights['query_bias'], zeros_mid, weights['value_bias']])
    projected = low(low_back(matmul(normed, weights['w_qkv']) + qkv_bias))
    queries = projected[:, :D].reshape(SEQ, HEADS, HEAD_DIM)
    key_rows = projected[:, D:2 * D].reshape(SEQ, HEADS, HEAD_DIM)
    value_rows = projected[:, 2 * D:].reshape(SEQ, HEADS, HEAD_DIM)
    scores = jnp.einsum('qhd,khd->hqk', queries, key_rows, precision=highest) * HEAD_DIM ** (-0.5)
    scores = low_back(jnp.where(same_image[None], scores, mask_fill))
    softened = jax.nn.softmax(scores, axis=-1)
    attended = jnp.einsum('hqk,khd->qhd', low(softened), value_rows, precision=highest).reshape(SEQ, D)
    branch_out = low_back(matmul(low(low_back(attended)), weights['w_proj']) + weights['proj_bias'])
    middle = stream + branch_out
    normed_mid = low(layer_norm(middle, weights['mid_gain'], weights['mid_bias']))
    hidden_pre = low_back(matmul(normed_mid, weights['w_fc1']) + weights['fc1_bias'])
    activated = low(jax.nn.gelu(hidden_pre, approximate=False))
    return middle + low_back(matmul(activated, weights['w_fc2']) + weights['fc2_bias'])

def sequence_loss(layer_rows, global_rows, patches, positions, segments, labels, teacher):
    parts = unpack(low(global_rows), global_plan())
    onehot = (positions[:, None] == jnp.arange(TABLE + 2)[None, :]).astype(jnp.float32)
    is_patch = (positions < TABLE).astype(jnp.float32)[:, None]
    projected = low_back(matmul(patches, parts['w_patch']) + parts['patch_bias'])
    stream = matmul(onehot, parts['pos_table']) + is_patch * projected
    same_image = segments[:, None] == segments[None, :]
    rounded = low(layer_rows)
    for depth in range(LAYERS):
        stream = jax.checkpoint(layer_forward)(stream, unpack(rounded[depth], layer_plan()), same_image)
    image_ids = jnp.arange(IMAGES)
    in_image = segments[None, :] == image_ids[:, None]
    picker = jnp.concatenate([in_image & (positions[None, :] == TABLE), in_image & (positions[None, :] == TABLE + 1)], axis=0).astype(jnp.float32)
    summary = low(layer_norm(matmul(picker, stream), parts['final_gain'], parts['final_bias']))
    head_rows = parts['w_head']
    head_shift = parts['head_bias']
    logit_class = low_back(matmul(summary[:IMAGES], head_rows[:, :CLASSES]) + head_shift[:CLASSES])
    logit_dist = low_back(matmul(summary[IMAGES:], head_rows[:, CLASSES:]) + head_shift[CLASSES:])
    logits = jnp.concatenate([logit_class, logit_dist], axis=0)
    targets = jnp.concatenate([labels, teacher])
    target_hits = (targets[:, None] == jnp.arange(CLASSES)[None, :]).astype(jnp.float32)
    return jnp.sum(jax.nn.logsumexp(logits, axis=-1) - lax.optimization_barrier(jnp.sum(logits * target_hits, axis=-1)))

def adam_update(master, moment, second, gradient, factor):
    clipped = gradient * factor
    new_moment = beta_one * moment + (1.0 - beta_one) * clipped
    new_second = beta_two * second + (1.0 - beta_two) * clipped * clipped
    fix_one = 1.0 - beta_one ** STEP
    fix_two = 1.0 - beta_two ** STEP
    update = new_moment / fix_one / (jnp.sqrt(new_second / fix_two) + adam_eps) + weight_decay * master
    return (master - learn_rate * update, new_moment, new_second)

def reference(patches, positions, segments, labels, teacher, layer_master, layer_moment, layer_second, global_master, global_moment, global_second):
    loss_scale = 1.0 / (2 * IMAGES * SEQS)

    def one_sequence(carry, data):
        layer_acc, global_acc, total = carry
        pixel_rows, pos_rows, seg_rows, label_rows, teacher_rows = data

        def loss_of(layer_rows, global_rows):
            return sequence_loss(layer_rows, global_rows, pixel_rows.astype(jnp.float32), pos_rows, seg_rows, label_rows, teacher_rows)
        value, pull = jax.vjp(loss_of, layer_master, global_master)
        layer_grad, global_grad = pull(jnp.ones_like(value) * loss_scale)
        return ((layer_acc + layer_grad, global_acc + global_grad, total + value), None)
    start = (jnp.zeros_like(layer_master), jnp.zeros_like(global_master), jnp.zeros((), jnp.float32))
    (layer_grad, global_grad, loss_sum), _ = lax.scan(one_sequence, start, (patches, positions, segments, labels, teacher))
    squares = jnp.sum(layer_grad * layer_grad) + jnp.sum(global_grad * global_grad)
    grad_norm = jnp.sqrt(squares)
    factor = jnp.minimum(1.0, clip_norm / grad_norm)
    new_layer = adam_update(layer_master, layer_moment, layer_second, layer_grad, factor)
    new_global = adam_update(global_master, global_moment, global_second, global_grad, factor)
    return (new_layer[0], new_layer[1], new_layer[2], new_global[0], new_global[1], new_global[2], grad_norm, loss_sum)
```

```python
import functools

import jax
import jax.numpy as jnp
from jax import lax
from jax.experimental import pallas as pl
from jax.experimental.pallas import tpu as pltpu
from jax.sharding import PartitionSpec as P

D = 384
HEADS = 6
HEAD_DIM = 64
FF = 1536
CLASSES = 1000
PATCH = 768
TABLE = 196
IMAGES = 15
SEQ = 768
STEP = 10
LANES = 128
PARTS = 32

NORM_EPS = 1e-06
BETA_ONE = 0.9
BETA_TWO = 0.999
ADAM_EPS = 1e-08
LEARN_RATE = 0.1
WEIGHT_DECAY = 0.05
CLIP_NORM = 0.01
MASK_FILL = -1000000000.0
SCORE_SCALE = HEAD_DIM ** (-0.5)
LOW = jnp.bfloat16
FULL = jnp.float32
HIGHEST = lax.Precision.HIGHEST

QKV_AT, PROJ_AT, FC1_AT, FC2_AT = 0, 3456, 4608, 9216
PRE_GAIN_AT, PRE_BIAS_AT, QUERY_BIAS_AT, VALUE_BIAS_AT = 13824, 13827, 13830, 13833
PROJ_BIAS_AT, MID_GAIN_AT, MID_BIAS_AT, FC1_BIAS_AT, FC2_BIAS_AT = 13836, 13839, 13842, 13845, 13857
LAYER_END = 13860
PATCH_AT, POS_AT, PATCH_BIAS_AT, FINAL_GAIN_AT, FINAL_BIAS_AT = 0, 2304, 2898, 2901, 2904
HEAD_AT, HEAD_BIAS_AT, GLOBAL_END = 2907, 8907, 8923
GROUP, GROUP_ROWS, GROUPS = 8, 125, 48
HEAD_LANES = 2048
PICKED = 32
WINDOWS, WINDOW = 8, 128
ROWS = 256
LAYER_ROWS, GLOBAL_ROWS = 440, 280


def dot(a, b, dims=(1, 0), precision=None):
    return lax.dot_general(
        a, b, (((dims[0],), (dims[1],)), ((), ())), precision=precision, preferred_element_type=FULL
    )


def dot_nt(a, b, precision=None):
    return dot(a, b, (1, 1), precision)


def dot_tn(a, b, precision=None):
    return dot(a, b, (0, 0), precision)


def row_mean(x):
    return jnp.sum(x, axis=-1, keepdims=True) * (1.0 / D)


def normalise(x):
    center = x - row_mean(x)
    inverse = lax.rsqrt(row_mean(center * center) + NORM_EPS)
    return center * inverse, inverse


def norm_back(grad, gain, unit, inverse):
    scaled = grad * gain
    return inverse * (scaled - row_mean(scaled) - unit * row_mean(scaled * unit))


def col_sum(x):
    return jnp.sum(x.astype(FULL), axis=0, keepdims=True)


def gelu_parts(x):
    size = jnp.abs(x)
    bell = jnp.exp(-0.5 * x * x)
    base = 1.0 + (0.3275911 * 0.7071067811865476) * size
    t = pl.reciprocal(base, approx=True)
    t = t * (2.0 - base * t)
    tail = ((((1.061405429 * t - 1.453152027) * t + 1.421413741) * t - 0.284496736) * t + 0.254829592) * t
    tail = 0.5 * tail * bell
    phi = jnp.where(x < 0, tail, 1.0 - tail)
    return x * phi, phi + x * (bell * 0.3989422804014327)


def step_kernel(
    loss_scale,
    pat, pos, seg, lab, tea, a0, a1, ag,
    g0, g1, gg, loss,
    b0, b1, bg, flat, flatg, wqkv, wproj, wfc1, wfc2, wpat, wpos, whead, vecs,
    pos_col, seg_col, unit_a, inv_a, h_a, unit_b, inv_b, h_b, qkv, probs, att, attl, x0, x1, dgelu, act, gpre,
    kv, low, sems,
):
    head_of_lane = lax.broadcasted_iota(jnp.int32, (1, LANES), 1) // HEAD_DIM

    loads = [
        pltpu.make_async_copy(src, dst, sems.at[i]) for i, (src, dst) in enumerate(((ag, bg), (a0, b0), (a1, b1)))
    ]
    for load in loads:
        load.start()

    def spread(buf, flat, rows):
        def one(s, carry):
            flat[pl.ds(pl.multiple_of(s * rows, 8), rows), :] = buf[s, :rows, :].astype(FULL)
            return carry

        lax.fori_loop(0, PARTS, one, 0)

    def gather_rows(buf, flat, rows):
        def one(s, carry):
            buf[s, :rows, :] = flat[pl.ds(pl.multiple_of(s * rows, 8), rows), :].astype(LOW)
            return carry

        lax.fori_loop(0, PARTS, one, 0)

    def take(flat, dst, at, rows, width):
        count = width // LANES

        def one(c, carry):
            value = flat[pl.ds(at + c, rows, stride=count), :].astype(LOW)
            dst[:rows, pl.ds(pl.multiple_of(c * LANES, LANES), LANES)] = value
            return carry

        lax.fori_loop(0, count, one, 0)

    def take_row(flat, at, width):
        return jnp.concatenate([flat[at + i : at + i + 1, :] for i in range(width // LANES)], axis=1)

    def put_row(at, value, flat=flat):
        for i in range(value.shape[1] // LANES):
            flat[at + i : at + i + 1, :] = value[:, i * LANES : (i + 1) * LANES]

    def put(at, start, width, value, first=0, flat=flat):
        count = width // LANES
        rows = value.shape[0]
        for i in range(value.shape[1] // LANES):
            flat[pl.ds(at + start * count + first + i, rows, stride=count), :] = value[:, i * LANES : (i + 1) * LANES]

    for i in range(SEQ // LANES):
        lanes = slice(i * LANES, (i + 1) * LANES)
        for src, dst in ((pos, pos_col), (seg, seg_col)):
            dst[lanes, :] = jnp.transpose(jnp.broadcast_to(src[0:1, lanes].astype(FULL), (LANES, LANES)))
    pos_row = pos[0:1, :]
    seg_row = seg[0:1, :]
    picked_row = lax.broadcasted_iota(jnp.int32, (PICKED, 1), 0)
    picked_image = jnp.where(picked_row < IMAGES, picked_row, picked_row - IMAGES)
    picked_image = jnp.where(picked_row < 2 * IMAGES, picked_image, -1)
    picked_place = jnp.where(picked_row < IMAGES, TABLE, TABLE + 1)
    picker = ((seg_row == picked_image) & (pos_row == picked_place)).astype(FULL)
    picker_low = picker.astype(LOW)

    loads[0].wait()
    spread(bg, flatg, GLOBAL_ROWS)
    take(flatg, wpat, PATCH_AT, PATCH, D)
    take(flatg, wpos, POS_AT, TABLE + 2, D)
    wpos[TABLE + 2 :, :] = jnp.zeros((wpos.shape[0] - TABLE - 2, D), LOW)

    def take_head(j, carry):
        value = flatg[pl.ds(HEAD_AT + j, GROUPS, stride=GROUP_ROWS), :].astype(LOW)
        whead[:, pl.ds(pl.multiple_of(j * LANES, LANES), LANES)] = value
        return carry

    lax.fori_loop(0, GROUP_ROWS, take_head, 0)
    whead[:, GROUP_ROWS * LANES :] = jnp.zeros((GROUPS, LANES), LOW)
    patch_bias = take_row(flatg, PATCH_BIAS_AT, D)
    final_gain = take_row(flatg, FINAL_GAIN_AT, D)
    final_bias = take_row(flatg, FINAL_BIAS_AT, D)
    head_bias = take_row(flatg, HEAD_BIAS_AT, HEAD_LANES)

    row_at = (
        (PRE_GAIN_AT, D), (PRE_BIAS_AT, D), (QUERY_BIAS_AT, D), (VALUE_BIAS_AT, D), (PROJ_BIAS_AT, D),
        (MID_GAIN_AT, D), (MID_BIAS_AT, D), (FC1_BIAS_AT, FF), (FC2_BIAS_AT, D),
    )

    def take_layer(n, buf):
        spread(buf, flat, LAYER_ROWS)
        take(flat, wqkv.at[n], QKV_AT, D, 3 * D)
        take(flat, wproj.at[n], PROJ_AT, D, D)
        take(flat, wfc1.at[n], FC1_AT, D, FF)
        take(flat, wfc2.at[n], FC2_AT, FF, D)
        for i, (at, width) in enumerate(row_at):
            vecs[n, i : i + 1, :width] = take_row(flat, at, width)

    def vec(n, i):
        return vecs[n, i : i + 1, : row_at[i][1]]

    loads[1].wait()
    take_layer(0, b0)

    def tile_rows(i):
        return pl.ds(pl.multiple_of(i * ROWS, ROWS), ROWS)

    def onehot_of(place):
        iota = lax.broadcasted_iota(jnp.int32, (1, wpos.shape[0]), 1).astype(FULL)
        return (place == iota).astype(LOW)

    def embed(i, carry):
        r = tile_rows(i)
        place = pos_col[r, 0:1]
        pixel = dot(pat[r, :], wpat[...]) + patch_bias
        stream = dot(onehot_of(place), wpos[...]) + jnp.where(place < TABLE, pixel, 0.0)
        x0[r, :] = stream
        unit, inverse = normalise(stream)
        unit_a[r, :] = unit
        inv_a[r, :] = jnp.broadcast_to(inverse, (ROWS, LANES))
        h = (unit * vec(0, 0) + vec(0, 1)).astype(LOW)
        h_a[r, :] = h
        bias = jnp.concatenate([vec(0, 2), jnp.zeros((1, D), FULL), vec(0, 3)], axis=1)
        qkv[r, :] = (dot(h, wqkv[0]) + bias).astype(LOW)
        return carry

    lax.fori_loop(0, SEQ // ROWS, embed, 0)

    def window_rows(j):
        start = jnp.minimum((102 * j) // 16 * 16, SEQ - WINDOW)
        return pl.ds(pl.multiple_of(start, 16), WINDOW)

    def both(x):
        zero = jnp.zeros_like(x)
        return jnp.concatenate([jnp.where(head_of_lane == 0, x, zero), jnp.where(head_of_lane == 1, x, zero)], axis=0)

    def merge(x):
        return jnp.where(head_of_lane == 0, x[:WINDOW], x[WINDOW:])

    att[...] = jnp.zeros_like(att)

    def attend(j, carry):
        r = window_rows(j)
        own = seg_col[r, :]
        other = jnp.transpose(own)
        first = (2 * j).astype(FULL)
        mask = (own == other) & (own >= first) & (own < first + 2.0)
        mask = jnp.concatenate([mask.astype(FULL)] * 2, axis=0) > 0.5
        for g in range(HEADS // 2):
            lanes = slice(g * LANES, (g + 1) * LANES)
            q2 = both(qkv[r, lanes])
            keys = qkv[r, D + g * LANES : D + (g + 1) * LANES]
            values = qkv[r, 2 * D + g * LANES : 2 * D + (g + 1) * LANES]
            scores = jnp.where(mask, dot_nt(q2, keys) * SCORE_SCALE, MASK_FILL)
            e = jnp.exp(scores - jnp.max(scores, axis=-1, keepdims=True))
            p = jnp.where(mask, e / jnp.sum(e, axis=-1, keepdims=True), 0.0)
            probs[j, g] = p
            att[r, lanes] += merge(dot(p.astype(LOW), values))
        return carry

    lax.fori_loop(0, WINDOWS, attend, 0)

    def feed(i, carry):
        r = tile_rows(i)
        attended = att[r, :].astype(LOW)
        attl[r, :] = attended
        middle = x0[r, :] + dot(attended, wproj[0]) + vec(0, 4)
        unit, inverse = normalise(middle)
        unit_b[r, :] = unit
        inv_b[r, :] = jnp.broadcast_to(inverse, (ROWS, LANES))
        h = (unit * vec(0, 5) + vec(0, 6)).astype(LOW)
        h_b[r, :] = h
        for c in range(4):
            lanes = slice(c * D, (c + 1) * D)
            value, slope = gelu_parts(dot(h, wfc1[0, :, lanes]) + vecs[0, 7:8, lanes])
            act[r, lanes] = value.astype(LOW)
            dgelu[r, lanes] = slope
        x1[r, :] = middle + dot(act[r, :], wfc2[0]) + vec(0, 8)
        return carry

    lax.fori_loop(0, SEQ // ROWS, feed, 0)

    loads[2].wait()
    take_layer(1, b1)
    unit_c = x0
    inv_c = att.at[:, 0:LANES]
    h_c = low

    def kv_rows(i, carry):
        r = tile_rows(i)
        unit, inverse = normalise(x1[r, :])
        unit_c[r, :] = unit
        inv_c[r, :] = jnp.broadcast_to(inverse, (ROWS, LANES))
        h = (unit * vec(1, 0) + vec(1, 1)).astype(LOW)
        h_c[r, :] = h
        bias = jnp.concatenate([jnp.zeros((1, D), FULL), vec(1, 3)], axis=1)
        kv[r, :] = (dot(h, wqkv[1, :, D:]) + bias).astype(LOW)
        return carry

    lax.fori_loop(0, SEQ // ROWS, kv_rows, 0)

    h_s = dot(picker_low, h_c[...]).astype(LOW)
    x_s = dot(picker, x1[...], precision=HIGHEST)
    q_s = (dot(h_s, wqkv[1, :, :D]) + vec(1, 2)).astype(LOW)
    stack_rows = lax.broadcasted_iota(jnp.int32, (HEADS * PICKED, 1), 0)
    stack_lanes = lax.broadcasted_iota(jnp.int32, (1, D), 1)
    own_head = (stack_rows // PICKED) == (stack_lanes // HEAD_DIM)

    def stack(x):
        tall = jnp.concatenate([x.astype(FULL)] * HEADS, axis=0)
        return jnp.where(own_head, tall, 0.0).astype(LOW)

    def unstack(x):
        x = jnp.where(own_head, x, 0.0)
        total = x[:PICKED]
        for h in range(1, HEADS):
            total += x[h * PICKED : (h + 1) * PICKED]
        return total

    q6 = stack(q_s)
    image6 = jnp.concatenate([picked_image] * HEADS, axis=0)
    mask6 = image6 == seg_row
    scores = jnp.where(mask6, dot_nt(q6, kv[:, :D]) * SCORE_SCALE, MASK_FILL)
    e = jnp.exp(scores - jnp.max(scores, axis=-1, keepdims=True))
    p6 = e / jnp.sum(e, axis=-1, keepdims=True)
    p6_low = p6.astype(LOW)
    att_s = unstack(dot(p6_low, kv[:, D:])).astype(LOW)
    mid_s = x_s + dot(att_s, wproj[1]) + vec(1, 4)
    unit_m, inv_m = normalise(mid_s)
    h2_s = (unit_m * vec(1, 5) + vec(1, 6)).astype(LOW)
    act_s, slope_s = gelu_parts(dot(h2_s, wfc1[1]) + vec(1, 7))
    act_s = act_s.astype(LOW)
    x2_s = mid_s + dot(act_s, wfc2[1]) + vec(1, 8)

    unit_f, inv_f = normalise(x2_s)
    summary = (unit_f * final_gain + final_bias).astype(LOW)
    arr_row = lax.broadcasted_iota(jnp.int32, (D, GROUP * LANES), 0)
    arr_lane = lax.broadcasted_iota(jnp.int32, (D, GROUP * LANES), 1)
    arrange = (
        (arr_row == (arr_lane % LANES) * GROUP + arr_lane // LANES) & (arr_lane % LANES < GROUPS)
    ).astype(FULL)
    arranged = dot(summary, arrange.astype(LOW)).astype(LOW)
    logits = head_bias
    spans = []
    for k in range(GROUP):
        at = 2 * CLASSES * k
        block, shift = at // LANES, at % LANES
        blocks = (at + 2 * CLASSES - 1) // LANES - block + 1
        spans.append((block, shift, blocks))
        s_k = arranged[:, k * LANES : k * LANES + GROUPS]
        wide = (HEAD_LANES // LANES + 1) * LANES
        part = dot(s_k, whead[:, block * LANES : block * LANES + wide])
        if shift:
            part = pltpu.roll(part, wide - shift, 1)
        logits = logits + part[:, :HEAD_LANES]
    column = lax.broadcasted_iota(jnp.int32, (PICKED, HEAD_LANES), 1)
    second = picked_row >= IMAGES
    low_end = jnp.where(second, CLASSES, 0)
    valid = (column >= low_end) & (column < low_end + CLASSES)
    live = picked_row < 2 * IMAGES
    target = jnp.zeros((PICKED, 1), jnp.int32)
    for i in range(IMAGES):
        target = jnp.where(picked_row == i, lab[0, i], target)
        target = jnp.where(picked_row == IMAGES + i, CLASSES + tea[0, i], target)
    hit = column == target
    logits = jnp.where(valid, logits, -3e38)
    top = jnp.max(logits, axis=-1, keepdims=True)
    e = jnp.exp(logits - top)
    total = jnp.sum(e, axis=-1, keepdims=True)
    hit_logit = jnp.sum(jnp.where(hit, logits, 0.0), axis=-1, keepdims=True)
    each = jnp.where(live, top + jnp.log(total) - hit_logit, 0.0)
    loss[...] = jnp.broadcast_to(jnp.sum(each, axis=0, keepdims=True), loss.shape)
    grad_logits = jnp.where(live, (e / total - hit.astype(FULL)) * loss_scale, 0.0)
    grad_low = grad_logits.astype(LOW)
    grad_wide = jnp.concatenate([grad_low.astype(FULL), jnp.zeros((PICKED, LANES), FULL)], axis=1)

    grad_arranged = []
    for k, (block, shift, blocks) in enumerate(spans):
        turned = (pltpu.roll(grad_wide, shift, 1) if shift else grad_wide).astype(LOW)
        turned = turned[:, : blocks * LANES]
        s_k = arranged[:, k * LANES : k * LANES + GROUPS]
        grad_w = dot_tn(s_k, turned)
        for j in range(blocks):
            rows = pl.ds(HEAD_AT + block + j, GROUPS, stride=GROUP_ROWS)
            piece = grad_w[:, j * LANES : (j + 1) * LANES]
            if k and j == 0:
                piece = piece + flatg[rows, :]
            flatg[rows, :] = piece
        back = dot_nt(turned, whead[:, block * LANES : (block + blocks) * LANES])
        grad_arranged.append(jnp.concatenate([back, jnp.zeros((PICKED, LANES - GROUPS), FULL)], axis=1))
    grad_summary = dot_nt(jnp.concatenate(grad_arranged, axis=1), arrange, HIGHEST)
    put_row(HEAD_BIAS_AT, col_sum(grad_low), flatg)
    put_row(FINAL_GAIN_AT, col_sum(grad_summary * unit_f), flatg)
    put_row(FINAL_BIAS_AT, col_sum(grad_summary), flatg)
    flatg[GLOBAL_END:, :] = jnp.zeros((PARTS * GLOBAL_ROWS - GLOBAL_END, LANES), FULL)
    dx_s = norm_back(grad_summary, final_gain, unit_f, inv_f)

    out_s = dx_s.astype(LOW)
    for c in range(4):
        put(FC2_AT, c * D, D, dot_tn(act_s[:, c * D : (c + 1) * D], out_s))
    put_row(FC2_BIAS_AT, col_sum(out_s))
    gpre_s = (dot_nt(out_s, wfc2[1]) * slope_s).astype(LOW)
    put(FC1_AT, 0, FF, dot_tn(h2_s, gpre_s))
    put_row(FC1_BIAS_AT, col_sum(gpre_s))
    gh2_s = dot_nt(gpre_s, wfc1[1])
    put_row(MID_GAIN_AT, col_sum(gh2_s * unit_m))
    put_row(MID_BIAS_AT, col_sum(gh2_s))
    gmid_s = dx_s + norm_back(gh2_s, vec(1, 5), unit_m, inv_m)
    gmid_low = gmid_s.astype(LOW)
    put(PROJ_AT, 0, D, dot_tn(att_s, gmid_low))
    put_row(PROJ_BIAS_AT, col_sum(gmid_low))
    gatt6 = stack(dot_nt(gmid_low, wproj[1]).astype(LOW))
    gprob = dot_nt(gatt6, kv[:, D:])
    gscore = (p6 * (gprob - jnp.sum(p6 * gprob, axis=-1, keepdims=True))).astype(LOW)
    gq_s = (unstack(dot(gscore, kv[:, :D])) * SCORE_SCALE).astype(LOW)
    gkeys = (dot_tn(gscore, q6) * SCORE_SCALE).astype(LOW)
    gvalues = dot_tn(p6_low, gatt6).astype(LOW)
    put_row(QUERY_BIAS_AT, col_sum(gq_s))
    put_row(VALUE_BIAS_AT, col_sum(gvalues))
    kv[:, :D] = gkeys
    kv[:, D:] = gvalues
    put(QKV_AT, 0, 3 * D, dot_tn(h_s, gq_s))
    put(QKV_AT, 0, 3 * D, dot_tn(h_c[...], kv[:, :D]), 3)
    put(QKV_AT, 0, 3 * D, dot_tn(h_c[...], kv[:, D:]), 6)
    back_s = jnp.concatenate([dot_nt(gq_s, wqkv[1, :, :D]), gmid_s], axis=1)

    dx = x1

    def kv_back(i, carry):
        gain_sum, bias_sum = carry
        r = tile_rows(i)
        image_col = seg_col[r, 0:1]
        place_col = pos_col[r, 0:1]
        lane = lax.broadcasted_iota(jnp.int32, (1, PICKED), 1).astype(FULL)
        lane_image = jnp.where(lane < IMAGES, lane, lane - IMAGES)
        lane_place = jnp.where(lane < IMAGES, float(TABLE), TABLE + 1.0)
        back_pick = (
            (image_col == lane_image) & (place_col == lane_place) & (lane < 2.0 * IMAGES)
        ).astype(FULL)
        back = dot(back_pick, back_s, precision=HIGHEST)
        grad = back[:, :D] + dot_nt(kv[r, :], wqkv[1, :, D:])
        unit = unit_c[r, :]
        dx[r, :] = back[:, D:] + norm_back(grad, vec(1, 0), unit, inv_c[r, 0:1])
        return gain_sum + col_sum(grad * unit), bias_sum + col_sum(grad)

    zero_row = jnp.zeros((1, D), FULL)
    gain_sum, bias_sum = lax.fori_loop(0, SEQ // ROWS, kv_back, (zero_row, zero_row))
    put_row(PRE_GAIN_AT, gain_sum)
    put_row(PRE_BIAS_AT, bias_sum)
    flat[LAYER_END:, :] = jnp.zeros((PARTS * LAYER_ROWS - LAYER_END, LANES), FULL)
    gather_rows(b1, flat, LAYER_ROWS)
    store1 = pltpu.make_async_copy(b1, g1, sems.at[3])
    store1.start()

    def feed_back(i, carry):
        fc1_sum, fc2_sum, proj_sum, gain_sum, bias_sum = carry
        r = tile_rows(i)
        grad_out = dx[r, :]
        out_low = grad_out.astype(LOW)
        low[r, :] = out_low
        for c in range(4):
            lanes = slice(c * D, (c + 1) * D)
            gpre[r, lanes] = (dot_nt(out_low, wfc2[0, lanes, :]) * dgelu[r, lanes]).astype(LOW)
        grad_h = dot_nt(gpre[r, :], wfc1[0])
        unit = unit_b[r, :]
        middle = grad_out + norm_back(grad_h, vec(0, 5), unit, inv_b[r, 0:1])
        dx[r, :] = middle
        middle_low = middle.astype(LOW)
        h2low[r, :] = middle_low
        gatt[r, :] = dot_nt(middle_low, wproj[0]).astype(LOW)
        return (
            fc1_sum + col_sum(gpre[r, :]), fc2_sum + col_sum(out_low), proj_sum + col_sum(middle_low),
            gain_sum + col_sum(grad_h * unit), bias_sum + col_sum(grad_h),
        )

    h2low = kv.at[:, 0:D]
    gatt = kv.at[:, D : 2 * D]
    sums = lax.fori_loop(0, SEQ // ROWS, feed_back, (jnp.zeros((1, FF), FULL),) + (zero_row,) * 4)
    for at, value in zip((FC1_BIAS_AT, FC2_BIAS_AT, PROJ_BIAS_AT, MID_GAIN_AT, MID_BIAS_AT), sums):
        put_row(at, value)

    for c in range(4):
        lanes = slice(c * D, (c + 1) * D)
        put(FC2_AT, c * D, D, dot_tn(act[:, lanes], low[...]))
        put(FC1_AT, 0, FF, dot_tn(h_b[...], gpre[:, lanes]), 3 * c)
    put(PROJ_AT, 0, D, dot_tn(attl[...], h2low[...]))

    dqkv = dgelu.at[:, : 3 * D]
    dqkv[...] = jnp.zeros(dqkv.shape, FULL)

    def attend_back(j, carry):
        r = window_rows(j)
        for g in range(HEADS // 2):
            lanes = slice(g * LANES, (g + 1) * LANES)
            key_lanes = slice(D + g * LANES, D + (g + 1) * LANES)
            value_lanes = slice(2 * D + g * LANES, 2 * D + (g + 1) * LANES)
            q2 = both(qkv[r, lanes])
            go2 = both(gatt[r, lanes])
            p = probs[j, g]
            gp = dot_nt(go2, qkv[r, value_lanes])
            gs = (p * (gp - jnp.sum(p * gp, axis=-1, keepdims=True))).astype(LOW)
            dqkv[r, lanes] += merge(dot(gs, qkv[r, key_lanes]))
            dqkv[r, key_lanes] += dot_tn(gs, q2)
            dqkv[r, value_lanes] += dot_tn(p.astype(LOW), go2)
        return carry

    lax.fori_loop(0, WINDOWS, attend_back, 0)

    def qkv_back(i, carry):
        query_sum, value_sum, gain_sum, bias_sum, embed_sum = carry
        r = tile_rows(i)
        gq = (dqkv[r, :D] * SCORE_SCALE).astype(LOW)
        gk = (dqkv[r, D : 2 * D] * SCORE_SCALE).astype(LOW)
        gv = dqkv[r, 2 * D :].astype(LOW)
        qkv[r, :D] = gq
        qkv[r, D : 2 * D] = gk
        qkv[r, 2 * D :] = gv
        grad = dot_nt(qkv[r, :], wqkv[0])
        unit = unit_a[r, :]
        full = dx[r, :] + norm_back(grad, vec(0, 0), unit, inv_a[r, 0:1])
        dx[r, :] = full
        place = pos_col[r, 0:1]
        pixel = jnp.where(place < TABLE, full, 0.0).astype(LOW)
        low[r, :] = pixel
        return (
            query_sum + col_sum(gq), value_sum + col_sum(gv), gain_sum + col_sum(grad * unit),
            bias_sum + col_sum(grad), embed_sum + col_sum(pixel),
        )

    sums = lax.fori_loop(0, SEQ // ROWS, qkv_back, (zero_row,) * 5)
    for at, value in zip((QUERY_BIAS_AT, VALUE_BIAS_AT, PRE_GAIN_AT, PRE_BIAS_AT), sums):
        put_row(at, value)
    for c in range(3):
        put(QKV_AT, 0, 3 * D, dot_tn(h_a[...], qkv[:, c * D : (c + 1) * D]), 3 * c)
    gather_rows(b0, flat, LAYER_ROWS)
    store0 = pltpu.make_async_copy(b0, g0, sems.at[4])
    store0.start()

    for c in range(2):
        put(PATCH_AT, c * D, D, dot_tn(pat[:, c * D : (c + 1) * D], low[...]), 0, flatg)
    place = pos_col[:, 0:1]
    onehot = onehot_of(place)
    high = dx[...].astype(LOW)
    rest = (dx[...] - high.astype(FULL)).astype(LOW)
    table = dot_tn(onehot, high) + dot_tn(onehot, rest)
    put(POS_AT, 0, D, table[: TABLE + 2], 0, flatg)
    put_row(PATCH_BIAS_AT, sums[4], flatg)
    gather_rows(bg, flatg, GLOBAL_ROWS)
    store1.wait()
    store0.wait()
    last = pltpu.make_async_copy(bg, gg, sems.at[5])
    last.start()
    last.wait()


def step_call(loss_scale, pat, pos, seg, lab, tea, a0, a1, ag):
    vmem = pl.BlockSpec(memory_space=pltpu.VMEM)
    smem = pl.BlockSpec(memory_space=pltpu.SMEM)
    hbm = pl.BlockSpec(memory_space=pl.ANY)
    shape = lambda *dims, kind=FULL: pltpu.VMEM(dims, kind)
    scratch = [
        shape(*a0.shape, kind=LOW), shape(*a1.shape, kind=LOW), shape(*ag.shape, kind=LOW),
        shape(PARTS * LAYER_ROWS, LANES), shape(PARTS * GLOBAL_ROWS, LANES),
        shape(2, D, 3 * D, kind=LOW), shape(2, D, D, kind=LOW), shape(2, D, FF, kind=LOW), shape(2, FF, D, kind=LOW),
        shape(PATCH, D, kind=LOW), shape(256, D, kind=LOW), shape(GROUPS, (GROUP_ROWS + 1) * LANES, kind=LOW),
        shape(2, 16, FF),
        shape(SEQ, LANES), shape(SEQ, LANES),
        shape(SEQ, D), shape(SEQ, LANES), shape(SEQ, D, kind=LOW),
        shape(SEQ, D), shape(SEQ, LANES), shape(SEQ, D, kind=LOW),
        shape(SEQ, 3 * D, kind=LOW), shape(WINDOWS, HEADS // 2, 2 * WINDOW, WINDOW),
        shape(SEQ, D), shape(SEQ, D, kind=LOW), shape(SEQ, D), shape(SEQ, D),
        shape(SEQ, FF), shape(SEQ, FF, kind=LOW), shape(SEQ, FF, kind=LOW),
        shape(SEQ, 2 * D, kind=LOW), shape(SEQ, D, kind=LOW),
        pltpu.SemaphoreType.DMA((6,)),
    ]
    return pl.pallas_call(
        functools.partial(step_kernel, loss_scale),
        out_shape=[jax.ShapeDtypeStruct(a.shape, LOW) for a in (a0, a1, ag)]
        + [jax.ShapeDtypeStruct((8, LANES), FULL)],
        in_specs=[vmem] * 3 + [smem] * 2 + [hbm] * 3,
        out_specs=[hbm] * 3 + [vmem],
        scratch_shapes=scratch,
        compiler_params=pltpu.CompilerParams(vmem_limit_bytes=VMEM_BYTES),
    )(pat, pos, seg, lab, tea, a0, a1, ag)


VMEM_BYTES = 62 * 1024 * 1024


def adam(master, moment, second, gradient, factor):
    clipped = gradient * factor
    new_moment = BETA_ONE * moment + (1.0 - BETA_ONE) * clipped
    new_second = BETA_TWO * second + (1.0 - BETA_TWO) * clipped * clipped
    fix_one = 1.0 - BETA_ONE**STEP
    fix_two = 1.0 - BETA_TWO**STEP
    update = new_moment / fix_one / (jnp.sqrt(new_second / fix_two) + ADAM_EPS) + WEIGHT_DECAY * master
    return master - LEARN_RATE * update, new_moment, new_second


MESH = pl.DeviceIdType.MESH


class Place:
    def __init__(self, sizes):
        dp, fsdp = sizes
        self.ny = dp // 2
        self.nx = next(v for v in range(min(self.ny, fsdp), 0, -1) if fsdp % v == 0)
        self.nz = fsdp // self.nx
        self.fsdp = fsdp
        self.count = dp * fsdp
        self.turn = self.nx == self.ny
        self.np_, self.nq = self.ny, self.nx

    def locate(self):
        dp, fsdp = lax.axis_index("dp"), lax.axis_index("fsdp")
        self.y, self.core = dp // 2, dp % 2
        self.z, self.x = fsdp // self.nx, fsdp % self.nx

    def order(self, dz, dp, dq):
        return (dz * self.np_ + dp) * self.nq + dq

    def at(self, dz, dp, dq, other=0):
        core = (self.core + other) % 2
        z = (self.z + dz) % self.nz
        if self.turn:
            y = jnp.where(core == 0, self.y + dp, self.y + dq) % self.ny
            x = jnp.where(core == 0, self.x + dq, self.x + dp) % self.nx
        else:
            y, x = (self.y + dp) % self.ny, (self.x + dq) % self.nx
        return y * 2 + core, z * self.nx + x

    def piece(self, dz, dp, dq, other=0):
        a, b = self.at(dz, dp, dq, other)
        return a * self.fsdp + b

    def offsets(self):
        return [(a, b, c) for a in range(self.nz) for b in range(self.np_) for c in range(self.nq)]

    def core_at(self, k):
        return self.at(0, 0, 0, k)

    def y_at(self, k):
        return (self.y + k) % self.ny * 2 + self.core, self.z * self.nx + self.x

    def x_at(self, k):
        return self.y * 2 + self.core, self.z * self.nx + (self.x + k) % self.nx

    def peers(self):
        ids = [self.at(0, 0, 0, 1)]
        ids += [self.at(k, 0, 0) for k in range(1, self.nz)]
        ids += [self.at(0, k, 0) for k in range(1, self.np_)]
        ids += [self.at(0, 0, k) for k in range(1, self.nq)]
        return ids

    def greet(self):
        barrier = pltpu.get_barrier_semaphore()
        ids = self.peers()
        for peer in ids:
            pl.semaphore_signal(barrier, inc=1, device_id=peer, device_id_type=MESH)
        pl.semaphore_wait(barrier, len(ids))


def gather_kernel(place, lm, gm, o0, o1, og, own0, own1, owng, send, local, recv):
    place.locate()
    me = place.piece(0, 0, 0)
    chunks = ((og, owng), (o0, own0), (o1, own1))
    owng[: gm.shape[0], :] = gm[...].astype(LOW)
    own0[: lm.shape[1], :] = lm[0].astype(LOW)
    own1[: lm.shape[1], :] = lm[1].astype(LOW)
    place.greet()

    def push(n, src, piece, index, peer):
        out = chunks[n][0]
        pltpu.make_async_remote_copy(
            src_ref=src, dst_ref=out.at[piece], send_sem=send.at[n], recv_sem=recv.at[n, index],
            device_id=peer, device_id_type=MESH,
        ).start()

    def forward(n, d):
        dz, dp, dq = d
        piece = place.piece(*d)
        mine = d == (0, 0, 0)
        src = chunks[n][1] if mine else chunks[n][0].at[piece]
        if mine:
            for k in range(1, place.nz):
                push(n, src, piece, place.order(-k % place.nz, 0, 0), place.at(k, 0, 0))
        if dp == 0 and dq == 0:
            for k in range(1, place.np_):
                push(n, src, piece, place.order(dz, -k % place.np_, 0), place.at(0, k, 0))
        if dq == 0:
            for k in range(1, place.nq):
                push(n, src, piece, place.order(dz, dp, -k % place.nq), place.at(0, 0, k))
        push(n, src, piece, place.count // 2 + place.order(*d), place.at(0, 0, 0, 1))

    def arrive(n, piece, index):
        out = chunks[n][0]
        pltpu.make_async_remote_copy(
            src_ref=out.at[piece], dst_ref=out.at[piece], send_sem=send.at[n], recv_sem=recv.at[n, index],
            device_id=place.at(0, 0, 0, 1), device_id_type=MESH,
        ).wait_recv()

    keeps = []
    for n, (out, own) in enumerate(chunks):
        forward(n, (0, 0, 0))
        keep = pltpu.make_async_copy(own, out.at[me], local.at[n])
        keep.start()
        keeps.append(keep)
    rest = sorted(place.offsets()[1:], key=lambda d: ((d[0] > 0) + 2 * (d[1] > 0) + 4 * (d[2] > 0), d))
    for n in range(3):
        for d in rest:
            arrive(n, place.piece(*d), place.order(*d))
            forward(n, d)
    for n, (out, own) in enumerate(chunks):
        for d in place.offsets():
            arrive(n, place.piece(*d, 1), place.count // 2 + place.order(*d))
        keeps[n].wait()
        sent = out.at[pl.ds(0, place.count - 1)]
        pltpu.make_async_copy(sent, sent, send.at[n]).wait()


def scatter_kernel(
    place, g0, g1, gg, loss, s0, s1, sg, total,
    l0, l1, lg, c0, c1, cg, q0, q1, qg, p0, p1, pg, z0, z1, zg, tiles,
    send, local, recv, tile_send, tile_recv,
):
    place.locate()
    nz, np_, nq = place.nz, place.np_, place.nq
    half = place.count // 2
    chunks = ((g1, l1, c1, q1, p1, z1, s1), (g0, l0, c0, q0, p0, z0, s0), (gg, lg, cg, qg, pg, zg, sg))
    far = sorted(place.offsets(), key=lambda d: (-(d[2] > 0), -(d[1] > 0), -(d[0] > 0), d))
    q_base, p_base, z_base = half, half + nz * np_ * (nq - 1), half + nz * np_ * (nq - 1) + nz * (np_ - 1)

    def push(n, src, dst, index, peer):
        pltpu.make_async_remote_copy(
            src_ref=src, dst_ref=dst, send_sem=send.at[n], recv_sem=recv.at[n, index],
            device_id=peer, device_id_type=MESH,
        ).start()

    def arrive(n, dst, index):
        pltpu.make_async_remote_copy(
            src_ref=dst, dst_ref=dst, send_sem=send.at[n], recv_sem=recv.at[n, index],
            device_id=place.at(0, 0, 0, 1), device_id_type=MESH,
        ).wait_recv()

    loads = {}
    for n, (g, l, *_) in enumerate(chunks):
        for d in far:
            i = place.order(*d)
            loads[n, d] = pltpu.make_async_copy(g.at[place.piece(*d)], l.at[i], local.at[n, i])
            loads[n, d].start()
    place.greet()
    for n, (g, l, c, *_) in enumerate(chunks):
        for d in far:
            i = place.order(*d)
            push(n, g.at[place.piece(*d, 1)], c.at[i], i, place.at(0, 0, 0, 1))

    def gathered(n, d):
        g, l, c, q, p, z, s = chunks[n]
        dz, dp, dq = d
        i = place.order(*d)
        loads[n, d].wait()
        arrive(n, c.at[i], i)
        refs = [l.at[i], c.at[i]]
        if dq == 0:
            for k in range(nq - 1):
                j = (dz * np_ + dp) * (nq - 1) + k
                arrive(n, q.at[j], q_base + j)
                refs.append(q.at[j])
        if dq == 0 and dp == 0:
            for k in range(np_ - 1):
                j = dz * (np_ - 1) + k
                arrive(n, p.at[j], p_base + j)
                refs.append(p.at[j])
        if d == (0, 0, 0):
            for k in range(nz - 1):
                arrive(n, z.at[k], z_base + k)
                refs.append(z.at[k])
        return refs

    def add_up(refs, dst, kind, rows):
        step = 64 if rows % 64 == 0 else 32 if rows % 32 == 0 else 16

        def one(t, carry):
            r = pl.ds(pl.multiple_of(t * step, step), step)
            value = refs[0][r, :].astype(FULL)
            for ref in refs[1:]:
                value += ref[r, :].astype(FULL)
            dst[r, :] = value.astype(kind)
            return carry

        lax.fori_loop(0, rows // step, one, 0)

    def stage_q(n):
        g, l, c, q, p, z, s = chunks[n]
        for d in far:
            dz, dp, dq = d
            if dq:
                refs = gathered(n, d)
                add_up(refs, refs[0], LOW, l.shape[1])
                j = (dz * np_ + dp) * (nq - 1) + (nq - dq) - 1
                push(n, refs[0], q.at[j], q_base + j, place.at(0, 0, dq))

    def stage_p(n):
        g, l, c, q, p, z, s = chunks[n]
        for d in far:
            dz, dp, dq = d
            if dq == 0 and dp:
                refs = gathered(n, d)
                add_up(refs, refs[0], LOW, l.shape[1])
                j = dz * (np_ - 1) + (np_ - dp) - 1
                push(n, refs[0], p.at[j], p_base + j, place.at(0, dp, 0))

    def stage_z(n):
        g, l, c, q, p, z, s = chunks[n]
        for d in far:
            dz, dp, dq = d
            if dq == 0 and dp == 0 and dz:
                refs = gathered(n, d)
                add_up(refs, refs[0], LOW, l.shape[1])
                j = (nz - dz) - 1
                push(n, refs[0], z.at[j], z_base + j, place.at(dz, 0, 0))

    def stage_own(n):
        g, l, c, q, p, z, s = chunks[n]
        add_up(gathered(n, (0, 0, 0)), s, FULL, l.shape[1])

    stages = (stage_q, stage_p, stage_z, stage_own)
    for t in range(3 + len(stages) - 1):
        for n in range(3):
            if 0 <= t - n < len(stages):
                stages[t - n](n)

    squares = jnp.zeros((1, 1), FULL)
    for s, rows in ((s0, place.rows[0]), (s1, place.rows[0]), (sg, place.rows[1])):
        used = s[:rows, :]
        squares += jnp.sum(jnp.sum(used * used, axis=0, keepdims=True), axis=1, keepdims=True)
    row = lax.broadcasted_iota(jnp.int32, (8, LANES), 0)
    tile = jnp.where(row == 0, squares, loss[...])
    base = 0
    axes = (
        (2, place.core, lambda k: place.core_at(k)), (place.ny, place.y, lambda k: place.y_at(k)),
        (place.nx, place.x, lambda k: place.x_at(k)), (nz, place.z, lambda k: place.at(k, 0, 0)),
    )
    sends = []
    for size, own, peer_at in axes:
        tiles[base + own] = tile
        for k in range(1, size):
            copy = pltpu.make_async_remote_copy(
                src_ref=tiles.at[base + own], dst_ref=tiles.at[base + own], send_sem=tile_send.at[base + k],
                recv_sem=tile_recv.at[base + (size - k)], device_id=peer_at(k), device_id_type=MESH,
            )
            copy.start()
            sends.append(copy)
        for k in range(1, size):
            slot = tiles.at[base + (own + k) % size]
            pltpu.make_async_remote_copy(
                src_ref=slot, dst_ref=slot, send_sem=tile_send.at[base + k], recv_sem=tile_recv.at[base + k],
                device_id=peer_at(k), device_id_type=MESH,
            ).wait_recv()
        tile = tiles[base]
        for k in range(1, size):
            tile += tiles[base + k]
        base += size
    total[...] = tile
    for copy in sends:
        copy.wait_send()
    for n, (g, *_) in enumerate(chunks):
        sent = g.at[pl.ds(0, place.count - 1)]
        pltpu.make_async_copy(sent, sent, send.at[n]).wait()


def padded(rows):
    return rows + -rows % 16


def gather_call(place, lm, gm):
    n, rows, global_rows = place.count, lm.shape[1], gm.shape[0]
    vmem = pl.BlockSpec(memory_space=pltpu.VMEM)
    hbm = pl.BlockSpec(memory_space=pl.ANY)
    shapes = [(padded(rows), LANES), (padded(rows), LANES), (padded(global_rows), LANES)]
    return pl.pallas_call(
        functools.partial(gather_kernel, place),
        out_shape=[jax.ShapeDtypeStruct((n,) + s, LOW) for s in shapes],
        in_specs=[vmem] * 2,
        out_specs=[hbm] * 3,
        scratch_shapes=[pltpu.VMEM(s, LOW) for s in shapes]
        + [
            pltpu.SemaphoreType.DMA((3,)), pltpu.SemaphoreType.DMA((3,)), pltpu.SemaphoreType.DMA((3, n)),
        ],
        compiler_params=pltpu.CompilerParams(collective_id=0, has_side_effects=True, vmem_limit_bytes=VMEM_BYTES),
    )(lm, gm)


def scatter_call(place, g0, g1, gg, loss):
    n = place.count
    vmem = pl.BlockSpec(memory_space=pltpu.VMEM)
    hbm = pl.BlockSpec(memory_space=pl.ANY)
    blocks = [g.shape[1:] for g in (g0, g1, gg)]
    counts = (
        n // 2, n // 2, place.nz * place.np_ * (place.nq - 1), place.nz * (place.np_ - 1), place.nz - 1
    )
    tiles = 2 + place.ny + place.nx + place.nz
    received = n // 2 + sum(counts[2:])
    return pl.pallas_call(
        functools.partial(scatter_kernel, place),
        out_shape=[jax.ShapeDtypeStruct(b, FULL) for b in blocks] + [jax.ShapeDtypeStruct((8, LANES), FULL)],
        in_specs=[hbm] * 3 + [vmem],
        out_specs=[vmem] * 4,
        scratch_shapes=[pltpu.VMEM((max(c, 1),) + b, LOW) for c in counts for b in blocks]
        + [
            pltpu.VMEM((tiles, 8, LANES), FULL),
            pltpu.SemaphoreType.DMA((3,)), pltpu.SemaphoreType.DMA((3, n // 2)),
            pltpu.SemaphoreType.DMA((3, received)),
            pltpu.SemaphoreType.DMA((tiles,)), pltpu.SemaphoreType.DMA((tiles,)),
        ],
        compiler_params=pltpu.CompilerParams(collective_id=1, has_side_effects=True, vmem_limit_bytes=VMEM_BYTES),
    )(g0, g1, gg, loss)


def repack(a, count, rows, new_count, new_rows):
    if (count, rows) == (new_count, new_rows):
        return a
    a = a[:, :rows].reshape(new_count, new_rows, LANES)
    return jnp.pad(a, ((0, 0), (0, padded(new_rows) - new_rows), (0, 0)))


def shards(sizes, pat, pos, seg, lab, tea, lm, lo, ls, gm, go, gs):
    place = Place(sizes)
    n = place.count
    rows, global_rows = lm.shape[1] // LANES, gm.shape[0] // LANES
    place.rows = rows, global_rows
    gathered = gather_call(place, lm.reshape(2, rows, LANES), gm.reshape(global_rows, LANES))
    own_rows = (rows, rows, global_rows)
    step_rows = (LAYER_ROWS, LAYER_ROWS, GLOBAL_ROWS)
    gathered = [repack(a, n, r, PARTS, t) for a, r, t in zip(gathered, own_rows, step_rows)]
    loss_scale = 1.0 / (2 * IMAGES * n)
    *grads, loss = step_call(loss_scale, pat[0], pos, seg, lab, tea, *gathered)
    grads = [repack(a, PARTS, t, n, r) for a, r, t in zip(grads, own_rows, step_rows)]
    s0, s1, sg, total = scatter_call(place, *grads, loss)
    layer = jnp.stack([s0[:rows].reshape(-1), s1[:rows].reshape(-1)])
    gg = sg[:global_rows].reshape(-1)
    norm = jnp.sqrt(total[0, 0])
    factor = jnp.minimum(1.0, CLIP_NORM / norm)
    return adam(lm, lo, ls, layer, factor) + adam(gm, go, gs, gg, factor) + (norm, total[1, 0])


def solution(mesh):
    axes = tuple(mesh.axis_names)
    split = P(axes)
    wide = P(None, axes)
    return jax.shard_map(
        functools.partial(shards, tuple(mesh.shape[a] for a in axes)),
        mesh=mesh,
        in_specs=(split,) * 5 + (wide,) * 3 + (split,) * 3,
        out_specs=(wide,) * 3 + (split,) * 3 + (P(), P()),
        check_vma=False,
    )
```

```python
import functools

import jax
import jax.numpy as jnp
from jax import lax
from jax.experimental import pallas as pl
from jax.experimental.pallas import tpu as pltpu
from jax.sharding import PartitionSpec as P

D = 384
HEADS = 6
HEAD_DIM = 64
FF = 1536
CLASSES = 1000
PATCH = 768
TABLE = 196
IMAGES = 15
SEQ = 768
STEP = 10
LANES = 128

NORM_EPS = 1e-06
BETA_ONE = 0.9
BETA_TWO = 0.999
ADAM_EPS = 1e-08
LEARN_RATE = 0.1
WEIGHT_DECAY = 0.05
CLIP_NORM = 0.01
MASK_FILL = -1000000000.0
SCORE_SCALE = HEAD_DIM ** (-0.5)
LOW = jnp.bfloat16
FULL = jnp.float32
HIGHEST = lax.Precision.HIGHEST

QKV_AT, PROJ_AT, FC1_AT, FC2_AT = 0, 3456, 4608, 9216
PRE_GAIN_AT, PRE_BIAS_AT, QUERY_BIAS_AT, VALUE_BIAS_AT = 13824, 13827, 13830, 13833
PROJ_BIAS_AT, MID_GAIN_AT, MID_BIAS_AT, FC1_BIAS_AT, FC2_BIAS_AT = 13836, 13839, 13842, 13845, 13857
LAYER_END = 13860
PATCH_AT, POS_AT, PATCH_BIAS_AT, FINAL_GAIN_AT, FINAL_BIAS_AT = 0, 2304, 2898, 2901, 2904
HEAD_AT, HEAD_BIAS_AT, GLOBAL_END = 2907, 8907, 8923
GROUP, GROUP_ROWS, GROUPS = 8, 125, 48
HEAD_LANES = 2048
PICKED = 32
WINDOWS, WINDOW = 8, 128
ROWS = 256
LAYER_ALL, GLOBAL_ALL = 14080, 8960
VMEM_BYTES = 64 * 1024 * 1024 - 64 * 1024
MESH = pl.DeviceIdType.MESH


def dot(a, b, dims=(1, 0), precision=None):
    return lax.dot_general(
        a, b, (((dims[0],), (dims[1],)), ((), ())), precision=precision, preferred_element_type=FULL
    )


def dot_nt(a, b, precision=None):
    return dot(a, b, (1, 1), precision)


def dot_tn(a, b, precision=None):
    return dot(a, b, (0, 0), precision)


def row_mean(x):
    return jnp.sum(x, axis=-1, keepdims=True) * (1.0 / D)


def normalise(x):
    center = x - row_mean(x)
    inverse = lax.rsqrt(row_mean(center * center) + NORM_EPS)
    return center * inverse, inverse


def norm_back(grad, gain, unit, inverse):
    scaled = grad * gain
    return inverse * (scaled - row_mean(scaled) - unit * row_mean(scaled * unit))


def col_sum(x):
    return jnp.sum(x.astype(FULL), axis=0, keepdims=True)


def gelu_parts(x):
    size = jnp.abs(x)
    bell = jnp.exp(-0.5 * x * x)
    base = 1.0 + (0.3275911 * 0.7071067811865476) * size
    t = pl.reciprocal(base, approx=True)
    t = t * (2.0 - base * t)
    tail = ((((1.061405429 * t - 1.453152027) * t + 1.421413741) * t - 0.284496736) * t + 0.254829592) * t
    tail = 0.5 * tail * bell
    phi = jnp.where(x < 0, tail, 1.0 - tail)
    return x * phi, phi + x * (bell * 0.3989422804014327)


def exact_parts(x):
    high = x.astype(LOW)
    rest = x - high.astype(FULL)
    middle = rest.astype(LOW)
    return high, middle, (rest - middle.astype(FULL)).astype(LOW)


def wrap(value, size):
    return jnp.where(value >= size, value - size, value)


class Place:
    def __init__(self, sizes):
        dp, fsdp = sizes
        self.n = self.ny = self.nx = dp // 2
        self.nz = fsdp // self.nx
        assert dp == 2 * self.n and fsdp == self.n * self.nz

    def locate(self):
        dp, fsdp = lax.axis_index("dp"), lax.axis_index("fsdp")
        self.y, self.core = dp // 2, dp % 2
        self.z, self.x = fsdp // self.nx, fsdp % self.nx
        self.even = self.core == 0
        self.zs = [wrap(self.z + k, self.nz) for k in range(self.nz)]
        self.ys = [wrap(self.y + k, self.n) for k in range(self.n)]
        self.xs = [wrap(self.x + k, self.n) for k in range(self.n)]
        spans = [(p, q) for p in range(self.n) for q in range(self.n)]
        self.short = {
            (p, q): (jnp.where(self.even, self.ys[p], self.ys[q]), jnp.where(self.even, self.xs[q], self.xs[p]))
            for p, q in spans
        }

    def yx(self, p, q):
        return self.short[p, q]

    def block(self, dz, p, q):
        y, x = self.yx(p, q)
        return y, self.core, self.zs[dz], x

    def device(self, y, core, z, x):
        return y * 2 + core, z * self.nx + x

    def meet(self):
        self.other = self.device(self.y, 1 - self.core, self.z, self.x)
        self.zp = [self.device(self.y, self.core, z, self.x) for z in self.zs]
        self.yp = [self.device(y, self.core, self.z, self.x) for y in self.ys]
        self.xp = [self.device(self.y, self.core, self.z, x) for x in self.xs]
        self.pp = [self.device(*self.block(0, k, 0)) for k in range(self.n)]
        self.qp = [self.device(*self.block(0, 0, k)) for k in range(self.n)]
        barrier = pltpu.get_barrier_semaphore()
        ids = [self.other] + self.zp[1:] + self.yp[1:] + self.xp[1:]
        for peer in ids:
            pl.semaphore_signal(barrier, inc=1, device_id=peer, device_id_type=MESH)
        pl.semaphore_wait(barrier, len(ids))


def push(src, dst, send, recv, peer):
    pltpu.make_async_remote_copy(
        src_ref=src, dst_ref=dst, send_sem=send, recv_sem=recv, device_id=peer, device_id_type=MESH
    ).start()


def landed(dst, recv):
    pltpu.make_async_copy(dst, dst, recv).wait()


class Gather:
    def __init__(self, place, buf, send, recv):
        self.place, self.buf, self.send, self.recv = place, buf, send, recv
        self.from_p = place.nz
        self.from_q = self.from_p + place.nz * place.n
        self.from_core = self.from_q + place.n

    def to_p(self, dz):
        a, t = self.place, self.buf.at[self.place.block(dz, 0, 0)]
        for k in range(1, a.n):
            push(t, t, self.send, self.recv.at[self.from_p + dz * a.n + a.n - k], a.pp[k])

    def to_q(self, dz, p):
        a, t = self.place, self.buf.at[self.place.block(dz, p, 0)]
        for k in range(1, a.n):
            push(t, t, self.send, self.recv.at[self.from_q + a.n - k], a.qp[k])

    def start(self):
        a, t = self.place, self.buf.at[self.place.block(0, 0, 0)]
        self.to_p(0)
        for k in range(1, a.nz):
            push(t, t, self.send, self.recv.at[a.nz - k], a.zp[k])
        self.to_q(0, 0)

    def z_came(self, dz):
        landed(self.buf.at[self.place.block(dz, 0, 0)], self.recv.at[dz])
        self.to_p(dz)
        self.to_q(dz, 0)

    def p_came(self, dz, p):
        landed(self.buf.at[self.place.block(dz, p, 0)], self.recv.at[self.from_p + dz * self.place.n + p])
        self.to_q(dz, p)

    def group(self, core, q):
        a = self.place
        return self.buf.at[:, 0, :, a.xs[q]] if core == 0 else self.buf.at[a.ys[q], 1]

    def to_core(self, q):
        a = self.place
        for core in range(2):

            @pl.when(a.core == core)
            def _():
                t = self.group(core, q)
                push(t, t, self.send, self.recv.at[self.from_core + q], a.other)

    def q_came(self, q):
        landed(self.buf.at[:, 0, :, 0], self.recv.at[self.from_q + q])
        self.to_core(q)

    def steps(self):
        a = self.place
        near = sorted(range(1, a.nz), key=lambda k: min(k, a.nz - k))
        out = [lambda p=p: self.p_came(0, p) for p in range(1, a.n)]
        out += [lambda k=k: self.z_came(k) for k in near]
        out += [lambda k=k, p=p: self.p_came(k, p) for k in near for p in range(1, a.n)]
        out += [lambda: self.to_core(0)]
        return out

    def last(self):
        for q in range(1, self.place.n):
            self.q_came(q)

    def finish(self):
        for q in range(self.place.n):
            landed(self.buf.at[:, 0, :, 0], self.recv.at[self.from_core + q])

    def drain(self):
        a = self.place
        for t in (self.buf.at[:, 0], self.buf.at[:, 0, :, pl.ds(0, a.n - 1)], self.buf.at[0, 0, :, pl.ds(0, a.n - 1)]):
            landed(t, self.send)
        landed(self.buf.at[0, 0, pl.ds(0, a.nz - 1), 0], self.send)


class Scatter:
    def __init__(self, place, buf, from_core, from_q, from_p, from_z, out, send, recv):
        self.place, self.buf, self.out, self.send, self.recv = place, buf, out, send, recv
        self.core_buf, self.q_buf, self.p_buf, self.z_buf = from_core, from_q, from_p, from_z
        n, nz = place.n, place.nz
        self.at_q = n
        self.at_p = self.at_q + n * n
        self.at_z = self.at_p + n

    def start(self):
        a = self.place
        for core in range(2):

            @pl.when(a.core == core)
            def _():
                for q in tuple(range(1, a.n)) + (0,):
                    if core == 1:
                        src, dst = self.buf.at[:, 0, :, a.xs[q]], self.core_buf.at[:, :, a.xs[q]]
                    else:
                        src, dst = self.buf.at[a.ys[q], 1], self.core_buf.at[a.ys[q]]
                    push(src, dst, self.send, self.recv.at[q], a.other)

    def core_came(self, q):
        landed(self.core_buf.at[0], self.recv.at[q])

    def add(self, p, q, z, extra):
        a = self.place
        y, x = a.yx(p, q)
        mine, theirs = self.buf.at[y, a.core, z, x], self.core_buf.at[y, z, x]
        add_up([mine, theirs] + [ref.at[z] for ref in extra], mine, LOW)

    def q_extra(self, p):
        return [self.q_buf.at[k, p] for k in range(self.place.n - 1)]

    def p_extra(self):
        return [self.p_buf.at[k] for k in range(self.place.n - 1)]

    def to_q(self, p, q):
        a = self.place

        def one(z, carry):
            self.add(p, q, z, [])
            return carry

        lax.fori_loop(0, a.nz, one, 0)
        y, x = a.yx(p, q)
        push(self.buf.at[y, a.core, :, x], self.q_buf.at[a.n - q - 1, p], self.send,
             self.recv.at[self.at_q + (a.n - q) * a.n + p], a.qp[q])

    def q_came(self, p):
        a = self.place
        for k in range(1, a.n):
            landed(self.q_buf.at[k - 1, p], self.recv.at[self.at_q + k * a.n + p])

    def to_p(self, p):
        a = self.place
        self.q_came(p)

        def one(z, carry):
            self.add(p, 0, z, self.q_extra(p))
            return carry

        lax.fori_loop(0, a.nz, one, 0)
        y, x = a.yx(p, 0)
        push(self.buf.at[y, a.core, :, x], self.p_buf.at[a.n - p - 1], self.send, self.recv.at[self.at_p + a.n - p], a.pp[p])

    def p_came(self):
        a = self.place
        self.q_came(0)
        for k in range(1, a.n):
            landed(self.p_buf.at[k - 1], self.recv.at[self.at_p + k])

    def to_z(self, k):
        a = self.place
        self.add(0, 0, a.zs[k], self.q_extra(0) + self.p_extra())
        t = self.buf.at[a.block(k, 0, 0)]
        push(t, self.z_buf.at[a.nz - k - 1], self.send, self.recv.at[self.at_z + a.nz - k], a.zp[k])

    def own(self):
        a = self.place
        for k in range(1, a.nz):
            landed(self.z_buf.at[k - 1], self.recv.at[self.at_z + k])
        mine, theirs = self.buf.at[a.block(0, 0, 0)], self.core_buf.at[a.y, a.z, a.x]
        extra = [ref.at[a.z] for ref in self.q_extra(0) + self.p_extra()]
        add_up([mine, theirs] + extra + [self.z_buf.at[k] for k in range(a.nz - 1)], self.out, FULL)

    def steps(self):
        a = self.place
        out = [self.start]
        for q in range(1, a.n):
            out.append(lambda q=q: self.core_came(q))
            for p in tuple(range(1, a.n)) + (0,):
                out.append(lambda p=p, q=q: self.to_q(p, q))
        out.append(lambda: self.core_came(0))
        for p in range(1, a.n):
            out.append(lambda p=p: self.to_p(p))
        out.append(self.p_came)
        for k in sorted(range(1, a.nz), key=lambda k: -min(k, a.nz - k)):
            out.append(lambda k=k: self.to_z(k))
        out.append(self.own)
        return out

    def drain(self):
        a = self.place
        landed(self.buf.at[:, 0], self.send)
        for _ in range(1, a.n):
            landed(self.buf.at[0, 0], self.send)
            landed(self.buf.at[0, 0, :, 0], self.send)
        landed(self.buf.at[0, 0, pl.ds(0, a.nz - 1), 0], self.send)


def add_up(refs, dst, kind):
    rows = dst.shape[0]
    step = next(v for v in (224, 144, 64, 48, 32, 16) if rows % v == 0)

    def one(t, carry):
        r = pl.ds(pl.multiple_of(t * step, step), step)
        value = refs[0][r, :].astype(FULL)
        for ref in refs[1:]:
            value += ref[r, :].astype(FULL)
        dst[r, :] = value.astype(kind)
        return carry

    lax.fori_loop(0, rows // step, one, 0)


def add_over_slice(place, tile, tiles, send, recv):
    axes = (
        (2, place.core, (None, place.other)), (place.n, place.y, place.yp), (place.n, place.x, place.xp),
        (place.nz, place.z, place.zp),
    )
    base = 0
    for size, own, peers in axes:
        mine = tiles.at[base + own]
        mine[...] = tile
        for k in range(1, size):
            push(mine, mine, send.at[base + k], recv.at[base + size - k], peers[k])
        for k in range(1, size):
            landed(tiles.at[base + wrap(own + k, size)], recv.at[base + k])
        tile = tiles[base]
        for k in range(1, size):
            tile += tiles[base + k]
        for k in range(1, size):
            landed(mine, send.at[base + k])
        base += size
    return tile


def step_kernel(
    place, loss_scale,
    pat, pos, seg, lab, tea, lm, gm,
    s0, s1, sg, shared,
    b0, b1, bg, r0c, r0q, r0p, r0z, r1c, r1q, r1p, r1z, rgc, rgq, rgp, rgz, flat, edge, stage, arrange,
    wqkv, wproj, wfc1, wfc2, wpat, wpos, whead, vecs,
    pos_col, seg_col, unit_a, inv_a, h_a, unit_b, inv_b, h_b, qkv, probs, attl, x0, x1, slope, act, kv, low, inv_c,
    tiles, sends, gather_recv, scatter_recv, tile_send, tile_recv,
):
    layer_rows, global_rows = lm.shape[1], gm.shape[0]
    place.locate()
    me = place.block(0, 0, 0)
    bg[me + (pl.ds(0, global_rows),)] = gm[...].astype(LOW)
    b0[me + (pl.ds(0, layer_rows),)] = lm[0].astype(LOW)
    b1[me + (pl.ds(0, layer_rows),)] = lm[1].astype(LOW)
    place.meet()
    gathers = [Gather(place, buf, sends.at[i], gather_recv.at[i]) for i, buf in enumerate((bg, b0, b1))]
    gather_g, gather_0, gather_1 = gathers
    for gather in gathers:
        gather.start()
    queue = []

    def pump(count=1):
        for _ in range(min(count, len(queue))):
            queue.pop(0)()

    head_of_lane = lax.broadcasted_iota(jnp.int32, (1, LANES), 1) // HEAD_DIM

    def each_block(low_end, high_end, one):
        def body(s, carry):
            x = lax.rem(s, place.nx)
            rest = lax.div(s, place.nx)
            z, rest = lax.rem(rest, place.nz), lax.div(rest, place.nz)
            one(s, (lax.div(rest, 2), lax.rem(rest, 2), z, x))
            return carry

        lax.fori_loop(low_end, high_end, body, 0)

    def spread(buf, rows, low_end=0, high_end=2 * place.n * place.n * place.nz):
        def one(s, t):
            if rows % 8 == 0:
                flat[pl.ds(pl.multiple_of(s * rows, 8), rows), :] = buf[t + (pl.ds(0, rows),)].astype(FULL)
            else:
                stage[: buf.shape[4], :] = buf[t].astype(FULL)

                def row(i, carry):
                    flat[pl.ds(s * rows + i, 1), :] = stage[pl.ds(i, 1), :]
                    return carry

                lax.fori_loop(0, rows, row, 0)

        each_block(low_end, high_end, one)

    def gather_rows(buf, rows, low_end=0, high_end=2 * place.n * place.n * place.nz):
        def one(s, t):
            if rows % 8 == 0:
                buf[t + (pl.ds(0, rows),)] = flat[pl.ds(pl.multiple_of(s * rows, 8), rows), :].astype(LOW)
            else:

                def row(i, carry):
                    stage[pl.ds(i, 1), :] = flat[pl.ds(s * rows + i, 1), :]
                    return carry

                lax.fori_loop(0, rows, row, 0)
                buf[t] = stage[: buf.shape[4], :].astype(LOW)

        each_block(low_end, high_end, one)

    def take(dst, at, rows, width):
        count = width // LANES

        def one(c, carry):
            value = flat[pl.ds(at + c, rows, stride=count), :].astype(LOW)
            dst[:rows, pl.ds(pl.multiple_of(c * LANES, LANES), LANES)] = value
            return carry

        lax.fori_loop(0, count, one, 0)

    def take_row(at, width):
        return jnp.concatenate([flat[at + i : at + i + 1, :] for i in range(width // LANES)], axis=1)

    def put_row(at, value):
        for i in range(value.shape[1] // LANES):
            flat[at + i : at + i + 1, :] = value[:, i * LANES : (i + 1) * LANES]

    def put(at, start, width, value, first=0):
        count = width // LANES
        rows = value.shape[0]
        for i in range(value.shape[1] // LANES):
            flat[pl.ds(at + start * count + first + i, rows, stride=count), :] = value[:, i * LANES : (i + 1) * LANES]

    for i in range(SEQ // LANES):
        lanes = slice(i * LANES, (i + 1) * LANES)
        for src, dst in ((pos, pos_col), (seg, seg_col)):
            dst[lanes, :] = jnp.transpose(jnp.broadcast_to(src[0:1, lanes].astype(FULL), (LANES, LANES)))
    pos_row = pos[0:1, :]
    seg_row = seg[0:1, :]
    picked_row = lax.broadcasted_iota(jnp.int32, (PICKED, 1), 0)
    picked_image = jnp.where(picked_row < IMAGES, picked_row, picked_row - IMAGES)
    picked_image = jnp.where(picked_row < 2 * IMAGES, picked_image, -1)
    picked_place = jnp.where(picked_row < IMAGES, TABLE, TABLE + 1)
    picker = ((seg_row == picked_image) & (pos_row == picked_place)).astype(FULL)
    picker_low = picker.astype(LOW)

    arr_row = lax.broadcasted_iota(jnp.int32, (D, GROUP * LANES), 0)
    arr_lane = lax.broadcasted_iota(jnp.int32, (D, GROUP * LANES), 1)
    arrange[...] = (
        (arr_row == (arr_lane % LANES) * GROUP + arr_lane // LANES) & (arr_lane % LANES < GROUPS)
    ).astype(FULL).astype(LOW)

    queue.extend(gather_g.steps())
    pump(99)
    queue.extend(gather_0.steps())
    pump(4)
    gather_g.last()
    gather_g.finish()
    spread(bg, global_rows)
    pump(99)
    take(wpat, PATCH_AT, PATCH, D)
    take(wpos, POS_AT, TABLE + 2, D)
    wpos[TABLE + 2 :, :] = jnp.zeros((wpos.shape[0] - TABLE - 2, D), LOW)

    def take_head(j, carry):
        value = flat[pl.ds(HEAD_AT + j, GROUPS, stride=GROUP_ROWS), :].astype(LOW)
        whead[:, pl.ds(pl.multiple_of(j * LANES, LANES), LANES)] = value
        return carry

    lax.fori_loop(0, GROUP_ROWS, take_head, 0)
    whead[:, GROUP_ROWS * LANES :] = jnp.zeros((GROUPS, LANES), LOW)
    patch_bias = take_row(PATCH_BIAS_AT, D)
    final_gain = take_row(FINAL_GAIN_AT, D)
    final_bias = take_row(FINAL_BIAS_AT, D)
    head_bias = take_row(HEAD_BIAS_AT, HEAD_LANES)

    row_at = (
        (PRE_GAIN_AT, D), (PRE_BIAS_AT, D), (QUERY_BIAS_AT, D), (VALUE_BIAS_AT, D), (PROJ_BIAS_AT, D),
        (MID_GAIN_AT, D), (MID_BIAS_AT, D), (FC1_BIAS_AT, FF), (FC2_BIAS_AT, D),
    )

    def take_layer(n, buf):
        spread(buf, layer_rows)
        take(wqkv.at[n], QKV_AT, D, 3 * D)
        take(wproj.at[n], PROJ_AT, D, D)
        take(wfc1.at[n], FC1_AT, D, FF)
        take(wfc2.at[n], FC2_AT, FF, D)
        for i, (at, width) in enumerate(row_at):
            vecs[n, i : i + 1, :width] = take_row(at, width)

    def vec(n, i):
        return vecs[n, i : i + 1, : row_at[i][1]]

    queue.extend(gather_1.steps())
    gather_0.last()
    pump(1)
    gather_0.finish()
    take_layer(0, b0)

    def tile_rows(i):
        return pl.ds(pl.multiple_of(i * ROWS, ROWS), ROWS)

    def onehot_of(place):
        iota = lax.broadcasted_iota(jnp.int32, (1, wpos.shape[0]), 1).astype(FULL)
        return (place == iota).astype(LOW)

    def embed(i, carry):
        r = tile_rows(i)
        place = pos_col[r, 0:1]
        pixel = dot(pat[r, :], wpat[...]) + patch_bias
        stream = dot(onehot_of(place), wpos[...]) + jnp.where(place < TABLE, pixel, 0.0)
        x0[r, :] = stream
        unit, inverse = normalise(stream)
        unit_a[r, :] = unit
        inv_a[r, :] = jnp.broadcast_to(inverse, (ROWS, LANES))
        h = (unit * vec(0, 0) + vec(0, 1)).astype(LOW)
        h_a[r, :] = h
        bias = jnp.concatenate([vec(0, 2), jnp.zeros((1, D), FULL), vec(0, 3)], axis=1)
        qkv[r, :] = (dot(h, wqkv[0]) + bias).astype(LOW)
        return carry

    lax.fori_loop(0, SEQ // ROWS, embed, 0)

    def window_rows(j):
        start = jnp.minimum((102 * j) // 16 * 16, SEQ - WINDOW)
        return pl.ds(pl.multiple_of(start, 16), WINDOW)

    def both(x):
        zero = jnp.zeros_like(x)
        return jnp.concatenate([jnp.where(head_of_lane == 0, x, zero), jnp.where(head_of_lane == 1, x, zero)], axis=0)

    def merge(x):
        return jnp.where(head_of_lane == 0, x[:WINDOW], x[WINDOW:])

    attl[...] = jnp.zeros_like(attl)

    def window_masks(j, r):
        own = seg_col[r, :]
        first = (2 * j).astype(FULL)
        mine = (own >= first) & (own < first + 2.0)
        other = jnp.transpose(jnp.where(mine, own, -1.0))
        pair = jnp.concatenate([own, own], axis=1) == jnp.concatenate([other, other], axis=1)
        return mine, pair

    def keep_own(mine, ref, r, lanes, value):
        ref[r, lanes] = jnp.where(mine, value, ref[r, lanes].astype(FULL)).astype(LOW)

    def attend(j, carry):
        r = window_rows(j)
        mine, pair = window_masks(j, r)
        for g in range(HEADS // 2):
            lanes = slice(g * LANES, (g + 1) * LANES)
            q2 = both(qkv[r, lanes])
            keys = qkv[r, D + g * LANES : D + (g + 1) * LANES]
            values = qkv[r, 2 * D + g * LANES : 2 * D + (g + 1) * LANES]
            scores = jnp.where(pair, dot_nt(keys, q2) * SCORE_SCALE, MASK_FILL)
            e = jnp.exp(scores - jnp.max(scores, axis=0, keepdims=True))
            p = jnp.where(pair, e * (1.0 / jnp.sum(e, axis=0, keepdims=True)), 0.0).astype(LOW)
            probs[j, g] = p
            keep_own(mine, attl, r, lanes, merge(dot_tn(p, values)))
        return carry

    for half in range(2):
        lax.fori_loop(half * WINDOWS // 2, (half + 1) * WINDOWS // 2, attend, 0)
        pump(2)

    def feed(i, carry):
        r = tile_rows(i)
        middle = x0[r, :] + dot(attl[r, :], wproj[0]) + vec(0, 4)
        unit, inverse = normalise(middle)
        unit_b[r, :] = unit
        inv_b[r, :] = jnp.broadcast_to(inverse, (ROWS, LANES))
        h = (unit * vec(0, 5) + vec(0, 6)).astype(LOW)
        h_b[r, :] = h
        for c in range(4):
            lanes = slice(c * D, (c + 1) * D)
            value, steep = gelu_parts(dot(h, wfc1[0, :, lanes]) + vecs[0, 7:8, lanes])
            act[r, lanes] = value.astype(LOW)
            slope[r, lanes] = steep.astype(LOW)
        x1[r, :] = middle + dot(act[r, :], wfc2[0]) + vec(0, 8)
        return carry

    lax.fori_loop(0, SEQ // ROWS, feed, 0)

    pump(99)
    gather_1.last()
    gather_1.finish()
    take_layer(1, b1)
    unit_c = x0
    h_c = low

    def kv_rows(i, carry):
        r = tile_rows(i)
        unit, inverse = normalise(x1[r, :])
        unit_c[r, :] = unit
        inv_c[r, :] = jnp.broadcast_to(inverse, (ROWS, LANES))
        h = (unit * vec(1, 0) + vec(1, 1)).astype(LOW)
        h_c[r, :] = h
        bias = jnp.concatenate([jnp.zeros((1, D), FULL), vec(1, 3)], axis=1)
        kv[r, :] = (dot(h, wqkv[1, :, D:]) + bias).astype(LOW)
        return carry

    lax.fori_loop(0, SEQ // ROWS, kv_rows, 0)

    h_s = dot(picker_low, h_c[...]).astype(LOW)
    x_s = sum(dot(picker_low, part) for part in exact_parts(x1[...]))
    q_s = (dot(h_s, wqkv[1, :, :D]) + vec(1, 2)).astype(LOW)
    stack_rows = lax.broadcasted_iota(jnp.int32, (HEADS * PICKED, 1), 0)
    stack_lanes = lax.broadcasted_iota(jnp.int32, (1, D), 1)
    own_head = (stack_rows // PICKED) == (stack_lanes // HEAD_DIM)

    def stack(x):
        tall = jnp.concatenate([x.astype(FULL)] * HEADS, axis=0)
        return jnp.where(own_head, tall, 0.0).astype(LOW)

    def unstack(x):
        x = jnp.where(own_head, x, 0.0)
        total = x[:PICKED]
        for h in range(1, HEADS):
            total += x[h * PICKED : (h + 1) * PICKED]
        return total

    q6 = stack(q_s)
    image6 = jnp.concatenate([picked_image] * HEADS, axis=0)
    mask6 = image6 == seg_row
    scores = jnp.where(mask6, dot_nt(q6, kv[:, :D]) * SCORE_SCALE, MASK_FILL)
    e = jnp.exp(scores - jnp.max(scores, axis=-1, keepdims=True))
    p6 = e / jnp.sum(e, axis=-1, keepdims=True)
    p6_low = p6.astype(LOW)
    att_s = unstack(dot(p6_low, kv[:, D:])).astype(LOW)
    mid_s = x_s + dot(att_s, wproj[1]) + vec(1, 4)
    unit_m, inv_m = normalise(mid_s)
    h2_s = (unit_m * vec(1, 5) + vec(1, 6)).astype(LOW)
    act_s, steep_s = gelu_parts(dot(h2_s, wfc1[1]) + vec(1, 7))
    act_s = act_s.astype(LOW)
    x2_s = mid_s + dot(act_s, wfc2[1]) + vec(1, 8)

    unit_f, inv_f = normalise(x2_s)
    summary = (unit_f * final_gain + final_bias).astype(LOW)
    arranged = dot(summary, arrange[...]).astype(LOW)
    logits = head_bias
    spans = []
    for k in range(GROUP):
        at = 2 * CLASSES * k
        block, shift = at // LANES, at % LANES
        blocks = (at + 2 * CLASSES - 1) // LANES - block + 1
        spans.append((block, shift, blocks))
        s_k = arranged[:, k * LANES : k * LANES + GROUPS]
        wide = (HEAD_LANES // LANES + 1) * LANES
        part = dot(s_k, whead[:, block * LANES : block * LANES + wide])
        if shift:
            part = pltpu.roll(part, wide - shift, 1)
        logits = logits + part[:, :HEAD_LANES]
    column = lax.broadcasted_iota(jnp.int32, (PICKED, HEAD_LANES), 1)
    second = picked_row >= IMAGES
    low_end = jnp.where(second, CLASSES, 0)
    valid = (column >= low_end) & (column < low_end + CLASSES)
    live = picked_row < 2 * IMAGES
    target = jnp.zeros((PICKED, 1), jnp.int32)
    for i in range(IMAGES):
        target = jnp.where(picked_row == i, lab[0, i], target)
        target = jnp.where(picked_row == IMAGES + i, CLASSES + tea[0, i], target)
    hit = column == target
    logits = jnp.where(valid, logits, -3e38)
    top = jnp.max(logits, axis=-1, keepdims=True)
    e = jnp.exp(logits - top)
    total = jnp.sum(e, axis=-1, keepdims=True)
    hit_logit = jnp.sum(jnp.where(hit, logits, 0.0), axis=-1, keepdims=True)
    each = jnp.where(live, top + jnp.log(total) - hit_logit, 0.0)
    loss_sum = jnp.sum(each, axis=0, keepdims=True)
    grad_logits = jnp.where(live, (e / total - hit.astype(FULL)) * loss_scale, 0.0)
    grad_low = grad_logits.astype(LOW)
    grad_wide = jnp.concatenate([grad_low.astype(FULL), jnp.zeros((PICKED, LANES), FULL)], axis=1)

    grad_arranged = []
    for k, (block, shift, blocks) in enumerate(spans):
        turned = (pltpu.roll(grad_wide, shift, 1) if shift else grad_wide).astype(LOW)
        turned = turned[:, : blocks * LANES]
        s_k = arranged[:, k * LANES : k * LANES + GROUPS]
        grad_w = dot_tn(s_k, turned)
        for j in range(blocks):
            rows = pl.ds(HEAD_AT + block + j, GROUPS, stride=GROUP_ROWS)
            piece = grad_w[:, j * LANES : (j + 1) * LANES]
            if k and j == 0:
                piece = piece + flat[rows, :]
            flat[rows, :] = piece
        back = dot_nt(turned, whead[:, block * LANES : (block + blocks) * LANES])
        grad_arranged.append(jnp.concatenate([back, jnp.zeros((PICKED, LANES - GROUPS), FULL)], axis=1))
    parts = jnp.concatenate(exact_parts(jnp.concatenate(grad_arranged, axis=1)), axis=0)
    parts = dot_nt(parts, arrange[...])
    grad_summary = parts[:PICKED] + parts[PICKED : 2 * PICKED] + parts[2 * PICKED :]
    put_row(HEAD_BIAS_AT, col_sum(grad_low))
    put_row(FINAL_GAIN_AT, col_sum(grad_summary * unit_f))
    put_row(FINAL_BIAS_AT, col_sum(grad_summary))
    flat[GLOBAL_END:GLOBAL_ALL, :] = jnp.zeros((GLOBAL_ALL - GLOBAL_END, LANES), FULL)
    for gather in gathers:
        gather.drain()
    border = FINAL_GAIN_AT // global_rows
    gather_rows(bg, global_rows, border + 1)
    kept = (border + 1) * global_rows - FINAL_GAIN_AT
    edge[:kept, :] = flat[FINAL_GAIN_AT : FINAL_GAIN_AT + kept, :]
    dx_s = norm_back(grad_summary, final_gain, unit_f, inv_f)

    out_s = dx_s.astype(LOW)
    for c in range(4):
        put(FC2_AT, c * D, D, dot_tn(act_s[:, c * D : (c + 1) * D], out_s))
    put_row(FC2_BIAS_AT, col_sum(out_s))
    gpre_s = (dot_nt(out_s, wfc2[1]) * steep_s).astype(LOW)
    put(FC1_AT, 0, FF, dot_tn(h2_s, gpre_s))
    put_row(FC1_BIAS_AT, col_sum(gpre_s))
    gh2_s = dot_nt(gpre_s, wfc1[1])
    put_row(MID_GAIN_AT, col_sum(gh2_s * unit_m))
    put_row(MID_BIAS_AT, col_sum(gh2_s))
    gmid_s = dx_s + norm_back(gh2_s, vec(1, 5), unit_m, inv_m)
    gmid_low = gmid_s.astype(LOW)
    put(PROJ_AT, 0, D, dot_tn(att_s, gmid_low))
    put_row(PROJ_BIAS_AT, col_sum(gmid_low))
    gatt6 = stack(dot_nt(gmid_low, wproj[1]).astype(LOW))
    gprob = dot_nt(gatt6, kv[:, D:])
    gscore = (p6 * (gprob - jnp.sum(p6 * gprob, axis=-1, keepdims=True))).astype(LOW)
    gq_s = (unstack(dot(gscore, kv[:, :D])) * SCORE_SCALE).astype(LOW)
    gkeys = (dot_tn(gscore, q6) * SCORE_SCALE).astype(LOW)
    gvalues = dot_tn(p6_low, gatt6).astype(LOW)
    put_row(QUERY_BIAS_AT, col_sum(gq_s))
    put_row(VALUE_BIAS_AT, col_sum(gvalues))
    kv[:, :D] = gkeys
    kv[:, D:] = gvalues
    put(QKV_AT, 0, 3 * D, dot_tn(h_s, gq_s))
    put(QKV_AT, 0, 3 * D, dot_tn(h_c[...], kv[:, :D]), 3)
    put(QKV_AT, 0, 3 * D, dot_tn(h_c[...], kv[:, D:]), 6)
    back_s = jnp.concatenate([dot_nt(gq_s, wqkv[1, :, :D]), gmid_s], axis=1)

    back_parts = jnp.concatenate(exact_parts(back_s), axis=0)
    dx = x1

    def kv_back(i, carry):
        gain_sum, bias_sum = carry
        r = tile_rows(i)
        image_col = seg_col[r, 0:1]
        place_col = pos_col[r, 0:1]
        lane = lax.broadcasted_iota(jnp.int32, (1, PICKED), 1).astype(FULL)
        lane_image = jnp.where(lane < IMAGES, lane, lane - IMAGES)
        lane_place = jnp.where(lane < IMAGES, float(TABLE), TABLE + 1.0)
        back_pick = (
            (image_col == lane_image) & (place_col == lane_place) & (lane < 2.0 * IMAGES)
        ).astype(LOW)
        back = dot(jnp.concatenate([back_pick] * 3, axis=1), back_parts)
        grad = back[:, :D] + dot_nt(kv[r, :], wqkv[1, :, D:])
        unit = unit_c[r, :]
        dx[r, :] = back[:, D:] + norm_back(grad, vec(1, 0), unit, inv_c[r, 0:1])
        return gain_sum + col_sum(grad * unit), bias_sum + col_sum(grad)

    zero_row = jnp.zeros((1, D), FULL)
    gain_sum, bias_sum = lax.fori_loop(0, SEQ // ROWS, kv_back, (zero_row, zero_row))
    put_row(PRE_GAIN_AT, gain_sum)
    put_row(PRE_BIAS_AT, bias_sum)
    flat[LAYER_END:, :] = jnp.zeros((LAYER_ALL - LAYER_END, LANES), FULL)
    gather_rows(b1, layer_rows)
    scatter_1 = Scatter(place, b1, r1c, r1q, r1p, r1z, s1, sends.at[3], scatter_recv.at[0])
    queue.extend(scatter_1.steps())
    pump(1)

    def feed_back(i, carry):
        fc1_sum, fc2_sum, proj_sum, gain_sum, bias_sum = carry
        r = tile_rows(i)
        grad_out = dx[r, :]
        out_low = grad_out.astype(LOW)
        low[r, :] = out_low
        for c in range(4):
            lanes = slice(c * D, (c + 1) * D)
            slope[r, lanes] = (dot_nt(out_low, wfc2[0, lanes, :]) * slope[r, lanes].astype(FULL)).astype(LOW)
        grad_h = dot_nt(slope[r, :], wfc1[0])
        unit = unit_b[r, :]
        middle = grad_out + norm_back(grad_h, vec(0, 5), unit, inv_b[r, 0:1])
        dx[r, :] = middle
        middle_low = middle.astype(LOW)
        h2low[r, :] = middle_low
        gatt[r, :] = dot_nt(middle_low, wproj[0]).astype(LOW)
        return (
            fc1_sum + col_sum(slope[r, :]), fc2_sum + col_sum(out_low), proj_sum + col_sum(middle_low),
            gain_sum + col_sum(grad_h * unit), bias_sum + col_sum(grad_h),
        )

    h2low = kv.at[:, 0:D]
    gatt = kv.at[:, D : 2 * D]
    sums = lax.fori_loop(0, SEQ // ROWS, feed_back, (jnp.zeros((1, FF), FULL),) + (zero_row,) * 4)
    pump(3)
    for at, value in zip((FC1_BIAS_AT, FC2_BIAS_AT, PROJ_BIAS_AT, MID_GAIN_AT, MID_BIAS_AT), sums):
        put_row(at, value)

    for c in range(4):
        lanes = slice(c * D, (c + 1) * D)
        put(FC2_AT, c * D, D, dot_tn(act[:, lanes], low[...]))
        put(FC1_AT, 0, FF, dot_tn(h_b[...], slope[:, lanes]), 3 * c)
    put(PROJ_AT, 0, D, dot_tn(attl[...], h2low[...]))

    pump(2)

    def attend_back(j, carry):
        r = window_rows(j)
        mine, _ = window_masks(j, r)
        for g in range(HEADS // 2):
            lanes = slice(g * LANES, (g + 1) * LANES)
            key_lanes = slice(D + g * LANES, D + (g + 1) * LANES)
            value_lanes = slice(2 * D + g * LANES, 2 * D + (g + 1) * LANES)
            q2 = both(qkv[r, lanes])
            go2 = both(gatt[r, lanes])
            keys = qkv[r, key_lanes]
            p_low = probs[j, g]
            p = p_low.astype(FULL)
            gp = dot_nt(qkv[r, value_lanes], go2)
            gs = (p * (gp - jnp.sum(p * gp, axis=0, keepdims=True))).astype(LOW)
            keep_own(mine, qkv, r, lanes, merge(dot_tn(gs, keys)) * SCORE_SCALE)
            keep_own(mine, qkv, r, key_lanes, dot(gs, q2) * SCORE_SCALE)
            keep_own(mine, qkv, r, value_lanes, dot(p_low, go2))
        return carry

    for half in range(2):
        lax.fori_loop(half * WINDOWS // 2, (half + 1) * WINDOWS // 2, attend_back, 0)
        pump(2)

    def qkv_back(i, carry):
        query_sum, value_sum, gain_sum, bias_sum, embed_sum = carry
        r = tile_rows(i)
        held = seg_col[r, 0:1] < float(IMAGES)
        grads = jnp.where(held, qkv[r, :].astype(FULL), 0.0)
        gq, gv = grads[:, :D], grads[:, 2 * D :]
        qkv[r, :] = grads.astype(LOW)
        grad = dot_nt(qkv[r, :], wqkv[0])
        unit = unit_a[r, :]
        full = dx[r, :] + norm_back(grad, vec(0, 0), unit, inv_a[r, 0:1])
        dx[r, :] = full
        place = pos_col[r, 0:1]
        pixel = jnp.where(place < TABLE, full, 0.0).astype(LOW)
        low[r, :] = pixel
        return (
            query_sum + col_sum(gq), value_sum + col_sum(gv), gain_sum + col_sum(grad * unit),
            bias_sum + col_sum(grad), embed_sum + col_sum(pixel),
        )

    sums = lax.fori_loop(0, SEQ // ROWS, qkv_back, (zero_row,) * 5)
    for at, value in zip((QUERY_BIAS_AT, VALUE_BIAS_AT, PRE_GAIN_AT, PRE_BIAS_AT), sums):
        put_row(at, value)
    for c in range(3):
        put(QKV_AT, 0, 3 * D, dot_tn(h_a[...], qkv[:, c * D : (c + 1) * D]), 3 * c)
    pump(99)
    gather_rows(b0, layer_rows)
    scatter_0 = Scatter(place, b0, r0c, r0q, r0p, r0z, s0, sends.at[4], scatter_recv.at[1])
    queue.extend(scatter_0.steps())
    pump(1)

    for c in range(2):
        put(PATCH_AT, c * D, D, dot_tn(pat[:, c * D : (c + 1) * D], low[...]))
    place_col = pos_col[:, 0:1]
    onehot = onehot_of(place_col)
    high = dx[...].astype(LOW)
    rest = (dx[...] - high.astype(FULL)).astype(LOW)
    table = dot_tn(onehot, high) + dot_tn(onehot, rest)
    put(POS_AT, 0, D, table[: TABLE + 2])
    put_row(PATCH_BIAS_AT, sums[4])
    flat[FINAL_GAIN_AT : FINAL_GAIN_AT + kept, :] = edge[:kept, :]
    gather_rows(bg, global_rows, 0, border + 1)
    scatter_g = Scatter(place, bg, rgc, rgq, rgp, rgz, sg, sends.at[5], scatter_recv.at[2])
    steps_0, steps_g = queue, scatter_g.steps()
    steps_g.pop(0)()
    queue = []
    while steps_0 or steps_g:
        for steps in (steps_0, steps_g):
            if steps:
                steps.pop(0)()

    squares = jnp.zeros((1, 1), FULL)
    for s, rows in ((s0, layer_rows), (s1, layer_rows), (sg, global_rows)):
        used = s[:rows, :]
        squares += jnp.sum(jnp.sum(used * used, axis=0, keepdims=True), axis=1, keepdims=True)
    row = lax.broadcasted_iota(jnp.int32, (8, LANES), 0)
    tile = jnp.where(row == 0, squares, loss_sum)
    shared[...] = add_over_slice(place, tile, tiles, tile_send, tile_recv)
    for scatter in (scatter_1, scatter_0, scatter_g):
        scatter.drain()


def padded(rows):
    return rows + -rows % 16


def step_call(place, loss_scale, pat, pos, seg, lab, tea, lm, gm):
    vmem = pl.BlockSpec(memory_space=pltpu.VMEM)
    smem = pl.BlockSpec(memory_space=pltpu.SMEM)
    n, nz = place.n, place.nz
    rows = padded(lm.shape[1]), padded(lm.shape[1]), padded(gm.shape[0])

    def shape(*dims, kind=FULL):
        return pltpu.VMEM(dims, kind)

    def low(*dims):
        return pltpu.VMEM(dims, LOW)

    scratch = [low(n, 2, nz, n, r, LANES) for r in rows]
    for r in rows:
        scratch += [
            low(n, nz, n, r, LANES), low(n - 1, n, nz, r, LANES), low(n - 1, nz, r, LANES), low(nz - 1, r, LANES)
        ]
    tiles = 2 + 2 * n + nz
    scratch += [
        shape(LAYER_ALL, LANES), shape(gm.shape[0] + 8, LANES), shape(rows[0], LANES), low(D, GROUP * LANES),
        low(2, D, 3 * D), low(2, D, D), low(2, D, FF), low(2, FF, D),
        low(PATCH, D), low(256, D), low(GROUPS, (GROUP_ROWS + 1) * LANES),
        shape(2, 16, FF),
        shape(SEQ, LANES), shape(SEQ, LANES),
        shape(SEQ, D), shape(SEQ, LANES), low(SEQ, D),
        shape(SEQ, D), shape(SEQ, LANES), low(SEQ, D),
        low(SEQ, 3 * D), low(WINDOWS, HEADS // 2, WINDOW, 2 * WINDOW),
        low(SEQ, D), shape(SEQ, D), shape(SEQ, D),
        low(SEQ, FF), low(SEQ, FF), low(SEQ, 2 * D), low(SEQ, D), shape(SEQ, LANES),
        shape(tiles, 8, LANES),
        pltpu.SemaphoreType.DMA((6,)),
        pltpu.SemaphoreType.DMA((3, nz + nz * n + 2 * n)), pltpu.SemaphoreType.DMA((3, 2 * n + n * n + nz)),
        pltpu.SemaphoreType.DMA((tiles,)), pltpu.SemaphoreType.DMA((tiles,)),
    ]
    return pl.pallas_call(
        functools.partial(step_kernel, place, loss_scale),
        out_shape=[jax.ShapeDtypeStruct((r, LANES), FULL) for r in rows] + [jax.ShapeDtypeStruct((8, LANES), FULL)],
        in_specs=[vmem] * 3 + [smem] * 2 + [vmem] * 2,
        out_specs=[vmem] * 4,
        scratch_shapes=scratch,
        compiler_params=pltpu.CompilerParams(collective_id=0, has_side_effects=True, vmem_limit_bytes=VMEM_BYTES),
    )(pat, pos, seg, lab, tea, lm, gm)

def adam(master, moment, second, gradient, factor):
    clipped = gradient * factor
    new_moment = BETA_ONE * moment + (1.0 - BETA_ONE) * clipped
    new_second = BETA_TWO * second + (1.0 - BETA_TWO) * clipped * clipped
    fix_one = 1.0 - BETA_ONE**STEP
    fix_two = 1.0 - BETA_TWO**STEP
    update = new_moment / fix_one / (jnp.sqrt(new_second / fix_two) + ADAM_EPS) + WEIGHT_DECAY * master
    return master - LEARN_RATE * update, new_moment, new_second


def shards(sizes, pat, pos, seg, lab, tea, lm, lo, ls, gm, go, gs):
    place = Place(sizes)
    rows, global_rows = lm.shape[1] // LANES, gm.shape[0] // LANES
    loss_scale = 1.0 / (2 * IMAGES * sizes[0] * sizes[1])
    assert pat.shape[0] == 1 and (lm.shape[1], gm.shape[0]) == (rows * LANES, global_rows * LANES)
    assert sizes[0] * sizes[1] * rows == LAYER_ALL and sizes[0] * sizes[1] * global_rows == GLOBAL_ALL
    s0, s1, sg, total = step_call(
        place, loss_scale, pat[0], pos, seg, lab, tea,
        lm.reshape(2, rows, LANES), gm.reshape(global_rows, LANES),
    )
    layer = jnp.stack([s0[:rows].reshape(-1), s1[:rows].reshape(-1)])
    gg = sg[:global_rows].reshape(-1)
    norm = jnp.sqrt(total[0, 0])
    factor = jnp.minimum(1.0, CLIP_NORM / norm)
    return adam(lm, lo, ls, layer, factor) + adam(gm, go, gs, gg, factor) + (norm, total[1, 0])


def solution(mesh):
    axes = tuple(mesh.axis_names)
    split = P(axes)
    wide = P(None, axes)
    return jax.shard_map(
        functools.partial(shards, tuple(mesh.shape[a] for a in axes)),
        mesh=mesh,
        in_specs=(split,) * 5 + (wide,) * 3 + (split,) * 3,
        out_specs=(wide,) * 3 + (split,) * 3 + (P(), P()),
        check_vma=False,
    )
```

```python
import functools

import jax
import jax.numpy as jnp
from jax import lax
from jax.experimental import pallas as pl
from jax.experimental.pallas import tpu as pltpu
from jax.sharding import PartitionSpec as P

D = 384
HEADS = 6
HEAD_DIM = 64
FF = 1536
CLASSES = 1000
PATCH = 768
TABLE = 196
IMAGES = 15
SEQ = 768
STEP = 10
LANES = 128

NORM_EPS = 1e-06
BETA_ONE = 0.9
BETA_TWO = 0.999
ADAM_EPS = 1e-08
LEARN_RATE = 0.1
WEIGHT_DECAY = 0.05
CLIP_NORM = 0.01
MASK_FILL = -1000000000.0
SCORE_SCALE = HEAD_DIM ** (-0.5)
LOW = jnp.bfloat16
FULL = jnp.float32
HIGHEST = lax.Precision.HIGHEST

QKV_AT, PROJ_AT, FC1_AT, FC2_AT = 0, 3456, 4608, 9216
PRE_GAIN_AT, PRE_BIAS_AT, QUERY_BIAS_AT, VALUE_BIAS_AT = 13824, 13827, 13830, 13833
PROJ_BIAS_AT, MID_GAIN_AT, MID_BIAS_AT, FC1_BIAS_AT, FC2_BIAS_AT = 13836, 13839, 13842, 13845, 13857
LAYER_END = 13860
PATCH_AT, POS_AT, PATCH_BIAS_AT, FINAL_GAIN_AT, FINAL_BIAS_AT = 0, 2304, 2898, 2901, 2904
HEAD_AT, HEAD_BIAS_AT, GLOBAL_END = 2907, 8907, 8923
GROUP, GROUP_ROWS, GROUPS = 8, 125, 48
HEAD_LANES = 2048
PICKED = 32
WINDOWS, WINDOW = 8, 128
ROWS = 256
LAYER_ALL, GLOBAL_ALL = 14080, 8960
VMEM_BYTES = 64 * 1024 * 1024 - 64 * 1024
MESH = pl.DeviceIdType.MESH


def dot(a, b, dims=(1, 0), precision=None):
    return lax.dot_general(
        a, b, (((dims[0],), (dims[1],)), ((), ())), precision=precision, preferred_element_type=FULL
    )


def dot_nt(a, b, precision=None):
    return dot(a, b, (1, 1), precision)


def dot_tn(a, b, precision=None):
    return dot(a, b, (0, 0), precision)


def row_mean(x):
    return jnp.sum(x, axis=-1, keepdims=True) * (1.0 / D)


def normalise(x):
    center = x - row_mean(x)
    inverse = lax.rsqrt(row_mean(center * center) + NORM_EPS)
    return center * inverse, inverse


def norm_back(grad, gain, unit, inverse):
    scaled = grad * gain
    return inverse * (scaled - row_mean(scaled) - unit * row_mean(scaled * unit))


def col_sum(x):
    return jnp.sum(x.astype(FULL), axis=0, keepdims=True)


def gelu_parts(x):
    size = jnp.abs(x)
    bell = jnp.exp(-0.5 * x * x)
    base = 1.0 + (0.3275911 * 0.7071067811865476) * size
    t = pl.reciprocal(base, approx=True)
    t = t * (2.0 - base * t)
    tail = ((((1.061405429 * t - 1.453152027) * t + 1.421413741) * t - 0.284496736) * t + 0.254829592) * t
    tail = 0.5 * tail * bell
    phi = jnp.where(x < 0, tail, 1.0 - tail)
    return x * phi, phi + x * (bell * 0.3989422804014327)


def exact_parts(x):
    high = x.astype(LOW)
    rest = x - high.astype(FULL)
    middle = rest.astype(LOW)
    return high, middle, (rest - middle.astype(FULL)).astype(LOW)


def wrap(value, size):
    return jnp.where(value >= size, value - size, value)


class Place:
    def __init__(self, sizes):
        dp, fsdp = sizes
        self.n = self.ny = self.nx = dp // 2
        self.nz = fsdp // self.nx
        assert dp == 2 * self.n and fsdp == self.n * self.nz

    def locate(self):
        dp, fsdp = lax.axis_index("dp"), lax.axis_index("fsdp")
        self.y, self.core = dp // 2, dp % 2
        self.z, self.x = fsdp // self.nx, fsdp % self.nx
        self.even = self.core == 0
        self.zs = [wrap(self.z + k, self.nz) for k in range(self.nz)]
        self.ys = [wrap(self.y + k, self.n) for k in range(self.n)]
        self.xs = [wrap(self.x + k, self.n) for k in range(self.n)]
        spans = [(p, q) for p in range(self.n) for q in range(self.n)]
        self.short = {
            (p, q): (jnp.where(self.even, self.ys[p], self.ys[q]), jnp.where(self.even, self.xs[q], self.xs[p]))
            for p, q in spans
        }

    def yx(self, p, q):
        return self.short[p, q]

    def block(self, dz, p, q):
        y, x = self.yx(p, q)
        return y, self.core, self.zs[dz], x

    def device(self, y, core, z, x):
        return y * 2 + core, z * self.nx + x

    def yx_other(self, p, q):
        return jnp.where(self.even, self.ys[q], self.ys[p]), jnp.where(self.even, self.xs[p], self.xs[q])

    def index(self, y, core, z, x):
        return ((y * 2 + core) * self.nz + z) * self.nx + x

    def meet(self):
        def there(y=0, core=0, z=0, x=0):
            return self.device(self.ys[y], 1 - self.core if core else self.core, self.zs[z], self.xs[x])

        self.other = there(core=1)
        self.zp = [there(z=k) for k in range(self.nz)]
        self.pp = [self.device(*self.block(0, k, 0)) for k in range(self.n)]
        self.qp = [self.device(*self.block(0, 0, k)) for k in range(self.n)]
        self.tall = [there(core=c, z=k) for c in range(2) for k in range(self.nz)][1:]
        self.flat = [there(y=j, x=k) for j in range(self.n) for k in range(self.n)][1:]
        barrier = pltpu.get_barrier_semaphore()
        for peer in self.tall + self.flat:
            pl.semaphore_signal(barrier, inc=1, device_id=peer, device_id_type=MESH)
        pl.semaphore_wait(barrier, len(self.tall + self.flat))


def push(src, dst, send, recv, peer):
    pltpu.make_async_remote_copy(
        src_ref=src, dst_ref=dst, send_sem=send, recv_sem=recv, device_id=peer, device_id_type=MESH
    ).start()


def landed(dst, recv):
    pltpu.make_async_copy(dst, dst, recv).wait()


class Gather:
    def __init__(self, place, buf, send, recv):
        self.place, self.buf, self.send, self.recv = place, buf, send, recv
        self.from_p = place.nz
        self.from_q = self.from_p + place.nz * place.n
        self.from_core = self.from_q + place.n

    def to_p(self, dz):
        a, t = self.place, self.buf.at[self.place.block(dz, 0, 0)]
        for k in range(1, a.n):
            push(t, t, self.send, self.recv.at[self.from_p + dz * a.n + a.n - k], a.pp[k])

    def to_q(self, dz, p):
        a, t = self.place, self.buf.at[self.place.block(dz, p, 0)]
        for k in range(1, a.n):
            push(t, t, self.send, self.recv.at[self.from_q + a.n - k], a.qp[k])

    def start(self):
        a, t = self.place, self.buf.at[self.place.block(0, 0, 0)]
        self.to_p(0)
        for k in range(1, a.nz):
            push(t, t, self.send, self.recv.at[a.nz - k], a.zp[k])
        self.to_q(0, 0)

    def z_came(self, dz):
        landed(self.buf.at[self.place.block(dz, 0, 0)], self.recv.at[dz])
        self.to_p(dz)
        self.to_q(dz, 0)

    def p_came(self, dz, p):
        landed(self.buf.at[self.place.block(dz, p, 0)], self.recv.at[self.from_p + dz * self.place.n + p])
        self.to_q(dz, p)

    def group(self, core, q):
        a = self.place
        return self.buf.at[:, 0, :, a.xs[q]] if core == 0 else self.buf.at[a.ys[q], 1]

    def to_core(self, q):
        a = self.place
        for core in range(2):

            @pl.when(a.core == core)
            def _():
                t = self.group(core, q)
                push(t, t, self.send, self.recv.at[self.from_core + q], a.other)

    def q_came(self, q):
        landed(self.buf.at[:, 0, :, 0], self.recv.at[self.from_q + q])
        self.to_core(q)

    def steps(self):
        a = self.place
        near = sorted(range(1, a.nz), key=lambda k: min(k, a.nz - k))
        out = [lambda p=p: self.p_came(0, p) for p in range(1, a.n)]
        out += [lambda k=k: self.z_came(k) for k in near]
        out += [lambda k=k, p=p: self.p_came(k, p) for k in near for p in range(1, a.n)]
        out += [lambda: self.to_core(0)]
        return out

    def last(self):
        for q in range(1, self.place.n):
            self.q_came(q)

    def finish(self):
        for q in range(self.place.n):
            landed(self.buf.at[:, 0, :, 0], self.recv.at[self.from_core + q])

    def drain(self):
        a = self.place
        for t in (self.buf.at[:, 0], self.buf.at[:, 0, :, pl.ds(0, a.n - 1)], self.buf.at[0, 0, :, pl.ds(0, a.n - 1)]):
            landed(t, self.send)
        landed(self.buf.at[0, 0, pl.ds(0, a.nz - 1), 0], self.send)


class Scatter:
    def __init__(self, place, buf, from_core, from_q, from_p, from_z, out, send, recv, late=None):
        self.place, self.buf, self.out, self.send, self.recv, self.late = place, buf, out, send, recv, late
        self.core_buf, self.q_buf, self.p_buf, self.z_buf = from_core, from_q, from_p, from_z
        n, nz = place.n, place.nz
        self.at_q = n * n * nz
        self.at_p = self.at_q + n * n * nz
        self.at_z = self.at_p + n * nz
        self.sent = []
        self.far = tuple(range(1, n))
        self.order = sorted(range(1, nz), key=lambda k: -min(k, nz - k)) + [0]

    def when(self, turn, block, body):
        if self.late is None:
            body()
        else:
            late = self.late(self.place.index(*block))
            pl.when(late if turn else jnp.logical_not(late))(body)

    def send_on(self, turn, block, src, dst, recv, peer):
        push(src, dst, self.send, recv, peer)
        self.sent.append((turn, block, src))

    def block(self, p, q, k):
        y, x = self.place.yx(p, q)
        return y, self.place.core, self.place.zs[k], x

    def start(self, turn=0):
        a = self.place
        for q in self.far + (0,):
            for k in self.order:
                for p in self.far + (0,):
                    y, x = a.yx_other(p, q)
                    z = a.zs[k]
                    block = y, 1 - a.core, z, x
                    recv = self.recv.at[(q * a.n + p) * a.nz + k]
                    self.when(turn, block, lambda: self.send_on(
                        turn, block, self.buf.at[block], self.core_buf.at[y, z, x], recv, a.other))

    def add(self, p, q, k, extra, out=None):
        a = self.place
        y, core, z, x = self.block(p, q, k)
        mine, theirs = self.buf.at[y, core, z, x], self.core_buf.at[y, z, x]
        landed(theirs, self.recv.at[(q * a.n + p) * a.nz + k])
        refs = [mine, theirs] + extra
        if out is None:
            add_up(refs, mine)
        else:
            out(refs)
        return mine

    def to_q(self, turn, p, q, k):
        a = self.place
        block = self.block(p, q, k)

        def body():
            mine = self.add(p, q, k, [])
            recv = self.recv.at[self.at_q + ((a.n - q) * a.n + p) * a.nz + k]
            self.send_on(turn, block, mine, self.q_buf.at[a.n - q - 1, p, a.zs[k]], recv, a.qp[q])

        self.when(turn, block, body)

    def q_came(self, p, k):
        a = self.place
        refs = [self.q_buf.at[q - 1, p, a.zs[k]] for q in self.far]
        for q, ref in zip(self.far, refs):
            landed(ref, self.recv.at[self.at_q + (q * a.n + p) * a.nz + k])
        return refs

    def to_p(self, turn, p, k):
        a = self.place
        block = self.block(p, 0, k)

        def body():
            mine = self.add(p, 0, k, self.q_came(p, k))
            recv = self.recv.at[self.at_p + (a.n - p) * a.nz + k]
            self.send_on(turn, block, mine, self.p_buf.at[a.n - p - 1, a.zs[k]], recv, a.pp[p])

        self.when(turn, block, body)

    def p_came(self, k):
        a = self.place
        refs = [self.p_buf.at[p - 1, a.zs[k]] for p in self.far]
        for p, ref in zip(self.far, refs):
            landed(ref, self.recv.at[self.at_p + p * a.nz + k])
        return refs

    def to_z(self, turn, k):
        a = self.place
        block = self.block(0, 0, k)

        def body():
            mine = self.add(0, 0, k, self.q_came(0, k) + self.p_came(k))
            recv = self.recv.at[self.at_z + a.nz - k]
            self.send_on(turn, block, mine, self.z_buf.at[a.nz - k - 1], recv, a.zp[k])

        self.when(turn, block, body)

    def own(self, turn=0):
        a = self.place

        def body():
            extra = self.q_came(0, 0) + self.p_came(0)
            for k in range(1, a.nz):
                landed(self.z_buf.at[k - 1], self.recv.at[self.at_z + k])
            self.add(0, 0, 0, extra + [self.z_buf.at[k] for k in range(a.nz - 1)], self.out)

        self.when(turn, self.block(0, 0, 0), body)

    def stages(self, turn=0):
        return [
            (
                [lambda k=k, p=p, q=q: self.to_q(turn, p, q, k) for q in self.far for p in self.far + (0,)],
                [lambda k=k, p=p: self.to_p(turn, p, k) for p in self.far],
                [(lambda k=k: self.to_z(turn, k)) if k else (lambda: self.own(turn))],
            )
            for k in self.order
        ]

    def queues(self, turn=0):
        stages = self.stages(turn)
        return [[step for stage in stages for step in stage[i]] for i in range(3)]

    def drain(self):
        for turn, block, src in self.sent:
            self.when(turn, block, lambda: landed(src, self.send))


def sum_rows(refs, r):
    value = refs[0][r, :].astype(FULL)
    for ref in refs[1:]:
        value += ref[r, :].astype(FULL)
    return value


def add_up(refs, dst):
    rows = dst.shape[0]
    step = next(v for v in (224, 144, 64, 48, 32, 16) if rows % v == 0)

    def one(t, carry):
        r = pl.ds(pl.multiple_of(t * step, step), step)
        dst[r, :] = sum_rows(refs, r).astype(LOW)
        return carry

    lax.fori_loop(0, rows // step, one, 0)


def add_over_slice(place, tile, tiles, send, recv):
    base = 0
    for turn, (peers, own) in enumerate((
        (place.tall, place.core * place.nz + place.z), (place.flat, place.y * place.n + place.x)
    )):
        mine = tiles.at[base + own]
        mine[...] = tile
        for peer in peers:
            push(mine, mine, send.at[turn], recv.at[turn], peer)
        landed(tiles.at[pl.ds(base, len(peers))], recv.at[turn])
        tile = tiles[base]
        for k in range(1, len(peers) + 1):
            tile += tiles[base + k]
        landed(tiles.at[pl.ds(base, len(peers))], send.at[turn])
        base += len(peers) + 1
    return tile


def step_kernel(
    place, loss_scale,
    pat, pos, seg, lab, tea, lm, gm,
    new_l, new_g, shared,
    b0, b1, bg, r0c, r0q, r0p, r0z, r1c, r1q, r1p, r1z, rgc, rgq, rgp, rgz, flat, edge, stage, arrange,
    wqkv, wproj, wfc1, wfc2, wpat, wpos, whead, vecs,
    pos_col, seg_col, unit_a, inv_a, h_a, unit_b, inv_b, h_b, qkv, probs, attl, x0, x1, slope, act, kv, low, inv_c,
    tiles, sends, gather_recv, scatter_recv, tile_send, tile_recv,
):
    layer_rows, global_rows = lm.shape[0] // 2, gm.shape[0]
    place.locate()
    me = place.block(0, 0, 0)
    bg[me + (pl.ds(0, global_rows),)] = gm[...].astype(LOW)
    b0[me + (pl.ds(0, layer_rows),)] = lm[pl.ds(0, layer_rows, stride=2), :].astype(LOW)
    b1[me + (pl.ds(0, layer_rows),)] = lm[pl.ds(1, layer_rows, stride=2), :].astype(LOW)
    place.meet()
    gathers = [Gather(place, buf, sends.at[i], gather_recv.at[i]) for i, buf in enumerate((bg, b0, b1))]
    gather_g, gather_0, gather_1 = gathers
    for gather in gathers:
        gather.start()
    queue = []

    def pump(count=1):
        for _ in range(min(count, len(queue))):
            queue.pop(0)()

    def split_rows(rows):
        half = rows // 32 * 16
        return [pl.ds(at, count) for at, count in ((0, half), (half, rows - half)) if count]

    def finish_layer(n):
        def out(refs):
            for r in split_rows(layer_rows):
                new_l[pl.ds(2 * r.start + n, r.size, stride=2), :] = sum_rows(refs, r)

        return out

    def finish_global(refs):
        for r in split_rows(global_rows):
            new_g[r, :] = sum_rows(refs, r)

    def late_layer(s):
        first, last = PRE_GAIN_AT // layer_rows, (PROJ_BIAS_AT - 1) // layer_rows
        return (s < -(-PROJ_AT // layer_rows)) | ((s >= first) & (s <= last))

    def late_global(s):
        return s < -(-FINAL_GAIN_AT // global_rows)

    scatters = [
        Scatter(place, bg, rgc, rgq, rgp, rgz, finish_global, sends.at[5], scatter_recv.at[2], late_global),
        Scatter(place, b0, r0c, r0q, r0p, r0z, finish_layer(0), sends.at[4], scatter_recv.at[1], late_layer),
        Scatter(place, b1, r1c, r1q, r1p, r1z, finish_layer(1), sends.at[3], scatter_recv.at[0]),
    ]
    scatter_g, scatter_0, scatter_1 = scatters

    head_of_lane = lax.broadcasted_iota(jnp.int32, (1, LANES), 1) // HEAD_DIM

    def loop(count, body, carry=None, after=()):
        for i in range(count):
            carry = body(i, carry)
            pump(after[i] if i < len(after) else 0)
        return carry

    def each_block(low_end, high_end, one):
        def body(s, carry):
            x = lax.rem(s, place.nx)
            rest = lax.div(s, place.nx)
            z, rest = lax.rem(rest, place.nz), lax.div(rest, place.nz)
            one(s, (lax.div(rest, 2), lax.rem(rest, 2), z, x))
            return carry

        lax.fori_loop(low_end, high_end, body, 0)

    def spread(buf, rows, low_end=0, high_end=2 * place.n * place.n * place.nz):
        def one(s, t):
            if rows % 8 == 0:
                flat[pl.ds(pl.multiple_of(s * rows, 8), rows), :] = buf[t + (pl.ds(0, rows),)].astype(FULL)
            else:
                stage[: buf.shape[4], :] = buf[t].astype(FULL)

                def row(i, carry):
                    flat[pl.ds(s * rows + i, 1), :] = stage[pl.ds(i, 1), :]
                    return carry

                lax.fori_loop(0, rows, row, 0)

        each_block(low_end, high_end, one)

    def gather_rows(buf, rows, low_end=0, high_end=2 * place.n * place.n * place.nz):
        def one(s, t):
            if rows % 8 == 0:
                buf[t + (pl.ds(0, rows),)] = flat[pl.ds(pl.multiple_of(s * rows, 8), rows), :].astype(LOW)
            else:

                def row(i, carry):
                    stage[pl.ds(i, 1), :] = flat[pl.ds(s * rows + i, 1), :]
                    return carry

                lax.fori_loop(0, rows, row, 0)
                buf[t] = stage[: buf.shape[4], :].astype(LOW)

        each_block(low_end, high_end, one)

    def take(dst, at, rows, width):
        count = width // LANES

        def one(c, carry):
            value = flat[pl.ds(at + c, rows, stride=count), :].astype(LOW)
            dst[:rows, pl.ds(pl.multiple_of(c * LANES, LANES), LANES)] = value
            return carry

        lax.fori_loop(0, count, one, 0)

    def take_row(at, width):
        return jnp.concatenate([flat[at + i : at + i + 1, :] for i in range(width // LANES)], axis=1)

    def put_row(at, value):
        for i in range(value.shape[1] // LANES):
            flat[at + i : at + i + 1, :] = value[:, i * LANES : (i + 1) * LANES]

    def put(at, start, width, value, first=0):
        count = width // LANES
        rows = value.shape[0]
        for i in range(value.shape[1] // LANES):
            flat[pl.ds(at + start * count + first + i, rows, stride=count), :] = value[:, i * LANES : (i + 1) * LANES]

    for i in range(SEQ // LANES):
        lanes = slice(i * LANES, (i + 1) * LANES)
        for src, dst in ((pos, pos_col), (seg, seg_col)):
            dst[lanes, :] = jnp.transpose(jnp.broadcast_to(src[0:1, lanes].astype(FULL), (LANES, LANES)))
    pos_row = pos[0:1, :]
    seg_row = seg[0:1, :]
    picked_row = lax.broadcasted_iota(jnp.int32, (PICKED, 1), 0)
    picked_image = jnp.where(picked_row < IMAGES, picked_row, picked_row - IMAGES)
    picked_image = jnp.where(picked_row < 2 * IMAGES, picked_image, -1)
    picked_place = jnp.where(picked_row < IMAGES, TABLE, TABLE + 1)
    picker = ((seg_row == picked_image) & (pos_row == picked_place)).astype(FULL)
    picker_low = picker.astype(LOW)

    arr_row = lax.broadcasted_iota(jnp.int32, (D, GROUP * LANES), 0)
    arr_lane = lax.broadcasted_iota(jnp.int32, (D, GROUP * LANES), 1)
    arrange[...] = (
        (arr_row == (arr_lane % LANES) * GROUP + arr_lane // LANES) & (arr_lane % LANES < GROUPS)
    ).astype(FULL).astype(LOW)

    queue.extend(gather_g.steps())
    pump(99)
    queue.extend(gather_0.steps())
    pump(4)
    gather_g.last()
    gather_g.finish()
    spread(bg, global_rows)
    pump(99)
    queue.extend(gather_1.steps())
    take(wpat, PATCH_AT, PATCH, D)
    take(wpos, POS_AT, TABLE + 2, D)
    wpos[TABLE + 2 :, :] = jnp.zeros((wpos.shape[0] - TABLE - 2, D), LOW)

    def take_head(j, carry):
        value = flat[pl.ds(HEAD_AT + j, GROUPS, stride=GROUP_ROWS), :].astype(LOW)
        whead[:, pl.ds(pl.multiple_of(j * LANES, LANES), LANES)] = value
        return carry

    lax.fori_loop(0, GROUP_ROWS, take_head, 0)
    whead[:, GROUP_ROWS * LANES :] = jnp.zeros((GROUPS, LANES), LOW)
    patch_bias = take_row(PATCH_BIAS_AT, D)
    final_gain = take_row(FINAL_GAIN_AT, D)
    final_bias = take_row(FINAL_BIAS_AT, D)
    head_bias = take_row(HEAD_BIAS_AT, HEAD_LANES)

    row_at = (
        (PRE_GAIN_AT, D), (PRE_BIAS_AT, D), (QUERY_BIAS_AT, D), (VALUE_BIAS_AT, D), (PROJ_BIAS_AT, D),
        (MID_GAIN_AT, D), (MID_BIAS_AT, D), (FC1_BIAS_AT, FF), (FC2_BIAS_AT, D),
    )

    def take_layer(n, buf):
        spread(buf, layer_rows)
        take(wqkv.at[n], QKV_AT, D, 3 * D)
        take(wproj.at[n], PROJ_AT, D, D)
        take(wfc1.at[n], FC1_AT, D, FF)
        take(wfc2.at[n], FC2_AT, FF, D)
        for i, (at, width) in enumerate(row_at):
            vecs[n, i : i + 1, :width] = take_row(at, width)

    def vec(n, i):
        return vecs[n, i : i + 1, : row_at[i][1]]

    pump(4)
    gather_0.last()
    pump(99)
    gather_0.finish()
    take_layer(0, b0)

    def tile_rows(i):
        return pl.ds(i * ROWS, ROWS)

    def onehot_of(place):
        iota = lax.broadcasted_iota(jnp.int32, (1, wpos.shape[0]), 1).astype(FULL)
        return (place == iota).astype(LOW)

    def embed(i, carry):
        r = tile_rows(i)
        place = pos_col[r, 0:1]
        pixel = dot(pat[r, :], wpat[...]) + patch_bias
        stream = dot(onehot_of(place), wpos[...]) + jnp.where(place < TABLE, pixel, 0.0)
        x0[r, :] = stream
        unit, inverse = normalise(stream)
        unit_a[r, :] = unit
        inv_a[r, :] = jnp.broadcast_to(inverse, (ROWS, LANES))
        h = (unit * vec(0, 0) + vec(0, 1)).astype(LOW)
        h_a[r, :] = h
        bias = jnp.concatenate([vec(0, 2), jnp.zeros((1, D), FULL), vec(0, 3)], axis=1)
        qkv[r, :] = (dot(h, wqkv[0]) + bias).astype(LOW)
        return carry

    loop(SEQ // ROWS, embed, None, (1, 1, 1))

    def window_rows(j):
        return pl.ds(min(102 * j // 16 * 16, SEQ - WINDOW), WINDOW)

    def both(x):
        zero = jnp.zeros_like(x)
        return jnp.concatenate([jnp.where(head_of_lane == 0, x, zero), jnp.where(head_of_lane == 1, x, zero)], axis=0)

    def merge(x):
        return jnp.where(head_of_lane == 0, x[:WINDOW], x[WINDOW:])

    attl[...] = jnp.zeros_like(attl)

    def window_masks(j, r):
        own = seg_col[r, :]
        first = 2.0 * j
        mine = (own >= first) & (own < first + 2.0)
        other = jnp.transpose(jnp.where(mine, own, -1.0))
        pair = jnp.concatenate([own, own], axis=1) == jnp.concatenate([other, other], axis=1)
        return mine, pair

    def keep_own(mine, ref, r, lanes, value):
        ref[r, lanes] = jnp.where(mine, value, ref[r, lanes].astype(FULL)).astype(LOW)

    def attend(j, carry):
        r = window_rows(j)
        mine, pair = window_masks(j, r)
        for g in range(HEADS // 2):
            lanes = slice(g * LANES, (g + 1) * LANES)
            q2 = both(qkv[r, lanes])
            keys = qkv[r, D + g * LANES : D + (g + 1) * LANES]
            values = qkv[r, 2 * D + g * LANES : 2 * D + (g + 1) * LANES]
            scores = jnp.where(pair, dot_nt(keys, q2) * SCORE_SCALE, MASK_FILL)
            e = jnp.exp(scores - jnp.max(scores, axis=0, keepdims=True))
            p = jnp.where(pair, e * (1.0 / jnp.sum(e, axis=0, keepdims=True)), 0.0).astype(LOW)
            probs[j, g] = p
            keep_own(mine, attl, r, lanes, merge(dot_tn(p, values)))
        return carry

    loop(WINDOWS, attend, None, (1,) * WINDOWS)

    def feed(i, carry):
        r = tile_rows(i)
        middle = x0[r, :] + dot(attl[r, :], wproj[0]) + vec(0, 4)
        unit, inverse = normalise(middle)
        unit_b[r, :] = unit
        inv_b[r, :] = jnp.broadcast_to(inverse, (ROWS, LANES))
        h = (unit * vec(0, 5) + vec(0, 6)).astype(LOW)
        h_b[r, :] = h
        for c in range(4):
            lanes = slice(c * D, (c + 1) * D)
            value, steep = gelu_parts(dot(h, wfc1[0, :, lanes]) + vecs[0, 7:8, lanes])
            act[r, lanes] = value.astype(LOW)
            slope[r, lanes] = steep.astype(LOW)
        x1[r, :] = middle + dot(act[r, :], wfc2[0]) + vec(0, 8)
        return carry

    loop(SEQ // ROWS, feed, None, (1, 1, 1))

    pump(99)
    gather_1.last()
    gather_1.finish()
    take_layer(1, b1)
    unit_c = x0
    h_c = low

    def kv_rows(i, carry):
        r = tile_rows(i)
        unit, inverse = normalise(x1[r, :])
        unit_c[r, :] = unit
        inv_c[r, :] = jnp.broadcast_to(inverse, (ROWS, LANES))
        h = (unit * vec(1, 0) + vec(1, 1)).astype(LOW)
        h_c[r, :] = h
        bias = jnp.concatenate([jnp.zeros((1, D), FULL), vec(1, 3)], axis=1)
        kv[r, :] = (dot(h, wqkv[1, :, D:]) + bias).astype(LOW)
        return carry

    loop(SEQ // ROWS, kv_rows)

    h_s = dot(picker_low, h_c[...]).astype(LOW)
    x_s = sum(dot(picker_low, part) for part in exact_parts(x1[...]))
    q_s = (dot(h_s, wqkv[1, :, :D]) + vec(1, 2)).astype(LOW)
    stack_rows = lax.broadcasted_iota(jnp.int32, (HEADS * PICKED, 1), 0)
    stack_lanes = lax.broadcasted_iota(jnp.int32, (1, D), 1)
    own_head = (stack_rows // PICKED) == (stack_lanes // HEAD_DIM)

    def stack(x):
        tall = jnp.concatenate([x.astype(FULL)] * HEADS, axis=0)
        return jnp.where(own_head, tall, 0.0).astype(LOW)

    def unstack(x):
        x = jnp.where(own_head, x, 0.0)
        total = x[:PICKED]
        for h in range(1, HEADS):
            total += x[h * PICKED : (h + 1) * PICKED]
        return total

    q6 = stack(q_s)
    image6 = jnp.concatenate([picked_image] * HEADS, axis=0)
    mask6 = image6 == seg_row
    scores = jnp.where(mask6, dot_nt(q6, kv[:, :D]) * SCORE_SCALE, MASK_FILL)
    e = jnp.exp(scores - jnp.max(scores, axis=-1, keepdims=True))
    p6 = e / jnp.sum(e, axis=-1, keepdims=True)
    p6_low = p6.astype(LOW)
    att_s = unstack(dot(p6_low, kv[:, D:])).astype(LOW)
    mid_s = x_s + dot(att_s, wproj[1]) + vec(1, 4)
    unit_m, inv_m = normalise(mid_s)
    h2_s = (unit_m * vec(1, 5) + vec(1, 6)).astype(LOW)
    act_s, steep_s = gelu_parts(dot(h2_s, wfc1[1]) + vec(1, 7))
    act_s = act_s.astype(LOW)
    x2_s = mid_s + dot(act_s, wfc2[1]) + vec(1, 8)

    unit_f, inv_f = normalise(x2_s)
    summary = (unit_f * final_gain + final_bias).astype(LOW)
    arranged = dot(summary, arrange[...]).astype(LOW)
    logits = head_bias
    spans = []
    for k in range(GROUP):
        at = 2 * CLASSES * k
        block, shift = at // LANES, at % LANES
        blocks = (at + 2 * CLASSES - 1) // LANES - block + 1
        spans.append((block, shift, blocks))
        s_k = arranged[:, k * LANES : k * LANES + GROUPS]
        wide = (HEAD_LANES // LANES + 1) * LANES
        part = dot(s_k, whead[:, block * LANES : block * LANES + wide])
        if shift:
            part = pltpu.roll(part, wide - shift, 1)
        logits = logits + part[:, :HEAD_LANES]
    column = lax.broadcasted_iota(jnp.int32, (PICKED, HEAD_LANES), 1)
    second = picked_row >= IMAGES
    low_end = jnp.where(second, CLASSES, 0)
    valid = (column >= low_end) & (column < low_end + CLASSES)
    live = picked_row < 2 * IMAGES
    target = jnp.zeros((PICKED, 1), jnp.int32)
    for i in range(IMAGES):
        target = jnp.where(picked_row == i, lab[0, i], target)
        target = jnp.where(picked_row == IMAGES + i, CLASSES + tea[0, i], target)
    hit = column == target
    logits = jnp.where(valid, logits, -3e38)
    top = jnp.max(logits, axis=-1, keepdims=True)
    e = jnp.exp(logits - top)
    total = jnp.sum(e, axis=-1, keepdims=True)
    hit_logit = jnp.sum(jnp.where(hit, logits, 0.0), axis=-1, keepdims=True)
    each = jnp.where(live, top + jnp.log(total) - hit_logit, 0.0)
    loss_sum = jnp.sum(each, axis=0, keepdims=True)
    grad_logits = jnp.where(live, (e / total - hit.astype(FULL)) * loss_scale, 0.0)
    grad_low = grad_logits.astype(LOW)
    grad_wide = jnp.concatenate([grad_low.astype(FULL), jnp.zeros((PICKED, LANES), FULL)], axis=1)

    grad_arranged = []
    for k, (block, shift, blocks) in enumerate(spans):
        turned = (pltpu.roll(grad_wide, shift, 1) if shift else grad_wide).astype(LOW)
        turned = turned[:, : blocks * LANES]
        s_k = arranged[:, k * LANES : k * LANES + GROUPS]
        grad_w = dot_tn(s_k, turned)
        for j in range(blocks):
            rows = pl.ds(HEAD_AT + block + j, GROUPS, stride=GROUP_ROWS)
            piece = grad_w[:, j * LANES : (j + 1) * LANES]
            if k and j == 0:
                piece = piece + flat[rows, :]
            flat[rows, :] = piece
        back = dot_nt(turned, whead[:, block * LANES : (block + blocks) * LANES])
        grad_arranged.append(jnp.concatenate([back, jnp.zeros((PICKED, LANES - GROUPS), FULL)], axis=1))
    parts = jnp.concatenate(exact_parts(jnp.concatenate(grad_arranged, axis=1)), axis=0)
    parts = dot_nt(parts, arrange[...])
    grad_summary = parts[:PICKED] + parts[PICKED : 2 * PICKED] + parts[2 * PICKED :]
    put_row(HEAD_BIAS_AT, col_sum(grad_low))
    put_row(FINAL_GAIN_AT, col_sum(grad_summary * unit_f))
    put_row(FINAL_BIAS_AT, col_sum(grad_summary))
    flat[GLOBAL_END:GLOBAL_ALL, :] = jnp.zeros((GLOBAL_ALL - GLOBAL_END, LANES), FULL)
    for gather in gathers:
        gather.drain()
    border = FINAL_GAIN_AT // global_rows
    gather_rows(bg, global_rows, border + 1)
    kept = (border + 1) * global_rows - FINAL_GAIN_AT
    edge[:kept, :] = flat[FINAL_GAIN_AT : FINAL_GAIN_AT + kept, :]
    scatter_g.start()
    g_q, g_p, g_z = scatter_g.queues()
    dx_s = norm_back(grad_summary, final_gain, unit_f, inv_f)

    out_s = dx_s.astype(LOW)
    for c in range(4):
        put(FC2_AT, c * D, D, dot_tn(act_s[:, c * D : (c + 1) * D], out_s))
    put_row(FC2_BIAS_AT, col_sum(out_s))
    gpre_s = (dot_nt(out_s, wfc2[1]) * steep_s).astype(LOW)
    put(FC1_AT, 0, FF, dot_tn(h2_s, gpre_s))
    put_row(FC1_BIAS_AT, col_sum(gpre_s))
    gh2_s = dot_nt(gpre_s, wfc1[1])
    put_row(MID_GAIN_AT, col_sum(gh2_s * unit_m))
    put_row(MID_BIAS_AT, col_sum(gh2_s))
    gmid_s = dx_s + norm_back(gh2_s, vec(1, 5), unit_m, inv_m)
    gmid_low = gmid_s.astype(LOW)
    put(PROJ_AT, 0, D, dot_tn(att_s, gmid_low))
    put_row(PROJ_BIAS_AT, col_sum(gmid_low))
    gatt6 = stack(dot_nt(gmid_low, wproj[1]).astype(LOW))
    gprob = dot_nt(gatt6, kv[:, D:])
    gscore = (p6 * (gprob - jnp.sum(p6 * gprob, axis=-1, keepdims=True))).astype(LOW)
    gq_s = (unstack(dot(gscore, kv[:, :D])) * SCORE_SCALE).astype(LOW)
    gkeys = (dot_tn(gscore, q6) * SCORE_SCALE).astype(LOW)
    gvalues = dot_tn(p6_low, gatt6).astype(LOW)
    put_row(QUERY_BIAS_AT, col_sum(gq_s))
    put_row(VALUE_BIAS_AT, col_sum(gvalues))
    kv[:, :D] = gkeys
    kv[:, D:] = gvalues
    queue.extend(g_q)
    pump(99)
    put(QKV_AT, 0, 3 * D, dot_tn(h_s, gq_s))
    put(QKV_AT, 0, 3 * D, dot_tn(h_c[...], kv[:, :D]), 3)
    put(QKV_AT, 0, 3 * D, dot_tn(h_c[...], kv[:, D:]), 6)
    back_s = jnp.concatenate([dot_nt(gq_s, wqkv[1, :, :D]), gmid_s], axis=1)

    back_parts = jnp.concatenate(exact_parts(back_s), axis=0)
    dx = x1

    def kv_back(i, carry):
        gain_sum, bias_sum = carry
        r = tile_rows(i)
        image_col = seg_col[r, 0:1]
        place_col = pos_col[r, 0:1]
        lane = lax.broadcasted_iota(jnp.int32, (1, PICKED), 1).astype(FULL)
        lane_image = jnp.where(lane < IMAGES, lane, lane - IMAGES)
        lane_place = jnp.where(lane < IMAGES, float(TABLE), TABLE + 1.0)
        back_pick = (
            (image_col == lane_image) & (place_col == lane_place) & (lane < 2.0 * IMAGES)
        ).astype(LOW)
        back = dot(jnp.concatenate([back_pick] * 3, axis=1), back_parts)
        grad = back[:, :D] + dot_nt(kv[r, :], wqkv[1, :, D:])
        unit = unit_c[r, :]
        dx[r, :] = back[:, D:] + norm_back(grad, vec(1, 0), unit, inv_c[r, 0:1])
        return gain_sum + col_sum(grad * unit), bias_sum + col_sum(grad)

    zero_row = jnp.zeros((1, D), FULL)
    gain_sum, bias_sum = loop(SEQ // ROWS, kv_back, (zero_row, zero_row))
    put_row(PRE_GAIN_AT, gain_sum)
    put_row(PRE_BIAS_AT, bias_sum)
    flat[LAYER_END:, :] = jnp.zeros((LAYER_ALL - LAYER_END, LANES), FULL)
    gather_rows(b1, layer_rows)
    scatter_1.start()
    one_q, one_p, one_z = scatter_1.queues()

    def feed_back(i, carry):
        fc1_sum, fc2_sum, proj_sum, gain_sum, bias_sum = carry
        r = tile_rows(i)
        grad_out = dx[r, :]
        out_low = grad_out.astype(LOW)
        low[r, :] = out_low
        for c in range(4):
            lanes = slice(c * D, (c + 1) * D)
            slope[r, lanes] = (dot_nt(out_low, wfc2[0, lanes, :]) * slope[r, lanes].astype(FULL)).astype(LOW)
        grad_h = dot_nt(slope[r, :], wfc1[0])
        unit = unit_b[r, :]
        middle = grad_out + norm_back(grad_h, vec(0, 5), unit, inv_b[r, 0:1])
        dx[r, :] = middle
        middle_low = middle.astype(LOW)
        h2low[r, :] = middle_low
        gatt[r, :] = dot_nt(middle_low, wproj[0]).astype(LOW)
        return (
            fc1_sum + col_sum(slope[r, :]), fc2_sum + col_sum(out_low), proj_sum + col_sum(middle_low),
            gain_sum + col_sum(grad_h * unit), bias_sum + col_sum(grad_h),
        )

    h2low = kv.at[:, 0:D]
    gatt = kv.at[:, D : 2 * D]
    sums = loop(SEQ // ROWS, feed_back, (jnp.zeros((1, FF), FULL),) + (zero_row,) * 4)
    queue.extend(g_p + one_q)
    pump(99)
    for at, value in zip((FC1_BIAS_AT, FC2_BIAS_AT, PROJ_BIAS_AT, MID_GAIN_AT, MID_BIAS_AT), sums):
        put_row(at, value)

    for c in range(4):
        lanes = slice(c * D, (c + 1) * D)
        put(FC2_AT, c * D, D, dot_tn(act[:, lanes], low[...]))
        put(FC1_AT, 0, FF, dot_tn(h_b[...], slope[:, lanes]), 3 * c)
    put(PROJ_AT, 0, D, dot_tn(attl[...], h2low[...]))
    flat[LAYER_END:, :] = jnp.zeros((LAYER_ALL - LAYER_END, LANES), FULL)
    first_early = -(-PROJ_AT // layer_rows)
    gather_rows(b0, layer_rows, first_early)
    scatter_0.start()
    zero_q, zero_p, zero_z = scatter_0.queues()
    queue.extend(g_z + one_p[:2] + zero_q + one_p[2:])

    def attend_back(j, carry):
        r = window_rows(j)
        mine, _ = window_masks(j, r)
        for g in range(HEADS // 2):
            lanes = slice(g * LANES, (g + 1) * LANES)
            key_lanes = slice(D + g * LANES, D + (g + 1) * LANES)
            value_lanes = slice(2 * D + g * LANES, 2 * D + (g + 1) * LANES)
            q2 = both(qkv[r, lanes])
            go2 = both(gatt[r, lanes])
            keys = qkv[r, key_lanes]
            p_low = probs[j, g]
            p = p_low.astype(FULL)
            gp = dot_nt(qkv[r, value_lanes], go2)
            gs = (p * (gp - jnp.sum(p * gp, axis=0, keepdims=True))).astype(LOW)
            keep_own(mine, qkv, r, lanes, merge(dot_tn(gs, keys)) * SCORE_SCALE)
            keep_own(mine, qkv, r, key_lanes, dot(gs, q2) * SCORE_SCALE)
            keep_own(mine, qkv, r, value_lanes, dot(p_low, go2))
        return carry

    loop(WINDOWS, attend_back, None, (0, 0, 0, 4, 0, 1, 0, 1))

    def qkv_back(i, carry):
        query_sum, value_sum, gain_sum, bias_sum, embed_sum = carry
        r = tile_rows(i)
        held = seg_col[r, 0:1] < float(IMAGES)
        grads = jnp.where(held, qkv[r, :].astype(FULL), 0.0)
        gq, gv = grads[:, :D], grads[:, 2 * D :]
        qkv[r, :] = grads.astype(LOW)
        grad = dot_nt(qkv[r, :], wqkv[0])
        unit = unit_a[r, :]
        full = dx[r, :] + norm_back(grad, vec(0, 0), unit, inv_a[r, 0:1])
        dx[r, :] = full
        place = pos_col[r, 0:1]
        pixel = jnp.where(place < TABLE, full, 0.0).astype(LOW)
        low[r, :] = pixel
        return (
            query_sum + col_sum(gq), value_sum + col_sum(gv), gain_sum + col_sum(grad * unit),
            bias_sum + col_sum(grad), embed_sum + col_sum(pixel),
        )

    sums = loop(SEQ // ROWS, qkv_back, (zero_row,) * 5, (4, 4, 1))
    for at, value in zip((QUERY_BIAS_AT, VALUE_BIAS_AT, PRE_GAIN_AT, PRE_BIAS_AT), sums):
        put_row(at, value)
    for c in range(3):
        put(QKV_AT, 0, 3 * D, dot_tn(h_a[...], qkv[:, c * D : (c + 1) * D]), 3 * c)
    gather_rows(b0, layer_rows, 0, first_early)
    gather_rows(b0, layer_rows, PRE_GAIN_AT // layer_rows, (PROJ_BIAS_AT - 1) // layer_rows + 1)
    scatter_0.start(1)
    pump(99)
    queue.extend(one_z[:2])

    for c in range(2):
        put(PATCH_AT, c * D, D, dot_tn(pat[:, c * D : (c + 1) * D], low[...]))
        pump(1)
    place_col = pos_col[:, 0:1]
    onehot = onehot_of(place_col)
    high = dx[...].astype(LOW)
    rest = (dx[...] - high.astype(FULL)).astype(LOW)
    table = dot_tn(onehot, high) + dot_tn(onehot, rest)
    put(POS_AT, 0, D, table[: TABLE + 2])
    put_row(PATCH_BIAS_AT, sums[4])
    flat[FINAL_GAIN_AT : FINAL_GAIN_AT + kept, :] = edge[:kept, :]
    gather_rows(bg, global_rows, 0, border + 1)
    scatter_g.start(1)
    late_0, late_g = scatter_0.queues(1), scatter_g.queues(1)
    queue.extend(one_z[2:3] + zero_p + late_0[0] + one_z[3:] + late_g[0] + zero_z[:3] + late_0[1] + late_g[1])
    queue.extend(zero_z[3:] + late_0[2] + late_g[2])
    pump(99)

    squares = jnp.zeros((1, 1), FULL)
    for ref in (new_l, new_g):
        used = ref[...]
        squares += jnp.sum(jnp.sum(used * used, axis=0, keepdims=True), axis=1, keepdims=True)
    row = lax.broadcasted_iota(jnp.int32, (8, LANES), 0)
    tile = jnp.where(row == 0, squares, loss_sum)
    shared[...] = add_over_slice(place, tile, tiles, tile_send, tile_recv)
    for scatter in scatters:
        scatter.drain()


def padded(rows):
    return rows + -rows % 16


def step_call(place, loss_scale, pat, pos, seg, lab, tea, lm, gm):
    vmem = pl.BlockSpec(memory_space=pltpu.VMEM)
    smem = pl.BlockSpec(memory_space=pltpu.SMEM)
    n, nz = place.n, place.nz
    rows = padded(lm.shape[0] // 2), padded(lm.shape[0] // 2), padded(gm.shape[0])

    def shape(*dims, kind=FULL):
        return pltpu.VMEM(dims, kind)

    def low(*dims):
        return pltpu.VMEM(dims, LOW)

    scratch = [low(n, 2, nz, n, r, LANES) for r in rows]
    for r in rows:
        scratch += [
            low(n, nz, n, r, LANES), low(n - 1, n, nz, r, LANES), low(n - 1, nz, r, LANES), low(nz - 1, r, LANES)
        ]
    tiles = 2 * nz + n * n
    scratch += [
        shape(LAYER_ALL, LANES), shape(gm.shape[0] + 8, LANES), shape(rows[0], LANES), low(D, GROUP * LANES),
        low(2, D, 3 * D), low(2, D, D), low(2, D, FF), low(2, FF, D),
        low(PATCH, D), low(256, D), low(GROUPS, (GROUP_ROWS + 1) * LANES),
        shape(2, 16, FF),
        shape(SEQ, LANES), shape(SEQ, LANES),
        shape(SEQ, D), shape(SEQ, LANES), low(SEQ, D),
        shape(SEQ, D), shape(SEQ, LANES), low(SEQ, D),
        low(SEQ, 3 * D), low(WINDOWS, HEADS // 2, WINDOW, 2 * WINDOW),
        low(SEQ, D), shape(SEQ, D), shape(SEQ, D),
        low(SEQ, FF), low(SEQ, FF), low(SEQ, 2 * D), low(SEQ, D), shape(SEQ, LANES),
        shape(tiles, 8, LANES),
        pltpu.SemaphoreType.DMA((6,)),
        pltpu.SemaphoreType.DMA((3, nz + nz * n + 2 * n)), pltpu.SemaphoreType.DMA((3, 2 * n * n * nz + n * nz + nz)),
        pltpu.SemaphoreType.DMA((2,)), pltpu.SemaphoreType.DMA((2,)),
    ]
    return pl.pallas_call(
        functools.partial(step_kernel, place, loss_scale),
        out_shape=[jax.ShapeDtypeStruct(a, FULL) for a in (lm.shape, gm.shape, (8, LANES))],
        in_specs=[vmem] * 3 + [smem] * 2 + [vmem] * 2,
        out_specs=[vmem] * 3,
        scratch_shapes=scratch,
        compiler_params=pltpu.CompilerParams(collective_id=0, has_side_effects=True, vmem_limit_bytes=VMEM_BYTES),
    )(pat, pos, seg, lab, tea, lm, gm)

def adam_kernel(total, gl, gg, lm, lo, ls, gm, go, gs, *outs):
    norm = jnp.sqrt(total[0:1, 0:1])
    factor = jnp.minimum(1.0, CLIP_NORM / norm)
    fix_one = 1.0 - BETA_ONE**STEP
    fix_two = 1.0 - BETA_TWO**STEP
    for at, (grad, master, moment, second) in ((0, (gl, lm, lo, ls)), (3, (gg, gm, go, gs))):
        clipped = grad[...] * factor
        new_moment = BETA_ONE * moment[...] + (1.0 - BETA_ONE) * clipped
        new_second = BETA_TWO * second[...] + (1.0 - BETA_TWO) * clipped * clipped
        old = master[...]
        update = new_moment / fix_one / (jnp.sqrt(new_second / fix_two) + ADAM_EPS) + WEIGHT_DECAY * old
        outs[at][...] = old - LEARN_RATE * update
        outs[at + 1][...] = new_moment
        outs[at + 2][...] = new_second
    outs[6][...] = norm


def interleave(x):
    rows = x.shape[1] // LANES
    return x.reshape(2, rows, LANES).transpose(1, 0, 2).reshape(2 * rows, LANES)


def layers_apart(x):
    rows = x.shape[0] // 2
    return x.reshape(rows, 2, LANES).transpose(1, 0, 2).reshape(2, rows * LANES)


def shards(sizes, pat, pos, seg, lab, tea, lm, lo, ls, gm, go, gs):
    place = Place(sizes)
    count = sizes[0] * sizes[1]
    assert pat.shape[0] == 1 and lm.shape[1] * count == LAYER_ALL * LANES and gm.shape[0] * count == GLOBAL_ALL * LANES
    lm, lo, ls = interleave(lm), interleave(lo), interleave(ls)
    gm, go, gs = gm.reshape(-1, LANES), go.reshape(-1, LANES), gs.reshape(-1, LANES)
    gl, gg, total = step_call(place, 1.0 / (2 * IMAGES * count), pat[0], pos, seg, lab, tea, lm, gm)
    *new, norm = pl.pallas_call(
        adam_kernel,
        out_shape=[jax.ShapeDtypeStruct(x.shape, FULL) for x in (lm, lm, lm, gm, gm, gm, total[:1, :1])],
        compiler_params=pltpu.CompilerParams(vmem_limit_bytes=VMEM_BYTES),
    )(total, gl, gg, lm, lo, ls, gm, go, gs)
    return tuple(layers_apart(x) for x in new[:3]) + tuple(x.reshape(-1) for x in new[3:]) + (norm[0, 0], total[1, 0])


def solution(mesh):
    axes = tuple(mesh.axis_names)
    split = P(axes)
    wide = P(None, axes)
    return jax.shard_map(
        functools.partial(shards, tuple(mesh.shape[a] for a in axes)),
        mesh=mesh,
        in_specs=(split,) * 5 + (wide,) * 3 + (split,) * 3,
        out_specs=(wide,) * 3 + (split,) * 3 + (P(), P()),
        check_vma=False,
    )
```

```python
import functools

import jax
import jax.numpy as jnp
from jax import lax
from jax.experimental import pallas as pl
from jax.experimental.pallas import tpu as pltpu
from jax.sharding import PartitionSpec as P

D = 384
HEADS = 6
HEAD_DIM = 64
FF = 1536
CLASSES = 1000
PATCH = 768
TABLE = 196
IMAGES = 15
SEQ = 768
STEP = 10
LANES = 128

NORM_EPS = 1e-06
BETA_ONE = 0.9
BETA_TWO = 0.999
ADAM_EPS = 1e-08
LEARN_RATE = 0.1
WEIGHT_DECAY = 0.05
CLIP_NORM = 0.01
MASK_FILL = -1000000000.0
SCORE_SCALE = HEAD_DIM ** (-0.5)
LOW = jnp.bfloat16
FULL = jnp.float32
HIGHEST = lax.Precision.HIGHEST

QKV_AT, PROJ_AT, FC1_AT, FC2_AT = 0, 3456, 4608, 9216
PRE_GAIN_AT, PRE_BIAS_AT, QUERY_BIAS_AT, VALUE_BIAS_AT = 13824, 13827, 13830, 13833
PROJ_BIAS_AT, MID_GAIN_AT, MID_BIAS_AT, FC1_BIAS_AT, FC2_BIAS_AT = 13836, 13839, 13842, 13845, 13857
LAYER_END = 13860
PATCH_AT, POS_AT, PATCH_BIAS_AT, FINAL_GAIN_AT, FINAL_BIAS_AT = 0, 2304, 2898, 2901, 2904
HEAD_AT, HEAD_BIAS_AT, GLOBAL_END = 2907, 8907, 8923
GROUP, GROUP_ROWS, GROUPS = 8, 125, 48
HEAD_LANES = 2048
PICKED = 32
WINDOWS, WINDOW = 8, 128
ROWS = 256
LAYER_ALL, GLOBAL_ALL = 14080, 8960
VMEM_BYTES = 64 * 1024 * 1024 - 64 * 1024
MESH = pl.DeviceIdType.MESH


def dot(a, b, dims=(1, 0), precision=None):
    return lax.dot_general(
        a, b, (((dims[0],), (dims[1],)), ((), ())), precision=precision, preferred_element_type=FULL
    )


def dot_nt(a, b, precision=None):
    return dot(a, b, (1, 1), precision)


def dot_tn(a, b, precision=None):
    return dot(a, b, (0, 0), precision)


def row_mean(x):
    return jnp.sum(x, axis=-1, keepdims=True) * (1.0 / D)


def normalise(x):
    center = x - row_mean(x)
    inverse = lax.rsqrt(row_mean(center * center) + NORM_EPS)
    return center * inverse, inverse


def norm_back(grad, gain, unit, inverse):
    scaled = grad * gain
    return inverse * (scaled - row_mean(scaled) - unit * row_mean(scaled * unit))


def col_sum(x):
    return jnp.sum(x.astype(FULL), axis=0, keepdims=True)


def gelu_parts(x):
    size = jnp.abs(x)
    bell = jnp.exp(-0.5 * x * x)
    base = 1.0 + (0.3275911 * 0.7071067811865476) * size
    t = pl.reciprocal(base, approx=True)
    t = t * (2.0 - base * t)
    tail = ((((1.061405429 * t - 1.453152027) * t + 1.421413741) * t - 0.284496736) * t + 0.254829592) * t
    tail = 0.5 * tail * bell
    phi = jnp.where(x < 0, tail, 1.0 - tail)
    return x * phi, phi + x * (bell * 0.3989422804014327)


def exact_parts(x):
    high = x.astype(LOW)
    rest = x - high.astype(FULL)
    middle = rest.astype(LOW)
    return high, middle, (rest - middle.astype(FULL)).astype(LOW)


def wrap(value, size):
    return jnp.where(value >= size, value - size, value)


class Place:
    def __init__(self, sizes):
        dp, fsdp = sizes
        self.n = self.ny = self.nx = dp // 2
        self.nz = fsdp // self.nx
        assert dp == 2 * self.n and fsdp == self.n * self.nz

    def locate(self):
        dp, fsdp = lax.axis_index("dp"), lax.axis_index("fsdp")
        self.y, self.core = dp // 2, dp % 2
        self.z, self.x = fsdp // self.nx, fsdp % self.nx
        self.even = self.core == 0
        self.zs = [wrap(self.z + k, self.nz) for k in range(self.nz)]
        self.ys = [wrap(self.y + k, self.n) for k in range(self.n)]
        self.xs = [wrap(self.x + k, self.n) for k in range(self.n)]
        spans = [(p, q) for p in range(self.n) for q in range(self.n)]
        self.short = {
            (p, q): (jnp.where(self.even, self.ys[p], self.ys[q]), jnp.where(self.even, self.xs[q], self.xs[p]))
            for p, q in spans
        }

    def yx(self, p, q):
        return self.short[p, q]

    def block(self, dz, p, q):
        y, x = self.yx(p, q)
        return y, self.core, self.zs[dz], x

    def device(self, y, core, z, x):
        return y * 2 + core, z * self.nx + x

    def yx_other(self, p, q):
        return jnp.where(self.even, self.ys[q], self.ys[p]), jnp.where(self.even, self.xs[p], self.xs[q])

    def index(self, y, core, z, x):
        return ((y * 2 + core) * self.nz + z) * self.nx + x

    def meet(self):
        def there(y=0, core=0, z=0, x=0):
            return self.device(self.ys[y], 1 - self.core if core else self.core, self.zs[z], self.xs[x])

        self.other = there(core=1)
        self.zp = [there(z=k) for k in range(self.nz)]
        self.pp = [self.device(*self.block(0, k, 0)) for k in range(self.n)]
        self.qp = [self.device(*self.block(0, 0, k)) for k in range(self.n)]
        self.tall = [there(core=c, z=k) for c in range(2) for k in range(self.nz)][1:]
        self.flat = [there(y=j, x=k) for j in range(self.n) for k in range(self.n)][1:]
        barrier = pltpu.get_barrier_semaphore()
        for peer in self.tall + self.flat:
            pl.semaphore_signal(barrier, inc=1, device_id=peer, device_id_type=MESH)
        pl.semaphore_wait(barrier, len(self.tall + self.flat))


def push(src, dst, send, recv, peer):
    pltpu.make_async_remote_copy(
        src_ref=src, dst_ref=dst, send_sem=send, recv_sem=recv, device_id=peer, device_id_type=MESH
    ).start()


def landed(dst, recv):
    pltpu.make_async_copy(dst, dst, recv).wait()


class Plan:
    HOP = 2.5
    RATES = (88e3, 66e3, 600e3)

    def __init__(self):
        self.now, self.free, self.came, self.steps = 0.0, [0.0] * 3, {}, []

    def sent(self, key, way, size):
        begin = max(self.now, self.free[way])
        self.free[way] = begin + size / self.RATES[way]
        self.came[key] = max(self.came.get(key, 0.0), self.free[way] + self.HOP)

    def add(self, needs, run, name=None):
        self.steps.append((needs, run, name))

    def ready(self, step):
        return max((self.came.get(key, 1e9) for key in step[0]), default=0.0)

    def run(self, step):
        self.steps.remove(step)
        self.now = max(self.now, self.ready(step)) + 0.03
        step[1]()

    def spend(self, time):
        self.now += time
        while True:
            step = next((step for step in self.steps if self.ready(step) <= self.now), None)
            if step is None:
                return
            self.run(step)

    def until(self, name=None):
        while self.steps and (name is None or any(step[2] == name for step in self.steps)):
            self.run(min(self.steps, key=self.ready))


class Gather:
    def __init__(self, place, plan, name, buf, send, recv):
        self.place, self.plan, self.name, self.buf, self.send, self.recv = place, plan, name, buf, send, recv
        self.from_p = place.nz
        self.from_q = self.from_p + place.nz * place.n
        self.from_core = self.from_q + place.n
        self.size = 2 * buf.shape[4] * LANES

    def sent(self, way, count, *key):
        self.plan.sent((self.name,) + key, way, count * self.size)

    def to_p(self, dz):
        a, t = self.place, self.buf.at[self.place.block(dz, 0, 0)]
        for k in range(1, a.n):
            push(t, t, self.send, self.recv.at[self.from_p + dz * a.n + a.n - k], a.pp[k])
            self.sent(0, 1, 1, dz, a.n - k)

    def to_q(self, dz, p):
        a, t = self.place, self.buf.at[self.place.block(dz, p, 0)]
        for k in range(1, a.n):
            push(t, t, self.send, self.recv.at[self.from_q + a.n - k], a.qp[k])
            self.sent(0, 1, 2, dz, p)

    def start(self):
        a, t = self.place, self.buf.at[self.place.block(0, 0, 0)]
        self.to_p(0)
        for k in range(1, a.nz):
            push(t, t, self.send, self.recv.at[a.nz - k], a.zp[k])
            self.sent(1, 1, 0, a.nz - k)
        self.to_q(0, 0)
        far = range(1, a.n)
        near = sorted(range(1, a.nz), key=lambda k: min(k, a.nz - k))
        add = self.plan.add
        for p in far:
            add([(self.name, 1, 0, p)], lambda p=p: self.p_came(0, p))
        for k in near:
            add([(self.name, 0, k)], lambda k=k: self.z_came(k))
        for k in near:
            for p in far:
                add([(self.name, 1, k, p)], lambda k=k, p=p: self.p_came(k, p))
        mine = [(self.name, 0, k) for k in near] + [(self.name, 1, k, p) for k in range(a.nz) for p in far]
        add(mine, lambda: self.to_core(0))
        for q in far:
            add([(self.name, 2, k, p) for k in range(a.nz) for p in range(a.n)], lambda q=q: self.q_came(q))
        add([(self.name, 3, q) for q in range(a.n)], self.finish, self.name)

    def z_came(self, dz):
        landed(self.buf.at[self.place.block(dz, 0, 0)], self.recv.at[dz])
        self.to_p(dz)
        self.to_q(dz, 0)

    def p_came(self, dz, p):
        landed(self.buf.at[self.place.block(dz, p, 0)], self.recv.at[self.from_p + dz * self.place.n + p])
        self.to_q(dz, p)

    def group(self, core, q):
        a = self.place
        return self.buf.at[:, 0, :, a.xs[q]] if core == 0 else self.buf.at[a.ys[q], 1]

    def to_core(self, q):
        a = self.place
        for core in range(2):

            @pl.when(a.core == core)
            def _():
                t = self.group(core, q)
                push(t, t, self.send, self.recv.at[self.from_core + q], a.other)

        self.sent(2, a.n * a.nz, 3, q)

    def q_came(self, q):
        landed(self.buf.at[:, 0, :, 0], self.recv.at[self.from_q + q])
        self.to_core(q)

    def finish(self):
        for q in range(self.place.n):
            landed(self.buf.at[:, 0, :, 0], self.recv.at[self.from_core + q])

    def drain(self):
        a = self.place
        for t in (self.buf.at[:, 0], self.buf.at[:, 0, :, pl.ds(0, a.n - 1)], self.buf.at[0, 0, :, pl.ds(0, a.n - 1)]):
            landed(t, self.send)
        landed(self.buf.at[0, 0, pl.ds(0, a.nz - 1), 0], self.send)


class Scatter:
    def __init__(self, place, plan, buf, from_core, from_q, from_p, from_z, out, send, recv, shares, turn_of):
        self.place, self.plan, self.buf, self.out, self.send, self.recv = place, plan, buf, out, send, recv
        self.core_buf, self.q_buf, self.p_buf, self.z_buf = from_core, from_q, from_p, from_z
        self.shares, self.turn_of = shares, turn_of
        n, nz = place.n, place.nz
        self.at_q = n * n * nz
        self.at_p = self.at_q + n * n * nz
        self.at_z = self.at_p + n * nz
        self.past = []
        self.far = tuple(range(1, n))
        self.order = sorted(range(1, nz), key=lambda k: -min(k, nz - k)) + [0]
        self.size = 2 * buf.shape[4] * LANES

    def when(self, turn, block, body):
        pl.when(self.turn_of(self.place.index(*block)) == turn)(body)

    def send_on(self, turn, block, src, dst, recv, peer):
        push(src, dst, self.send, recv, peer)
        self.past.append((turn, block, src))

    def sent(self, turn, way, *key):
        self.plan.sent((id(self), turn) + key, way, self.size * self.shares[turn])

    def block(self, p, q, k):
        y, x = self.place.yx(p, q)
        return y, self.place.core, self.place.zs[k], x

    def start(self, turn):
        a, name = self.place, (id(self), turn)
        for k in self.order:
            for q in self.far + (0,):
                for p in self.far + (0,):
                    y, x = a.yx_other(p, q)
                    z = a.zs[k]
                    block = y, 1 - a.core, z, x
                    recv = self.recv.at[(q * a.n + p) * a.nz + k]
                    self.when(turn, block, lambda: self.send_on(
                        turn, block, self.buf.at[block], self.core_buf.at[y, z, x], recv, a.other))
                    self.sent(turn, 2, 0, p, q, k)
        add = self.plan.add
        for k in self.order:
            for q in self.far:
                for p in self.far + (0,):
                    add([name + (0, p, q, k)], lambda p=p, q=q, k=k: self.to_q(turn, p, q, k))

            def needs(p):
                return [name + (0, p, 0, k)] + [name + (1, p, q, k) for q in self.far]

            for p in self.far:
                add(needs(p), lambda p=p, k=k: self.to_p(turn, p, k))
            here = needs(0) + [name + (2, p, k) for p in self.far]
            if k:
                add(here, lambda k=k: self.to_z(turn, k))
            else:
                add(here + [name + (3, j) for j in range(1, a.nz)], lambda: self.own(turn))

    def add(self, p, q, k, extra, out=None):
        a = self.place
        y, core, z, x = self.block(p, q, k)
        mine, theirs = self.buf.at[y, core, z, x], self.core_buf.at[y, z, x]
        landed(theirs, self.recv.at[(q * a.n + p) * a.nz + k])
        refs = [mine, theirs] + extra
        if out is None:
            add_up(refs, mine)
        else:
            out(refs)
        return mine

    def to_q(self, turn, p, q, k):
        a = self.place
        block = self.block(p, q, k)

        def body():
            mine = self.add(p, q, k, [])
            recv = self.recv.at[self.at_q + ((a.n - q) * a.n + p) * a.nz + k]
            self.send_on(turn, block, mine, self.q_buf.at[a.n - q - 1, p, a.zs[k]], recv, a.qp[q])

        self.when(turn, block, body)
        self.sent(turn, 0, 1, p, a.n - q, k)

    def q_came(self, p, k):
        a = self.place
        refs = [self.q_buf.at[q - 1, p, a.zs[k]] for q in self.far]
        for q, ref in zip(self.far, refs):
            landed(ref, self.recv.at[self.at_q + (q * a.n + p) * a.nz + k])
        return refs

    def to_p(self, turn, p, k):
        a = self.place
        block = self.block(p, 0, k)

        def body():
            mine = self.add(p, 0, k, self.q_came(p, k))
            recv = self.recv.at[self.at_p + (a.n - p) * a.nz + k]
            self.send_on(turn, block, mine, self.p_buf.at[a.n - p - 1, a.zs[k]], recv, a.pp[p])

        self.when(turn, block, body)
        self.sent(turn, 0, 2, a.n - p, k)

    def p_came(self, k):
        a = self.place
        refs = [self.p_buf.at[p - 1, a.zs[k]] for p in self.far]
        for p, ref in zip(self.far, refs):
            landed(ref, self.recv.at[self.at_p + p * a.nz + k])
        return refs

    def to_z(self, turn, k):
        a = self.place
        block = self.block(0, 0, k)

        def body():
            mine = self.add(0, 0, k, self.q_came(0, k) + self.p_came(k))
            recv = self.recv.at[self.at_z + a.nz - k]
            self.send_on(turn, block, mine, self.z_buf.at[a.nz - k - 1], recv, a.zp[k])

        self.when(turn, block, body)
        self.sent(turn, 1, 3, a.nz - k)

    def own(self, turn):
        a = self.place

        def body():
            extra = self.q_came(0, 0) + self.p_came(0)
            for k in range(1, a.nz):
                landed(self.z_buf.at[k - 1], self.recv.at[self.at_z + k])
            self.add(0, 0, 0, extra + [self.z_buf.at[k] for k in range(a.nz - 1)], self.out)

        self.when(turn, self.block(0, 0, 0), body)

    def drain(self):
        for turn, block, src in self.past:
            self.when(turn, block, lambda: landed(src, self.send))


def sum_rows(refs, r):
    value = refs[0][r, :].astype(FULL)
    for ref in refs[1:]:
        value += ref[r, :].astype(FULL)
    return value


def add_up(refs, dst):
    rows = dst.shape[0]
    step = next(v for v in (224, 144, 64, 48, 32, 16) if rows % v == 0)

    def one(t, carry):
        r = pl.ds(pl.multiple_of(t * step, step), step)
        dst[r, :] = sum_rows(refs, r).astype(LOW)
        return carry

    lax.fori_loop(0, rows // step, one, 0)


def add_over_slice(place, tile, tiles, send, recv):
    base = 0
    for turn, (peers, own) in enumerate((
        (place.tall, place.core * place.nz + place.z), (place.flat, place.y * place.n + place.x)
    )):
        mine = tiles.at[base + own]
        mine[...] = tile
        for peer in peers:
            push(mine, mine, send.at[turn], recv.at[turn], peer)
        landed(tiles.at[pl.ds(base, len(peers))], recv.at[turn])
        tile = tiles[base]
        for k in range(1, len(peers) + 1):
            tile += tiles[base + k]
        landed(tiles.at[pl.ds(base, len(peers))], send.at[turn])
        base += len(peers) + 1
    return tile


def step_kernel(
    place, loss_scale,
    pat, pos, seg, lab, tea, lm, gm,
    new_l, new_g, shared,
    b0, b1, bg, r0c, r0q, r0p, r0z, r1c, r1q, r1p, r1z, rgc, rgq, rgp, rgz, flat, edge, stage, arrange,
    wqkv, wproj, wfc1, wfc2, wpat, wpos, whead, vecs,
    pos_col, seg_col, unit_a, inv_a, h_a, unit_b, inv_b, h_b, qkv, probs, attl, x0, x1, slope, act, kv, low, inv_c,
    tiles, sends, gather_recv, scatter_recv, tile_send, tile_recv,
):
    layer_rows, global_rows = lm.shape[0] // 2, gm.shape[0]
    place.locate()
    me = place.block(0, 0, 0)
    bg[me + (pl.ds(0, global_rows),)] = gm[...].astype(LOW)
    b0[me + (pl.ds(0, layer_rows),)] = lm[pl.ds(0, layer_rows, stride=2), :].astype(LOW)
    b1[me + (pl.ds(0, layer_rows),)] = lm[pl.ds(1, layer_rows, stride=2), :].astype(LOW)
    place.meet()
    plan = Plan()
    gathers = [
        Gather(place, plan, i, buf, sends.at[i], gather_recv.at[i]) for i, buf in enumerate((bg, b0, b1))
    ]
    gathers[0].start()
    gathers[1].start()

    def split_rows(rows):
        half = rows // 32 * 16
        return [pl.ds(at, count) for at, count in ((0, half), (half, rows - half)) if count]

    def finish_layer(n):
        def out(refs):
            for r in split_rows(layer_rows):
                new_l[pl.ds(2 * r.start + n, r.size, stride=2), :] = sum_rows(refs, r)

        return out

    def finish_global(refs):
        for r in split_rows(global_rows):
            new_g[r, :] = sum_rows(refs, r)

    def layer_turn(s):
        first, last = PRE_GAIN_AT // layer_rows, (PROJ_BIAS_AT - 1) // layer_rows
        late = (s < -(-PROJ_AT // layer_rows)).astype(jnp.int32)
        return jnp.where((s >= first) & (s <= last), 2, late)

    def global_turn(s):
        return (s < -(-FINAL_GAIN_AT // global_rows)).astype(jnp.int32)

    scatter_g = Scatter(place, plan, bg, rgc, rgq, rgp, rgz, finish_global, sends.at[5], scatter_recv.at[2],
                        (0.7, 0.5), global_turn)
    scatter_0 = Scatter(place, plan, b0, r0c, r0q, r0p, r0z, finish_layer(0), sends.at[4], scatter_recv.at[1],
                        (0.9, 0.5, 0.05), layer_turn)
    scatter_1 = Scatter(place, plan, b1, r1c, r1q, r1p, r1z, finish_layer(1), sends.at[3], scatter_recv.at[0],
                        (1.0,), lambda s: 0 * s)
    scatters = [scatter_g, scatter_0, scatter_1]
    first_early = -(-PROJ_AT // layer_rows)
    vector_blocks = PRE_GAIN_AT // layer_rows, (PROJ_BIAS_AT - 1) // layer_rows + 1

    head_of_lane = lax.broadcasted_iota(jnp.int32, (1, LANES), 1) // HEAD_DIM

    def loop(count, body, carry=None, time=0.0):
        for i in range(count):
            carry = body(i, carry)
            plan.spend(time)
        return carry

    def rolled(count, body, carry=None, time=0.0):
        carry = lax.fori_loop(0, count, body, 0 if carry is None else carry)
        plan.spend(time)
        return carry

    def each_block(low_end, high_end, one):
        def body(s, carry):
            x = lax.rem(s, place.nx)
            rest = lax.div(s, place.nx)
            z, rest = lax.rem(rest, place.nz), lax.div(rest, place.nz)
            one(s, (lax.div(rest, 2), lax.rem(rest, 2), z, x))
            return carry

        lax.fori_loop(low_end, high_end, body, 0)

    def spread(buf, rows, low_end=0, high_end=2 * place.n * place.n * place.nz):
        def one(s, t):
            if rows % 8 == 0:
                flat[pl.ds(pl.multiple_of(s * rows, 8), rows), :] = buf[t + (pl.ds(0, rows),)].astype(FULL)
            else:
                stage[: buf.shape[4], :] = buf[t].astype(FULL)

                def row(i, carry):
                    flat[pl.ds(s * rows + i, 1), :] = stage[pl.ds(i, 1), :]
                    return carry

                lax.fori_loop(0, rows, row, 0)

        each_block(low_end, high_end, one)

    def gather_rows(buf, rows, low_end=0, high_end=2 * place.n * place.n * place.nz):
        def one(s, t):
            if rows % 8 == 0:
                buf[t + (pl.ds(0, rows),)] = flat[pl.ds(pl.multiple_of(s * rows, 8), rows), :].astype(LOW)
            else:

                def row(i, carry):
                    stage[pl.ds(i, 1), :] = flat[pl.ds(s * rows + i, 1), :]
                    return carry

                lax.fori_loop(0, rows, row, 0)
                buf[t] = stage[: buf.shape[4], :].astype(LOW)

        each_block(low_end, high_end, one)

    def take(dst, at, rows, width):
        count = width // LANES

        def one(c, carry):
            value = flat[pl.ds(at + c, rows, stride=count), :].astype(LOW)
            dst[:rows, pl.ds(pl.multiple_of(c * LANES, LANES), LANES)] = value
            return carry

        lax.fori_loop(0, count, one, 0)

    def take_row(at, width):
        return jnp.concatenate([flat[at + i : at + i + 1, :] for i in range(width // LANES)], axis=1)

    def put_row(at, value):
        for i in range(value.shape[1] // LANES):
            flat[at + i : at + i + 1, :] = value[:, i * LANES : (i + 1) * LANES]

    def put(at, start, width, value, first=0):
        count = width // LANES
        rows = value.shape[0]
        for i in range(value.shape[1] // LANES):
            flat[pl.ds(at + start * count + first + i, rows, stride=count), :] = value[:, i * LANES : (i + 1) * LANES]

    for i in range(SEQ // LANES):
        lanes = slice(i * LANES, (i + 1) * LANES)
        for src, dst in ((pos, pos_col), (seg, seg_col)):
            dst[lanes, :] = jnp.transpose(jnp.broadcast_to(src[0:1, lanes].astype(FULL), (LANES, LANES)))
    pos_row = pos[0:1, :]
    seg_row = seg[0:1, :]
    picked_row = lax.broadcasted_iota(jnp.int32, (PICKED, 1), 0)
    picked_image = jnp.where(picked_row < IMAGES, picked_row, picked_row - IMAGES)
    picked_image = jnp.where(picked_row < 2 * IMAGES, picked_image, -1)
    picked_place = jnp.where(picked_row < IMAGES, TABLE, TABLE + 1)
    picker = ((seg_row == picked_image) & (pos_row == picked_place)).astype(FULL)
    picker_low = picker.astype(LOW)

    arr_row = lax.broadcasted_iota(jnp.int32, (D, GROUP * LANES), 0)
    arr_lane = lax.broadcasted_iota(jnp.int32, (D, GROUP * LANES), 1)
    arrange[...] = (
        (arr_row == (arr_lane % LANES) * GROUP + arr_lane // LANES) & (arr_lane % LANES < GROUPS)
    ).astype(FULL).astype(LOW)

    plan.spend(1.0)
    plan.until(0)
    gathers[2].start()
    spread(bg, global_rows)
    plan.spend(1.2)
    take(wpat, PATCH_AT, PATCH, D)
    take(wpos, POS_AT, TABLE + 2, D)
    wpos[TABLE + 2 :, :] = jnp.zeros((wpos.shape[0] - TABLE - 2, D), LOW)

    def take_head(j, carry):
        value = flat[pl.ds(HEAD_AT + j, GROUPS, stride=GROUP_ROWS), :].astype(LOW)
        whead[:, pl.ds(pl.multiple_of(j * LANES, LANES), LANES)] = value
        return carry

    lax.fori_loop(0, GROUP_ROWS, take_head, 0)
    whead[:, GROUP_ROWS * LANES :] = jnp.zeros((GROUPS, LANES), LOW)
    patch_bias = take_row(PATCH_BIAS_AT, D)
    final_gain = take_row(FINAL_GAIN_AT, D)
    final_bias = take_row(FINAL_BIAS_AT, D)
    head_bias = take_row(HEAD_BIAS_AT, HEAD_LANES)

    row_at = (
        (PRE_GAIN_AT, D), (PRE_BIAS_AT, D), (QUERY_BIAS_AT, D), (VALUE_BIAS_AT, D), (PROJ_BIAS_AT, D),
        (MID_GAIN_AT, D), (MID_BIAS_AT, D), (FC1_BIAS_AT, FF), (FC2_BIAS_AT, D),
    )

    def take_layer(n, buf):
        spread(buf, layer_rows)
        take(wqkv.at[n], QKV_AT, D, 3 * D)
        take(wproj.at[n], PROJ_AT, D, D)
        take(wfc1.at[n], FC1_AT, D, FF)
        take(wfc2.at[n], FC2_AT, FF, D)
        for i, (at, width) in enumerate(row_at):
            vecs[n, i : i + 1, :width] = take_row(at, width)

    def vec(n, i):
        return vecs[n, i : i + 1, : row_at[i][1]]

    plan.spend(2.0)

    def tile_rows(i):
        return pl.ds(pl.multiple_of(i * ROWS, ROWS), ROWS)

    def onehot_of(place):
        iota = lax.broadcasted_iota(jnp.int32, (1, wpos.shape[0]), 1).astype(FULL)
        return (place == iota).astype(LOW)

    def embed(i, carry):
        r = tile_rows(i)
        place = pos_col[r, 0:1]
        pixel = dot(pat[r, :], wpat[...]) + patch_bias
        stream = dot(onehot_of(place), wpos[...]) + jnp.where(place < TABLE, pixel, 0.0)
        x0[r, :] = stream
        unit, inverse = normalise(stream)
        unit_a[r, :] = unit
        inv_a[r, :] = jnp.broadcast_to(inverse, (ROWS, LANES))
        return carry

    rolled(SEQ // ROWS, embed, None, 1.8)
    plan.until(1)
    take_layer(0, b0)
    plan.spend(1.8)
    qkv_bias = jnp.concatenate([vec(0, 2), jnp.zeros((1, D), FULL), vec(0, 3)], axis=1)

    def project(i, carry):
        r = tile_rows(i)
        h = (unit_a[r, :] * vec(0, 0) + vec(0, 1)).astype(LOW)
        h_a[r, :] = h
        qkv[r, :] = (dot(h, wqkv[0]) + qkv_bias).astype(LOW)
        return carry

    rolled(SEQ // ROWS, project, None, 1.2)

    def window_rows(j):
        return pl.ds(min(102 * j // 16 * 16, SEQ - WINDOW), WINDOW)

    def both(x):
        zero = jnp.zeros_like(x)
        return jnp.concatenate([jnp.where(head_of_lane == 0, x, zero), jnp.where(head_of_lane == 1, x, zero)], axis=0)

    def merge(x):
        return jnp.where(head_of_lane == 0, x[:WINDOW], x[WINDOW:])

    attl[...] = jnp.zeros_like(attl)

    def window_masks(j, r):
        own = seg_col[r, :]
        first = 2.0 * j
        mine = (own >= first) & (own < first + 2.0)
        other = jnp.transpose(jnp.where(mine, own, -1.0))
        pair = jnp.concatenate([own, own], axis=1) == jnp.concatenate([other, other], axis=1)
        return mine, pair

    def keep_own(mine, ref, r, lanes, value):
        ref[r, lanes] = jnp.where(mine, value, ref[r, lanes].astype(FULL)).astype(LOW)

    def attend(j, carry):
        r = window_rows(j)
        mine, pair = window_masks(j, r)
        for g in range(HEADS // 2):
            lanes = slice(g * LANES, (g + 1) * LANES)
            q2 = both(qkv[r, lanes])
            keys = qkv[r, D + g * LANES : D + (g + 1) * LANES]
            values = qkv[r, 2 * D + g * LANES : 2 * D + (g + 1) * LANES]
            scores = jnp.where(pair, dot_nt(keys, q2) * SCORE_SCALE, MASK_FILL)
            e = jnp.exp(scores - jnp.max(scores, axis=0, keepdims=True))
            p = jnp.where(pair, e * (1.0 / jnp.sum(e, axis=0, keepdims=True)), 0.0).astype(LOW)
            probs[j, g] = p
            keep_own(mine, attl, r, lanes, merge(dot_tn(p, values)))
        return carry

    loop(WINDOWS, attend, None, 0.28)

    def feed(i, carry):
        r = tile_rows(i)
        middle = x0[r, :] + dot(attl[r, :], wproj[0]) + vec(0, 4)
        unit, inverse = normalise(middle)
        unit_b[r, :] = unit
        inv_b[r, :] = jnp.broadcast_to(inverse, (ROWS, LANES))
        h = (unit * vec(0, 5) + vec(0, 6)).astype(LOW)
        h_b[r, :] = h
        for c in range(4):
            lanes = slice(c * D, (c + 1) * D)
            value, steep = gelu_parts(dot(h, wfc1[0, :, lanes]) + vecs[0, 7:8, lanes])
            act[r, lanes] = value.astype(LOW)
            slope[r, lanes] = steep.astype(LOW)
        x1[r, :] = middle + dot(act[r, :], wfc2[0]) + vec(0, 8)
        return carry

    rolled(SEQ // ROWS, feed, None, 8.0)

    plan.until(2)
    take_layer(1, b1)
    plan.spend(1.5)
    unit_c = x0
    h_c = low

    def kv_rows(i, carry):
        r = tile_rows(i)
        unit, inverse = normalise(x1[r, :])
        unit_c[r, :] = unit
        inv_c[r, :] = jnp.broadcast_to(inverse, (ROWS, LANES))
        h = (unit * vec(1, 0) + vec(1, 1)).astype(LOW)
        h_c[r, :] = h
        bias = jnp.concatenate([jnp.zeros((1, D), FULL), vec(1, 3)], axis=1)
        kv[r, :] = (dot(h, wqkv[1, :, D:]) + bias).astype(LOW)
        return carry

    rolled(SEQ // ROWS, kv_rows, None, 1.2)

    h_s = dot(picker_low, h_c[...]).astype(LOW)
    x_s = sum(dot(picker_low, part) for part in exact_parts(x1[...]))
    q_s = (dot(h_s, wqkv[1, :, :D]) + vec(1, 2)).astype(LOW)
    stack_rows = lax.broadcasted_iota(jnp.int32, (HEADS * PICKED, 1), 0)
    stack_lanes = lax.broadcasted_iota(jnp.int32, (1, D), 1)
    own_head = (stack_rows // PICKED) == (stack_lanes // HEAD_DIM)

    def stack(x):
        tall = jnp.concatenate([x.astype(FULL)] * HEADS, axis=0)
        return jnp.where(own_head, tall, 0.0).astype(LOW)

    def unstack(x):
        x = jnp.where(own_head, x, 0.0)
        total = x[:PICKED]
        for h in range(1, HEADS):
            total += x[h * PICKED : (h + 1) * PICKED]
        return total

    q6 = stack(q_s)
    image6 = jnp.concatenate([picked_image] * HEADS, axis=0)
    mask6 = image6 == seg_row
    scores = jnp.where(mask6, dot_nt(q6, kv[:, :D]) * SCORE_SCALE, MASK_FILL)
    e = jnp.exp(scores - jnp.max(scores, axis=-1, keepdims=True))
    p6 = e / jnp.sum(e, axis=-1, keepdims=True)
    p6_low = p6.astype(LOW)
    att_s = unstack(dot(p6_low, kv[:, D:])).astype(LOW)
    mid_s = x_s + dot(att_s, wproj[1]) + vec(1, 4)
    unit_m, inv_m = normalise(mid_s)
    h2_s = (unit_m * vec(1, 5) + vec(1, 6)).astype(LOW)
    act_s, steep_s = gelu_parts(dot(h2_s, wfc1[1]) + vec(1, 7))
    act_s = act_s.astype(LOW)
    x2_s = mid_s + dot(act_s, wfc2[1]) + vec(1, 8)

    unit_f, inv_f = normalise(x2_s)
    summary = (unit_f * final_gain + final_bias).astype(LOW)
    arranged = dot(summary, arrange[...]).astype(LOW)
    logits = head_bias
    spans = []
    for k in range(GROUP):
        at = 2 * CLASSES * k
        block, shift = at // LANES, at % LANES
        blocks = (at + 2 * CLASSES - 1) // LANES - block + 1
        spans.append((block, shift, blocks))
        s_k = arranged[:, k * LANES : k * LANES + GROUPS]
        wide = (HEAD_LANES // LANES + 1) * LANES
        part = dot(s_k, whead[:, block * LANES : block * LANES + wide])
        if shift:
            part = pltpu.roll(part, wide - shift, 1)
        logits = logits + part[:, :HEAD_LANES]
    column = lax.broadcasted_iota(jnp.int32, (PICKED, HEAD_LANES), 1)
    second = picked_row >= IMAGES
    low_end = jnp.where(second, CLASSES, 0)
    valid = (column >= low_end) & (column < low_end + CLASSES)
    live = picked_row < 2 * IMAGES
    target = jnp.zeros((PICKED, 1), jnp.int32)
    for i in range(IMAGES):
        target = jnp.where(picked_row == i, lab[0, i], target)
        target = jnp.where(picked_row == IMAGES + i, CLASSES + tea[0, i], target)
    hit = column == target
    logits = jnp.where(valid, logits, -3e38)
    top = jnp.max(logits, axis=-1, keepdims=True)
    e = jnp.exp(logits - top)
    total = jnp.sum(e, axis=-1, keepdims=True)
    hit_logit = jnp.sum(jnp.where(hit, logits, 0.0), axis=-1, keepdims=True)
    each = jnp.where(live, top + jnp.log(total) - hit_logit, 0.0)
    loss_sum = jnp.sum(each, axis=0, keepdims=True)
    grad_logits = jnp.where(live, (e / total - hit.astype(FULL)) * loss_scale, 0.0)
    grad_low = grad_logits.astype(LOW)
    grad_wide = jnp.concatenate([grad_low.astype(FULL), jnp.zeros((PICKED, LANES), FULL)], axis=1)

    grad_arranged = []
    for k, (block, shift, blocks) in enumerate(spans):
        turned = (pltpu.roll(grad_wide, shift, 1) if shift else grad_wide).astype(LOW)
        turned = turned[:, : blocks * LANES]
        s_k = arranged[:, k * LANES : k * LANES + GROUPS]
        grad_w = dot_tn(s_k, turned)
        for j in range(blocks):
            rows = pl.ds(HEAD_AT + block + j, GROUPS, stride=GROUP_ROWS)
            piece = grad_w[:, j * LANES : (j + 1) * LANES]
            if k and j == 0:
                piece = piece + flat[rows, :]
            flat[rows, :] = piece
        back = dot_nt(turned, whead[:, block * LANES : (block + blocks) * LANES])
        grad_arranged.append(jnp.concatenate([back, jnp.zeros((PICKED, LANES - GROUPS), FULL)], axis=1))
    parts = jnp.concatenate(exact_parts(jnp.concatenate(grad_arranged, axis=1)), axis=0)
    parts = dot_nt(parts, arrange[...])
    grad_summary = parts[:PICKED] + parts[PICKED : 2 * PICKED] + parts[2 * PICKED :]
    put_row(HEAD_BIAS_AT, col_sum(grad_low))
    put_row(FINAL_GAIN_AT, col_sum(grad_summary * unit_f))
    put_row(FINAL_BIAS_AT, col_sum(grad_summary))
    flat[GLOBAL_END:GLOBAL_ALL, :] = jnp.zeros((GLOBAL_ALL - GLOBAL_END, LANES), FULL)
    for gather in gathers:
        gather.drain()
    border = FINAL_GAIN_AT // global_rows
    gather_rows(bg, global_rows, border + 1)
    kept = (border + 1) * global_rows - FINAL_GAIN_AT
    edge[:kept, :] = flat[FINAL_GAIN_AT : FINAL_GAIN_AT + kept, :]
    plan.spend(6.0)
    scatter_g.start(0)

    dx_s = norm_back(grad_summary, final_gain, unit_f, inv_f)

    out_s = dx_s.astype(LOW)
    for c in range(4):
        put(FC2_AT, c * D, D, dot_tn(act_s[:, c * D : (c + 1) * D], out_s))
    put_row(FC2_BIAS_AT, col_sum(out_s))
    gpre_s = (dot_nt(out_s, wfc2[1]) * steep_s).astype(LOW)
    put(FC1_AT, 0, FF, dot_tn(h2_s, gpre_s))
    put_row(FC1_BIAS_AT, col_sum(gpre_s))
    gh2_s = dot_nt(gpre_s, wfc1[1])
    put_row(MID_GAIN_AT, col_sum(gh2_s * unit_m))
    put_row(MID_BIAS_AT, col_sum(gh2_s))
    gmid_s = dx_s + norm_back(gh2_s, vec(1, 5), unit_m, inv_m)
    gmid_low = gmid_s.astype(LOW)
    put(PROJ_AT, 0, D, dot_tn(att_s, gmid_low))
    put_row(PROJ_BIAS_AT, col_sum(gmid_low))
    plan.spend(1.0)
    gatt6 = stack(dot_nt(gmid_low, wproj[1]).astype(LOW))
    gprob = dot_nt(gatt6, kv[:, D:])
    gscore = (p6 * (gprob - jnp.sum(p6 * gprob, axis=-1, keepdims=True))).astype(LOW)
    gq_s = (unstack(dot(gscore, kv[:, :D])) * SCORE_SCALE).astype(LOW)
    gkeys = (dot_tn(gscore, q6) * SCORE_SCALE).astype(LOW)
    gvalues = dot_tn(p6_low, gatt6).astype(LOW)
    put_row(QUERY_BIAS_AT, col_sum(gq_s))
    put_row(VALUE_BIAS_AT, col_sum(gvalues))
    kv[:, :D] = gkeys
    kv[:, D:] = gvalues
    plan.spend(2.2)
    put(QKV_AT, 0, 3 * D, dot_tn(h_s, gq_s))
    put(QKV_AT, 0, 3 * D, dot_tn(h_c[...], kv[:, :D]), 3)
    put(QKV_AT, 0, 3 * D, dot_tn(h_c[...], kv[:, D:]), 6)
    back_s = jnp.concatenate([dot_nt(gq_s, wqkv[1, :, :D]), gmid_s], axis=1)

    back_parts = jnp.concatenate(exact_parts(back_s), axis=0)
    dx = x1

    def kv_back(i, carry):
        gain_sum, bias_sum = carry
        r = tile_rows(i)
        image_col = seg_col[r, 0:1]
        place_col = pos_col[r, 0:1]
        lane = lax.broadcasted_iota(jnp.int32, (1, PICKED), 1).astype(FULL)
        lane_image = jnp.where(lane < IMAGES, lane, lane - IMAGES)
        lane_place = jnp.where(lane < IMAGES, float(TABLE), TABLE + 1.0)
        back_pick = (
            (image_col == lane_image) & (place_col == lane_place) & (lane < 2.0 * IMAGES)
        ).astype(LOW)
        back = dot(jnp.concatenate([back_pick] * 3, axis=1), back_parts)
        grad = back[:, :D] + dot_nt(kv[r, :], wqkv[1, :, D:])
        unit = unit_c[r, :]
        dx[r, :] = back[:, D:] + norm_back(grad, vec(1, 0), unit, inv_c[r, 0:1])
        return gain_sum + col_sum(grad * unit), bias_sum + col_sum(grad)

    zero_row = jnp.zeros((1, D), FULL)
    gain_sum, bias_sum = rolled(SEQ // ROWS, kv_back, (zero_row, zero_row), 1.1)
    put_row(PRE_GAIN_AT, gain_sum)
    put_row(PRE_BIAS_AT, bias_sum)
    flat[LAYER_END:, :] = jnp.zeros((LAYER_ALL - LAYER_END, LANES), FULL)
    gather_rows(b1, layer_rows)
    plan.spend(1.5)
    scatter_1.start(0)

    def feed_back(i, carry):
        fc1_sum, fc2_sum, proj_sum, gain_sum, bias_sum = carry
        r = tile_rows(i)
        grad_out = dx[r, :]
        out_low = grad_out.astype(LOW)
        low[r, :] = out_low
        for c in range(4):
            lanes = slice(c * D, (c + 1) * D)
            slope[r, lanes] = (dot_nt(out_low, wfc2[0, lanes, :]) * slope[r, lanes].astype(FULL)).astype(LOW)
        grad_h = dot_nt(slope[r, :], wfc1[0])
        unit = unit_b[r, :]
        middle = grad_out + norm_back(grad_h, vec(0, 5), unit, inv_b[r, 0:1])
        dx[r, :] = middle
        middle_low = middle.astype(LOW)
        h2low[r, :] = middle_low
        gatt[r, :] = dot_nt(middle_low, wproj[0]).astype(LOW)
        return (
            fc1_sum + col_sum(slope[r, :]), fc2_sum + col_sum(out_low), proj_sum + col_sum(middle_low),
            gain_sum + col_sum(grad_h * unit), bias_sum + col_sum(grad_h),
        )

    h2low = kv.at[:, 0:D]
    gatt = kv.at[:, D : 2 * D]
    sums = rolled(SEQ // ROWS, feed_back, (jnp.zeros((1, FF), FULL),) + (zero_row,) * 4, 4.5)
    for at, value in zip((FC1_BIAS_AT, FC2_BIAS_AT, PROJ_BIAS_AT, MID_GAIN_AT, MID_BIAS_AT), sums):
        put_row(at, value)


    def feed_weights(c, carry):
        lanes = pl.ds(pl.multiple_of(c * D, D), D)
        put(FC2_AT, c * D, D, dot_tn(act[:, lanes], low[...]))
        put(FC1_AT, 0, FF, dot_tn(h_b[...], slope[:, lanes]), 3 * c)
        return carry

    rolled(4, feed_weights, None, 2.0)
    put(PROJ_AT, 0, D, dot_tn(attl[...], h2low[...]))
    flat[LAYER_END:, :] = jnp.zeros((LAYER_ALL - LAYER_END, LANES), FULL)
    gather_rows(b0, layer_rows, first_early)
    plan.spend(1.6)
    scatter_0.start(0)

    def attend_back(j, carry):
        r = window_rows(j)
        mine, _ = window_masks(j, r)
        for g in range(HEADS // 2):
            lanes = slice(g * LANES, (g + 1) * LANES)
            key_lanes = slice(D + g * LANES, D + (g + 1) * LANES)
            value_lanes = slice(2 * D + g * LANES, 2 * D + (g + 1) * LANES)
            q2 = both(qkv[r, lanes])
            go2 = both(gatt[r, lanes])
            keys = qkv[r, key_lanes]
            p_low = probs[j, g]
            p = p_low.astype(FULL)
            gp = dot_nt(qkv[r, value_lanes], go2)
            gs = (p * (gp - jnp.sum(p * gp, axis=0, keepdims=True))).astype(LOW)
            keep_own(mine, qkv, r, lanes, merge(dot_tn(gs, keys)) * SCORE_SCALE)
            keep_own(mine, qkv, r, key_lanes, dot(gs, q2) * SCORE_SCALE)
            keep_own(mine, qkv, r, value_lanes, dot(p_low, go2))
        return carry

    loop(WINDOWS, attend_back, None, 0.7)

    def qkv_cast(i, carry):
        query_sum, value_sum = carry
        r = tile_rows(i)
        held = seg_col[r, 0:1] < float(IMAGES)
        grads = jnp.where(held, qkv[r, :].astype(FULL), 0.0)
        qkv[r, :] = grads.astype(LOW)
        return query_sum + col_sum(grads[:, :D]), value_sum + col_sum(grads[:, 2 * D :])

    query_sum, value_sum = rolled(SEQ // ROWS, qkv_cast, (zero_row, zero_row), 0.5)
    put_row(QUERY_BIAS_AT, query_sum)
    put_row(VALUE_BIAS_AT, value_sum)

    def qkv_weights(c, carry):
        put(QKV_AT, 0, 3 * D, dot_tn(h_a[...], qkv[:, pl.ds(pl.multiple_of(c * D, D), D)]), 3 * c)
        return carry

    lax.fori_loop(0, 3, qkv_weights, 0)
    gather_rows(b0, layer_rows, 0, first_early)
    plan.spend(1.2)
    scatter_0.start(1)

    def qkv_back(i, carry):
        gain_sum, bias_sum, embed_sum = carry
        r = tile_rows(i)
        grad = dot_nt(qkv[r, :], wqkv[0])
        unit = unit_a[r, :]
        full = dx[r, :] + norm_back(grad, vec(0, 0), unit, inv_a[r, 0:1])
        dx[r, :] = full
        place = pos_col[r, 0:1]
        pixel = jnp.where(place < TABLE, full, 0.0).astype(LOW)
        low[r, :] = pixel
        return gain_sum + col_sum(grad * unit), bias_sum + col_sum(grad), embed_sum + col_sum(pixel)

    gain_sum, bias_sum, embed_sum = rolled(SEQ // ROWS, qkv_back, (zero_row,) * 3, 2.1)
    put_row(PRE_GAIN_AT, gain_sum)
    put_row(PRE_BIAS_AT, bias_sum)
    gather_rows(b0, layer_rows, *vector_blocks)
    plan.spend(0.1)
    scatter_0.start(2)

    for c in range(2):
        put(PATCH_AT, c * D, D, dot_tn(pat[:, c * D : (c + 1) * D], low[...]))
    place_col = pos_col[:, 0:1]
    onehot = onehot_of(place_col)
    high = dx[...].astype(LOW)
    rest = (dx[...] - high.astype(FULL)).astype(LOW)
    table = dot_tn(onehot, high) + dot_tn(onehot, rest)
    put(POS_AT, 0, D, table[: TABLE + 2])
    put_row(PATCH_BIAS_AT, embed_sum)
    flat[FINAL_GAIN_AT : FINAL_GAIN_AT + kept, :] = edge[:kept, :]
    gather_rows(bg, global_rows, 0, border + 1)
    plan.spend(1.5)
    scatter_g.start(1)
    plan.until()

    squares = jnp.zeros((1, 1), FULL)
    for ref in (new_l, new_g):
        used = ref[...]
        squares += jnp.sum(jnp.sum(used * used, axis=0, keepdims=True), axis=1, keepdims=True)
    row = lax.broadcasted_iota(jnp.int32, (8, LANES), 0)
    tile = jnp.where(row == 0, squares, loss_sum)
    shared[...] = add_over_slice(place, tile, tiles, tile_send, tile_recv)
    for scatter in scatters:
        scatter.drain()


def padded(rows):
    return rows + -rows % 16


def step_call(place, loss_scale, pat, pos, seg, lab, tea, lm, gm):
    vmem = pl.BlockSpec(memory_space=pltpu.VMEM)
    smem = pl.BlockSpec(memory_space=pltpu.SMEM)
    n, nz = place.n, place.nz
    rows = padded(lm.shape[0] // 2), padded(lm.shape[0] // 2), padded(gm.shape[0])

    def shape(*dims, kind=FULL):
        return pltpu.VMEM(dims, kind)

    def low(*dims):
        return pltpu.VMEM(dims, LOW)

    scratch = [low(n, 2, nz, n, r, LANES) for r in rows]
    for r in rows:
        scratch += [
            low(n, nz, n, r, LANES), low(n - 1, n, nz, r, LANES), low(n - 1, nz, r, LANES), low(nz - 1, r, LANES)
        ]
    tiles = 2 * nz + n * n
    scratch += [
        shape(LAYER_ALL, LANES), shape(gm.shape[0] + 8, LANES), shape(rows[0], LANES), low(D, GROUP * LANES),
        low(2, D, 3 * D), low(2, D, D), low(2, D, FF), low(2, FF, D),
        low(PATCH, D), low(256, D), low(GROUPS, (GROUP_ROWS + 1) * LANES),
        shape(2, 16, FF),
        shape(SEQ, LANES), shape(SEQ, LANES),
        shape(SEQ, D), shape(SEQ, LANES), low(SEQ, D),
        shape(SEQ, D), shape(SEQ, LANES), low(SEQ, D),
        low(SEQ, 3 * D), low(WINDOWS, HEADS // 2, WINDOW, 2 * WINDOW),
        low(SEQ, D), shape(SEQ, D), shape(SEQ, D),
        low(SEQ, FF), low(SEQ, FF), low(SEQ, 2 * D), low(SEQ, D), shape(SEQ, LANES),
        shape(tiles, 8, LANES),
        pltpu.SemaphoreType.DMA((6,)),
        pltpu.SemaphoreType.DMA((3, nz + nz * n + 2 * n)), pltpu.SemaphoreType.DMA((3, 2 * n * n * nz + n * nz + nz)),
        pltpu.SemaphoreType.DMA((2,)), pltpu.SemaphoreType.DMA((2,)),
    ]
    return pl.pallas_call(
        functools.partial(step_kernel, place, loss_scale),
        out_shape=[jax.ShapeDtypeStruct(a, FULL) for a in (lm.shape, gm.shape, (8, LANES))],
        in_specs=[vmem] * 3 + [smem] * 2 + [vmem] * 2,
        out_specs=[vmem] * 3,
        scratch_shapes=scratch,
        compiler_params=pltpu.CompilerParams(collective_id=0, has_side_effects=True, vmem_limit_bytes=VMEM_BYTES),
    )(pat, pos, seg, lab, tea, lm, gm)

def adam_kernel(total, gl, gg, lm, lo, ls, gm, go, gs, *outs):
    norm = jnp.sqrt(total[0:1, 0:1])
    factor = jnp.minimum(1.0, CLIP_NORM / norm)
    fix_one = 1.0 - BETA_ONE**STEP
    fix_two = 1.0 - BETA_TWO**STEP
    for at, (grad, master, moment, second) in ((0, (gl, lm, lo, ls)), (3, (gg, gm, go, gs))):
        clipped = grad[...] * factor
        new_moment = BETA_ONE * moment[...] + (1.0 - BETA_ONE) * clipped
        new_second = BETA_TWO * second[...] + (1.0 - BETA_TWO) * clipped * clipped
        old = master[...]
        update = new_moment / fix_one / (jnp.sqrt(new_second / fix_two) + ADAM_EPS) + WEIGHT_DECAY * old
        outs[at][...] = old - LEARN_RATE * update
        outs[at + 1][...] = new_moment
        outs[at + 2][...] = new_second
    outs[6][0, 0] = norm[0, 0]
    outs[7][0, 0] = total[1, 0]


def interleave(x):
    rows = x.shape[1] // LANES
    return x.reshape(2, rows, LANES).transpose(1, 0, 2).reshape(2 * rows, LANES)


def layers_apart(x):
    rows = x.shape[0] // 2
    return x.reshape(rows, 2, LANES).transpose(1, 0, 2).reshape(2, rows * LANES)


def shards(sizes, pat, pos, seg, lab, tea, lm, lo, ls, gm, go, gs):
    place = Place(sizes)
    count = sizes[0] * sizes[1]
    assert pat.shape[0] == 1 and lm.shape[1] * count == LAYER_ALL * LANES and gm.shape[0] * count == GLOBAL_ALL * LANES
    lm, lo, ls = interleave(lm), interleave(lo), interleave(ls)
    gm, go, gs = gm.reshape(-1, LANES), go.reshape(-1, LANES), gs.reshape(-1, LANES)
    gl, gg, total = step_call(place, 1.0 / (2 * IMAGES * count), pat[0], pos, seg, lab, tea, lm, gm)
    vmem, smem = pl.BlockSpec(memory_space=pltpu.VMEM), pl.BlockSpec(memory_space=pltpu.SMEM)
    shapes = [lm.shape] * 3 + [gm.shape] * 3 + [(1, 1)] * 2
    *new, norm, loss = pl.pallas_call(
        adam_kernel,
        out_shape=[jax.ShapeDtypeStruct(x, FULL) for x in shapes],
        out_specs=[vmem] * 6 + [smem] * 2,
        compiler_params=pltpu.CompilerParams(vmem_limit_bytes=VMEM_BYTES),
    )(total, gl, gg, lm, lo, ls, gm, go, gs)
    return tuple(layers_apart(x) for x in new[:3]) + tuple(x.reshape(-1) for x in new[3:]) + (norm.reshape(()), loss.reshape(()))


def solution(mesh):
    axes = tuple(mesh.axis_names)
    split = P(axes)
    wide = P(None, axes)
    return jax.shard_map(
        functools.partial(shards, tuple(mesh.shape[a] for a in axes)),
        mesh=mesh,
        in_specs=(split,) * 5 + (wide,) * 3 + (split,) * 3,
        out_specs=(wide,) * 3 + (split,) * 3 + (P(), P()),
        check_vma=False,
    )
```

```python
import functools

import jax
import jax.numpy as jnp
from jax import lax
from jax.experimental import pallas as pl
from jax.experimental.pallas import tpu as pltpu
from jax.sharding import PartitionSpec as P

D = 384
HEADS = 6
HEAD_DIM = 64
FF = 1536
CLASSES = 1000
PATCH = 768
TABLE = 196
IMAGES = 15
SEQ = 768
STEP = 10
LANES = 128

NORM_EPS = 1e-06
BETA_ONE = 0.9
BETA_TWO = 0.999
ADAM_EPS = 1e-08
LEARN_RATE = 0.1
WEIGHT_DECAY = 0.05
CLIP_NORM = 0.01
MASK_FILL = -1000000000.0
SCORE_SCALE = HEAD_DIM ** (-0.5)
LOW = jnp.bfloat16
FULL = jnp.float32
HIGHEST = lax.Precision.HIGHEST

QKV_AT, PROJ_AT, FC1_AT, FC2_AT = 0, 3456, 4608, 9216
PRE_GAIN_AT, PRE_BIAS_AT, QUERY_BIAS_AT, VALUE_BIAS_AT = 13824, 13827, 13830, 13833
PROJ_BIAS_AT, MID_GAIN_AT, MID_BIAS_AT, FC1_BIAS_AT, FC2_BIAS_AT = 13836, 13839, 13842, 13845, 13857
LAYER_END = 13860
PATCH_AT, POS_AT, PATCH_BIAS_AT, FINAL_GAIN_AT, FINAL_BIAS_AT = 0, 2304, 2898, 2901, 2904
HEAD_AT, HEAD_BIAS_AT, GLOBAL_END = 2907, 8907, 8923
GROUP, GROUP_ROWS, GROUPS = 8, 125, 48
HEAD_LANES = 2048
PICKED = 32
WINDOWS, WINDOW = 8, 128
ROWS = 384
LAYER_ALL, GLOBAL_ALL = 14080, 8960
VMEM_BYTES = 64 * 1024 * 1024 - 64 * 1024
MESH = pl.DeviceIdType.MESH


def dot(a, b, dims=(1, 0), precision=None):
    return lax.dot_general(
        a, b, (((dims[0],), (dims[1],)), ((), ())), precision=precision, preferred_element_type=FULL
    )


def dot_nt(a, b, precision=None):
    return dot(a, b, (1, 1), precision)


def dot_tn(a, b, precision=None):
    return dot(a, b, (0, 0), precision)


def row_mean(x):
    return jnp.sum(x, axis=-1, keepdims=True) * (1.0 / D)


def normalise(x):
    center = x - row_mean(x)
    inverse = lax.rsqrt(row_mean(center * center) + NORM_EPS)
    return center * inverse, inverse


def norm_back(grad, gain, unit, inverse):
    scaled = grad * gain
    return inverse * (scaled - row_mean(scaled) - unit * row_mean(scaled * unit))


def col_sum(x):
    return jnp.sum(x.astype(FULL), axis=0, keepdims=True)


def gelu_parts(x):
    bell = jnp.exp2(x * x * (-0.5 * 1.4426950408889634))
    base = 1.0 + (0.3275911 * 0.7071067811865476) * jnp.abs(x)
    t = pl.reciprocal(base, approx=True)
    t = t * (2.0 - base * t)
    tail = (((0.5307027145 * t - 0.7265760135) * t + 0.7107068705) * t - 0.142248368) * t + 0.127414796
    tail = tail * t * bell
    phi = jnp.where(x < 0, tail, 1.0 - tail)
    return x * phi, phi + x * bell * 0.3989422804014327


def exact_parts(x):
    high = x.astype(LOW)
    rest = x - high.astype(FULL)
    middle = rest.astype(LOW)
    return high, middle, (rest - middle.astype(FULL)).astype(LOW)


def wrap(value, size):
    return jnp.where(value >= size, value - size, value)


class Place:
    def __init__(self, sizes):
        dp, fsdp = sizes
        self.n = self.ny = self.nx = dp // 2
        self.nz = fsdp // self.nx
        assert dp == 2 * self.n and fsdp == self.n * self.nz

    def locate(self):
        dp, fsdp = lax.axis_index("dp"), lax.axis_index("fsdp")
        self.y, self.core = dp // 2, dp % 2
        self.z, self.x = fsdp // self.nx, fsdp % self.nx
        self.even = self.core == 0
        self.zs = [wrap(self.z + k, self.nz) for k in range(self.nz)]
        self.ys = [wrap(self.y + k, self.n) for k in range(self.n)]
        self.xs = [wrap(self.x + k, self.n) for k in range(self.n)]
        spans = [(p, q) for p in range(self.n) for q in range(self.n)]
        self.short = {
            (p, q): (jnp.where(self.even, self.ys[p], self.ys[q]), jnp.where(self.even, self.xs[q], self.xs[p]))
            for p, q in spans
        }

    def yx(self, p, q):
        return self.short[p, q]

    def block(self, dz, p, q):
        y, x = self.yx(p, q)
        return y, self.core, self.zs[dz], x

    def device(self, y, core, z, x):
        return y * 2 + core, z * self.nx + x

    def yx_other(self, p, q):
        return jnp.where(self.even, self.ys[q], self.ys[p]), jnp.where(self.even, self.xs[p], self.xs[q])

    def index(self, y, core, z, x):
        return ((y * 2 + core) * self.nz + z) * self.nx + x

    def meet(self):
        def there(y=0, core=0, z=0, x=0):
            return self.device(self.ys[y], 1 - self.core if core else self.core, self.zs[z], self.xs[x])

        self.other = there(core=1)
        self.zp = [there(z=k) for k in range(self.nz)]
        self.pp = [self.device(*self.block(0, k, 0)) for k in range(self.n)]
        self.qp = [self.device(*self.block(0, 0, k)) for k in range(self.n)]
        self.tall = [there(core=c, z=k) for c in range(2) for k in range(self.nz)][1:]
        self.flat = [there(y=j, x=k) for j in range(self.n) for k in range(self.n)][1:]
        barrier = pltpu.get_barrier_semaphore()
        for peer in self.tall + self.flat:
            pl.semaphore_signal(barrier, inc=1, device_id=peer, device_id_type=MESH)
        pl.semaphore_wait(barrier, len(self.tall + self.flat))


def push(src, dst, send, recv, peer):
    pltpu.make_async_remote_copy(
        src_ref=src, dst_ref=dst, send_sem=send, recv_sem=recv, device_id=peer, device_id_type=MESH
    ).start()


def landed(dst, recv):
    pltpu.make_async_copy(dst, dst, recv).wait()


class Plan:
    HOP = 2.5
    RATES = (88e3, 66e3, 600e3)

    def __init__(self):
        self.now, self.free, self.came, self.steps = 0.0, [0.0] * 3, {}, []

    def sent(self, key, way, size):
        begin = max(self.now, self.free[way])
        self.free[way] = begin + size / self.RATES[way]
        self.came[key] = max(self.came.get(key, 0.0), self.free[way] + self.HOP)

    def add(self, needs, run, name=None):
        self.steps.append((needs, run, name))

    def ready(self, step):
        return max((self.came.get(key, 1e9) for key in step[0]), default=0.0)

    def run(self, step):
        self.steps.remove(step)
        self.now = max(self.now, self.ready(step)) + 0.03
        step[1]()

    def spend(self, time):
        self.now += time
        while True:
            step = min((step for step in self.steps if self.ready(step) <= self.now), key=self.ready, default=None)
            if step is None:
                return
            self.run(step)

    def due(self, time):
        return any(self.ready(step) <= self.now + time for step in self.steps)

    def until(self, name=None):
        while self.steps and (name is None or any(step[2] == name for step in self.steps)):
            self.run(min(self.steps, key=self.ready))


class Gather:
    def __init__(self, place, plan, name, buf, send, recv):
        self.place, self.plan, self.name, self.buf, self.send, self.recv = place, plan, name, buf, send, recv
        self.from_p = place.nz
        self.from_q = self.from_p + place.nz * place.n
        self.from_core = self.from_q + place.n
        self.size = 2 * buf.shape[4] * LANES

    def sent(self, way, count, *key):
        self.plan.sent((self.name,) + key, way, count * self.size)

    def to_p(self, dz):
        a, t = self.place, self.buf.at[self.place.block(dz, 0, 0)]
        for k in range(1, a.n):
            push(t, t, self.send, self.recv.at[self.from_p + dz * a.n + a.n - k], a.pp[k])
            self.sent(0, 1, 1, dz, a.n - k)

    def to_q(self, dz, p):
        a, t = self.place, self.buf.at[self.place.block(dz, p, 0)]
        for k in range(1, a.n):
            push(t, t, self.send, self.recv.at[self.from_q + a.n - k], a.qp[k])
            self.sent(0, 1, 2, dz, p)

    def start(self):
        a, t = self.place, self.buf.at[self.place.block(0, 0, 0)]
        self.to_p(0)
        for k in range(1, a.nz):
            push(t, t, self.send, self.recv.at[a.nz - k], a.zp[k])
            self.sent(1, 1, 0, a.nz - k)
        self.to_q(0, 0)
        far = range(1, a.n)
        near = sorted(range(1, a.nz), key=lambda k: min(k, a.nz - k))
        add = self.plan.add
        for p in far:
            add([(self.name, 1, 0, p)], lambda p=p: self.p_came(0, p))
        for k in near:
            add([(self.name, 0, k)], lambda k=k: self.z_came(k))
        for k in near:
            for p in far:
                add([(self.name, 1, k, p)], lambda k=k, p=p: self.p_came(k, p))
        mine = [(self.name, 0, k) for k in near] + [(self.name, 1, k, p) for k in range(a.nz) for p in far]
        add(mine, lambda: self.to_core(0))
        for q in far:
            add([(self.name, 2, k, p) for k in range(a.nz) for p in range(a.n)], lambda q=q: self.q_came(q))
        add([(self.name, 3, q) for q in range(a.n)], self.finish, self.name)

    def z_came(self, dz):
        landed(self.buf.at[self.place.block(dz, 0, 0)], self.recv.at[dz])
        self.to_p(dz)
        self.to_q(dz, 0)

    def p_came(self, dz, p):
        landed(self.buf.at[self.place.block(dz, p, 0)], self.recv.at[self.from_p + dz * self.place.n + p])
        self.to_q(dz, p)

    def group(self, core, q):
        a = self.place
        return self.buf.at[:, 0, :, a.xs[q]] if core == 0 else self.buf.at[a.ys[q], 1]

    def to_core(self, q):
        a = self.place
        for core in range(2):

            @pl.when(a.core == core)
            def _():
                t = self.group(core, q)
                push(t, t, self.send, self.recv.at[self.from_core + q], a.other)

        self.sent(2, a.n * a.nz, 3, q)

    def q_came(self, q):
        landed(self.buf.at[:, 0, :, 0], self.recv.at[self.from_q + q])
        self.to_core(q)

    def finish(self):
        for q in range(self.place.n):
            landed(self.buf.at[:, 0, :, 0], self.recv.at[self.from_core + q])

    def drain(self):
        a = self.place
        for t in (self.buf.at[:, 0], self.buf.at[:, 0, :, pl.ds(0, a.n - 1)], self.buf.at[0, 0, :, pl.ds(0, a.n - 1)]):
            landed(t, self.send)
        landed(self.buf.at[0, 0, pl.ds(0, a.nz - 1), 0], self.send)


class Scatter:
    def __init__(self, place, plan, buf, from_core, from_q, from_p, from_z, out, send, recv, shares, turn_of):
        self.place, self.plan, self.buf, self.out, self.send, self.recv = place, plan, buf, out, send, recv
        self.core_buf, self.q_buf, self.p_buf, self.z_buf = from_core, from_q, from_p, from_z
        self.shares, self.turn_of = shares, turn_of
        n, nz = place.n, place.nz
        self.at_q = n * n * nz
        self.at_p = self.at_q + n * n * nz
        self.at_z = self.at_p + n * nz
        self.past = []
        self.far = tuple(range(1, n))
        self.order = sorted(range(1, nz), key=lambda k: -min(k, nz - k)) + [0]
        self.size = 2 * buf.shape[4] * LANES

    def when(self, turn, block, body):
        pl.when(self.turn_of(self.place.index(*block)) == turn)(body)

    def send_on(self, turn, block, src, dst, recv, peer):
        push(src, dst, self.send, recv, peer)
        self.past.append((turn, block, src))

    def sent(self, turn, way, *key):
        self.plan.sent((id(self), turn) + key, way, self.size * self.shares[turn])

    def block(self, p, q, k):
        y, x = self.place.yx(p, q)
        return y, self.place.core, self.place.zs[k], x

    def start(self, turn):
        a, name = self.place, (id(self), turn)
        for k in self.order:
            for q in self.far + (0,):
                for p in self.far + (0,):
                    y, x = a.yx_other(p, q)
                    z = a.zs[k]
                    block = y, 1 - a.core, z, x
                    recv = self.recv.at[(q * a.n + p) * a.nz + k]
                    self.when(turn, block, lambda: self.send_on(
                        turn, block, self.buf.at[block], self.core_buf.at[y, z, x], recv, a.other))
                    self.sent(turn, 2, 0, p, q, k)
        add = self.plan.add
        for k in self.order:
            for q in self.far:
                for p in self.far + (0,):
                    add([name + (0, p, q, k)], lambda p=p, q=q, k=k: self.to_q(turn, p, q, k))

            def needs(p):
                return [name + (0, p, 0, k)] + [name + (1, p, q, k) for q in self.far]

            for p in self.far:
                add(needs(p), lambda p=p, k=k: self.to_p(turn, p, k))
            here = needs(0) + [name + (2, p, k) for p in self.far]
            if k:
                add(here, lambda k=k: self.to_z(turn, k))
            else:
                add(here + [name + (3, j) for j in range(1, a.nz)], lambda: self.own(turn))

    def add(self, p, q, k, extra, out=None):
        a = self.place
        y, core, z, x = self.block(p, q, k)
        mine, theirs = self.buf.at[y, core, z, x], self.core_buf.at[y, z, x]
        landed(theirs, self.recv.at[(q * a.n + p) * a.nz + k])
        refs = [mine, theirs] + extra
        if out is None:
            add_up(refs, mine)
        else:
            out(refs)
        return mine

    def to_q(self, turn, p, q, k):
        a = self.place
        block = self.block(p, q, k)

        def body():
            mine = self.add(p, q, k, [])
            recv = self.recv.at[self.at_q + ((a.n - q) * a.n + p) * a.nz + k]
            self.send_on(turn, block, mine, self.q_buf.at[a.n - q - 1, p, a.zs[k]], recv, a.qp[q])

        self.when(turn, block, body)
        self.sent(turn, 0, 1, p, a.n - q, k)

    def q_came(self, p, k):
        a = self.place
        refs = [self.q_buf.at[q - 1, p, a.zs[k]] for q in self.far]
        for q, ref in zip(self.far, refs):
            landed(ref, self.recv.at[self.at_q + (q * a.n + p) * a.nz + k])
        return refs

    def to_p(self, turn, p, k):
        a = self.place
        block = self.block(p, 0, k)

        def body():
            mine = self.add(p, 0, k, self.q_came(p, k))
            recv = self.recv.at[self.at_p + (a.n - p) * a.nz + k]
            self.send_on(turn, block, mine, self.p_buf.at[a.n - p - 1, a.zs[k]], recv, a.pp[p])

        self.when(turn, block, body)
        self.sent(turn, 0, 2, a.n - p, k)

    def p_came(self, k):
        a = self.place
        refs = [self.p_buf.at[p - 1, a.zs[k]] for p in self.far]
        for p, ref in zip(self.far, refs):
            landed(ref, self.recv.at[self.at_p + p * a.nz + k])
        return refs

    def to_z(self, turn, k):
        a = self.place
        block = self.block(0, 0, k)

        def body():
            mine = self.add(0, 0, k, self.q_came(0, k) + self.p_came(k))
            recv = self.recv.at[self.at_z + a.nz - k]
            self.send_on(turn, block, mine, self.z_buf.at[a.nz - k - 1], recv, a.zp[k])

        self.when(turn, block, body)
        self.sent(turn, 1, 3, a.nz - k)

    def own(self, turn):
        a = self.place

        def body():
            extra = self.q_came(0, 0) + self.p_came(0)
            for k in range(1, a.nz):
                landed(self.z_buf.at[k - 1], self.recv.at[self.at_z + k])
            self.add(0, 0, 0, extra + [self.z_buf.at[k] for k in range(a.nz - 1)], self.out)

        self.when(turn, self.block(0, 0, 0), body)

    def drain(self):
        for turn, block, src in self.past:
            self.when(turn, block, lambda: landed(src, self.send))


def sum_rows(refs, r):
    value = refs[0][r, :].astype(FULL)
    for ref in refs[1:]:
        value += ref[r, :].astype(FULL)
    return value


def add_up(refs, dst):
    rows = dst.shape[0]
    step = next(v for v in (224, 144, 64, 48, 32, 16) if rows % v == 0)

    def one(t, carry):
        r = pl.ds(pl.multiple_of(t * step, step), step)
        dst[r, :] = sum_rows(refs, r).astype(LOW)
        return carry

    lax.fori_loop(0, rows // step, one, 0)


def add_over_slice(place, tile, tiles, send, recv):
    base = 0
    for turn, (peers, own) in enumerate((
        (place.tall, place.core * place.nz + place.z), (place.flat, place.y * place.n + place.x)
    )):
        mine = tiles.at[base + own]
        mine[...] = tile
        for peer in peers:
            push(mine, mine, send.at[turn], recv.at[turn], peer)
        landed(tiles.at[pl.ds(base, len(peers))], recv.at[turn])
        tile = tiles[base]
        for k in range(1, len(peers) + 1):
            tile += tiles[base + k]
        landed(tiles.at[pl.ds(base, len(peers))], send.at[turn])
        base += len(peers) + 1
    return tile


def step_kernel(
    place, loss_scale,
    pat_hbm, pos, seg, lab, tea, lm, gm,
    new_l, new_g, shared,
    b0, b1, bg, r0c, r0q, r0p, r0z, r1c, r1q, r1p, r1z, rgc, rgq, rgp, rgz, flat, edge, stage, arrange,
    wqkv, wproj, wfc1, wfc2, wpat, wpos, whead, vecs,
    pos_col, seg_col, unit_a, inv_a, h_a, unit_b, inv_b, h_b, qkv, probs, attl, x0, x1, slope, act, kv, low, inv_c,
    pat, pat_sem, tiles, sends, gather_recv, scatter_recv, tile_send, tile_recv,
):
    layer_rows, global_rows = lm.shape[0] // 2, gm.shape[0]
    place.locate()
    me = place.block(0, 0, 0)
    pat_load = pltpu.make_async_copy(pat_hbm, pat, pat_sem)
    pat_load.start()
    bg[me + (pl.ds(0, global_rows),)] = gm[...].astype(LOW)
    b0[me + (pl.ds(0, layer_rows),)] = lm[pl.ds(0, layer_rows, stride=2), :].astype(LOW)
    b1[me + (pl.ds(0, layer_rows),)] = lm[pl.ds(1, layer_rows, stride=2), :].astype(LOW)
    place.meet()
    plan = Plan()
    gathers = [
        Gather(place, plan, i, buf, sends.at[i], gather_recv.at[i]) for i, buf in enumerate((bg, b0, b1))
    ]
    gathers[0].start()
    gathers[1].start()

    def split_rows(rows):
        half = rows // 32 * 16
        return [pl.ds(at, count) for at, count in ((0, half), (half, rows - half)) if count]

    def finish_layer(n):
        def out(refs):
            for r in split_rows(layer_rows):
                new_l[pl.ds(2 * r.start + n, r.size, stride=2), :] = sum_rows(refs, r)

        return out

    def finish_global(refs):
        for r in split_rows(global_rows):
            new_g[r, :] = sum_rows(refs, r)

    def layer_turn(s):
        first, last = PRE_GAIN_AT // layer_rows, (PROJ_BIAS_AT - 1) // layer_rows
        late = (s < -(-PROJ_AT // layer_rows)).astype(jnp.int32)
        return jnp.where((s >= first) & (s <= last), 2, late)

    def global_turn(s):
        return (s < -(-FINAL_GAIN_AT // global_rows)).astype(jnp.int32)

    scatter_g = Scatter(place, plan, bg, rgc, rgq, rgp, rgz, finish_global, sends.at[5], scatter_recv.at[2],
                        (0.65, 0.4), global_turn)
    scatter_0 = Scatter(place, plan, b0, r0c, r0q, r0p, r0z, finish_layer(0), sends.at[4], scatter_recv.at[1],
                        (0.75, 0.35, 0.03), layer_turn)
    scatter_1 = Scatter(place, plan, b1, r1c, r1q, r1p, r1z, finish_layer(1), sends.at[3], scatter_recv.at[0],
                        (1.0,), lambda s: 0 * s)
    scatters = [scatter_g, scatter_0, scatter_1]
    first_early = -(-PROJ_AT // layer_rows)
    vector_blocks = PRE_GAIN_AT // layer_rows, (PROJ_BIAS_AT - 1) // layer_rows + 1

    head_of_lane = lax.broadcasted_iota(jnp.int32, (1, LANES), 1) // HEAD_DIM

    def loop(count, body, carry=None, time=0.0):
        for i in range(count):
            carry = body(i, carry)
            plan.spend(time)
        return carry

    def rolled(count, body, carry=None, time=0.0):
        traced = []

        def one(i, carry):
            assert not traced
            traced.append(i)
            carry = body(i, carry)
            for k in range(count):
                if plan.due(time):
                    pl.when(i == k)(lambda: plan.spend(time))
                else:
                    plan.spend(time)
            return carry

        return lax.fori_loop(0, count, one, 0 if carry is None else carry)

    def each_block(low_end, high_end, one):
        def body(s, carry):
            x = lax.rem(s, place.nx)
            rest = lax.div(s, place.nx)
            z, rest = lax.rem(rest, place.nz), lax.div(rest, place.nz)
            one(s, (lax.div(rest, 2), lax.rem(rest, 2), z, x))
            return carry

        lax.fori_loop(low_end, high_end, body, 0)

    def spread(buf, rows, low_end=0, high_end=2 * place.n * place.n * place.nz):
        def one(s, t):
            if rows % 8 == 0:
                flat[pl.ds(pl.multiple_of(s * rows, 8), rows), :] = buf[t + (pl.ds(0, rows),)].astype(FULL)
            else:
                stage[: buf.shape[4], :] = buf[t].astype(FULL)

                def row(i, carry):
                    flat[pl.ds(s * rows + i, 1), :] = stage[pl.ds(i, 1), :]
                    return carry

                lax.fori_loop(0, rows, row, 0)

        each_block(low_end, high_end, one)

    def gather_rows(buf, rows, low_end=0, high_end=2 * place.n * place.n * place.nz):
        def one(s, t):
            if rows % 8 == 0:
                buf[t + (pl.ds(0, rows),)] = flat[pl.ds(pl.multiple_of(s * rows, 8), rows), :].astype(LOW)
            else:

                def row(i, carry):
                    stage[pl.ds(i, 1), :] = flat[pl.ds(s * rows + i, 1), :]
                    return carry

                lax.fori_loop(0, rows, row, 0)
                buf[t] = stage[: buf.shape[4], :].astype(LOW)

        each_block(low_end, high_end, one)

    def take(dst, at, rows, width):
        count = width // LANES

        def one(c, carry):
            value = flat[pl.ds(at + c, rows, stride=count), :].astype(LOW)
            dst[:rows, pl.ds(pl.multiple_of(c * LANES, LANES), LANES)] = value
            return carry

        lax.fori_loop(0, count, one, 0)

    def take_row(at, width):
        return jnp.concatenate([flat[at + i : at + i + 1, :] for i in range(width // LANES)], axis=1)

    def put_row(at, value):
        for i in range(value.shape[1] // LANES):
            flat[at + i : at + i + 1, :] = value[:, i * LANES : (i + 1) * LANES]

    def put(at, start, width, value, first=0):
        count = width // LANES
        rows = value.shape[0]
        for i in range(value.shape[1] // LANES):
            flat[pl.ds(at + start * count + first + i, rows, stride=count), :] = value[:, i * LANES : (i + 1) * LANES]

    for i in range(SEQ // LANES):
        lanes = slice(i * LANES, (i + 1) * LANES)
        for src, dst in ((pos, pos_col), (seg, seg_col)):
            dst[lanes, :] = jnp.transpose(jnp.broadcast_to(src[0:1, lanes].astype(FULL), (LANES, LANES)))
    pos_row = pos[0:1, :]
    seg_row = seg[0:1, :]
    picked_row = lax.broadcasted_iota(jnp.int32, (PICKED, 1), 0)
    picked_image = jnp.where(picked_row < IMAGES, picked_row, picked_row - IMAGES)
    picked_image = jnp.where(picked_row < 2 * IMAGES, picked_image, -1)
    picked_place = jnp.where(picked_row < IMAGES, TABLE, TABLE + 1)
    picker = ((seg_row == picked_image) & (pos_row == picked_place)).astype(FULL)
    picker_low = picker.astype(LOW)

    arr_row = lax.broadcasted_iota(jnp.int32, (D, GROUP * LANES), 0)
    arr_lane = lax.broadcasted_iota(jnp.int32, (D, GROUP * LANES), 1)
    arrange[...] = (
        (arr_row == (arr_lane % LANES) * GROUP + arr_lane // LANES) & (arr_lane % LANES < GROUPS)
    ).astype(FULL).astype(LOW)

    plan.spend(1.0)
    plan.until(0)
    gathers[2].start()
    spread(bg, global_rows)
    plan.spend(1.2)
    take(wpat, PATCH_AT, PATCH, D)
    take(wpos, POS_AT, TABLE + 2, D)
    wpos[TABLE + 2 :, :] = jnp.zeros((wpos.shape[0] - TABLE - 2, D), LOW)

    def take_head(j, carry):
        value = flat[pl.ds(HEAD_AT + j, GROUPS, stride=GROUP_ROWS), :].astype(LOW)
        whead[:, pl.ds(pl.multiple_of(j * LANES, LANES), LANES)] = value
        return carry

    lax.fori_loop(0, GROUP_ROWS, take_head, 0)
    whead[:, GROUP_ROWS * LANES :] = jnp.zeros((GROUPS, LANES), LOW)
    patch_bias = take_row(PATCH_BIAS_AT, D)
    final_gain = take_row(FINAL_GAIN_AT, D)
    final_bias = take_row(FINAL_BIAS_AT, D)
    head_bias = take_row(HEAD_BIAS_AT, HEAD_LANES)

    row_at = (
        (PRE_GAIN_AT, D), (PRE_BIAS_AT, D), (QUERY_BIAS_AT, D), (VALUE_BIAS_AT, D), (PROJ_BIAS_AT, D),
        (MID_GAIN_AT, D), (MID_BIAS_AT, D), (FC1_BIAS_AT, FF), (FC2_BIAS_AT, D),
    )

    def take_layer(n, buf):
        spread(buf, layer_rows)
        take(wqkv.at[n], QKV_AT, D, 3 * D)
        take(wproj.at[n], PROJ_AT, D, D)
        take(wfc1.at[n], FC1_AT, D, FF)
        take(wfc2.at[n], FC2_AT, FF, D)
        for i, (at, width) in enumerate(row_at):
            vecs[n, i : i + 1, :width] = take_row(at, width)

    def vec(n, i):
        return vecs[n, i : i + 1, : row_at[i][1]]

    plan.spend(2.0)

    def tile_rows(i):
        return pl.ds(pl.multiple_of(i * ROWS, ROWS), ROWS)

    def onehot_of(place):
        iota = lax.broadcasted_iota(jnp.int32, (1, wpos.shape[0]), 1).astype(FULL)
        return (place == iota).astype(LOW)

    def embed(i, carry):
        r = tile_rows(i)
        place = pos_col[r, 0:1]
        pixel = dot(pat[r, :], wpat[...]) + patch_bias
        stream = dot(onehot_of(place), wpos[...]) + jnp.where(place < TABLE, pixel, 0.0)
        x0[r, :] = stream
        unit, inverse = normalise(stream)
        unit_a[r, :] = unit
        inv_a[r, :] = jnp.broadcast_to(inverse, (ROWS, LANES))
        return carry

    pat_load.wait()
    rolled(SEQ // ROWS, embed, None, 0.9)
    plan.until(1)
    take_layer(0, b0)
    plan.spend(1.8)
    qkv_bias = jnp.concatenate([vec(0, 2), jnp.zeros((1, D), FULL), vec(0, 3)], axis=1)

    def project(i, carry):
        r = tile_rows(i)
        h = (unit_a[r, :] * vec(0, 0) + vec(0, 1)).astype(LOW)
        h_a[r, :] = h
        qkv[r, :] = (dot(h, wqkv[0]) + qkv_bias).astype(LOW)
        return carry

    rolled(SEQ // ROWS, project, None, 0.6)

    def window_rows(j):
        return pl.ds(min(102 * j // 16 * 16, SEQ - WINDOW), WINDOW)

    def both(x):
        zero = jnp.zeros_like(x)
        return jnp.concatenate([jnp.where(head_of_lane == 0, x, zero), jnp.where(head_of_lane == 1, x, zero)], axis=0)

    def merge(x):
        return jnp.where(head_of_lane == 0, x[:WINDOW], x[WINDOW:])

    attl[...] = jnp.zeros_like(attl)

    def window_masks(j, r):
        own = seg_col[r, :]
        first = 2.0 * j
        mine = (own >= first) & (own < first + 2.0)
        other = jnp.transpose(jnp.where(mine, own, -1.0))
        pair = jnp.concatenate([own, own], axis=1) == jnp.concatenate([other, other], axis=1)
        return mine, pair

    def keep_own(mine, ref, r, lanes, value):
        ref[r, lanes] = jnp.where(mine, value, ref[r, lanes].astype(FULL)).astype(LOW)

    def attend(j, carry):
        r = window_rows(j)
        mine, pair = window_masks(j, r)
        for g in range(HEADS // 2):
            lanes = slice(g * LANES, (g + 1) * LANES)
            q2 = both(qkv[r, lanes])
            keys = qkv[r, D + g * LANES : D + (g + 1) * LANES]
            values = qkv[r, 2 * D + g * LANES : 2 * D + (g + 1) * LANES]
            scores = jnp.where(pair, dot_nt(keys, q2) * SCORE_SCALE, MASK_FILL)
            e = jnp.exp(scores - jnp.max(scores, axis=0, keepdims=True))
            p = jnp.where(pair, e * (1.0 / jnp.sum(e, axis=0, keepdims=True)), 0.0).astype(LOW)
            probs[j, g] = p
            keep_own(mine, attl, r, lanes, merge(dot_tn(p, values)))
        return carry

    loop(WINDOWS, attend, None, 0.28)

    def feed(i, carry):
        r = tile_rows(i)
        middle = x0[r, :] + dot(attl[r, :], wproj[0]) + vec(0, 4)
        unit, inverse = normalise(middle)
        unit_b[r, :] = unit
        inv_b[r, :] = jnp.broadcast_to(inverse, (ROWS, LANES))
        h = (unit * vec(0, 5) + vec(0, 6)).astype(LOW)
        h_b[r, :] = h
        for c in range(4):
            lanes = slice(c * D, (c + 1) * D)
            value, steep = gelu_parts(dot(h, wfc1[0, :, lanes]) + vecs[0, 7:8, lanes])
            act[r, lanes] = value.astype(LOW)
            slope[r, lanes] = steep.astype(LOW)
        x1[r, :] = middle + dot(act[r, :], wfc2[0]) + vec(0, 8)
        return carry

    rolled(SEQ // ROWS, feed, None, 4.0)

    plan.until(2)
    take_layer(1, b1)
    plan.spend(1.5)
    unit_c = x0
    h_c = low

    def kv_rows(i, carry):
        r = tile_rows(i)
        unit, inverse = normalise(x1[r, :])
        unit_c[r, :] = unit
        inv_c[r, :] = jnp.broadcast_to(inverse, (ROWS, LANES))
        h = (unit * vec(1, 0) + vec(1, 1)).astype(LOW)
        h_c[r, :] = h
        bias = jnp.concatenate([jnp.zeros((1, D), FULL), vec(1, 3)], axis=1)
        kv[r, :] = (dot(h, wqkv[1, :, D:]) + bias).astype(LOW)
        return carry

    rolled(SEQ // ROWS, kv_rows, None, 0.6)

    h_s = dot(picker_low, h_c[...]).astype(LOW)
    x_s = sum(dot(picker_low, part) for part in exact_parts(x1[...]))
    q_s = (dot(h_s, wqkv[1, :, :D]) + vec(1, 2)).astype(LOW)
    stack_rows = lax.broadcasted_iota(jnp.int32, (HEADS * PICKED, 1), 0)
    stack_lanes = lax.broadcasted_iota(jnp.int32, (1, D), 1)
    own_head = (stack_rows // PICKED) == (stack_lanes // HEAD_DIM)

    def stack(x):
        tall = jnp.concatenate([x.astype(FULL)] * HEADS, axis=0)
        return jnp.where(own_head, tall, 0.0).astype(LOW)

    def unstack(x):
        x = jnp.where(own_head, x, 0.0)
        total = x[:PICKED]
        for h in range(1, HEADS):
            total += x[h * PICKED : (h + 1) * PICKED]
        return total

    q6 = stack(q_s)
    image6 = jnp.concatenate([picked_image] * HEADS, axis=0)
    mask6 = image6 == seg_row
    scores = jnp.where(mask6, dot_nt(q6, kv[:, :D]) * SCORE_SCALE, MASK_FILL)
    e = jnp.exp(scores - jnp.max(scores, axis=-1, keepdims=True))
    p6 = e / jnp.sum(e, axis=-1, keepdims=True)
    p6_low = p6.astype(LOW)
    att_s = unstack(dot(p6_low, kv[:, D:])).astype(LOW)
    mid_s = x_s + dot(att_s, wproj[1]) + vec(1, 4)
    unit_m, inv_m = normalise(mid_s)
    h2_s = (unit_m * vec(1, 5) + vec(1, 6)).astype(LOW)
    act_s, steep_s = gelu_parts(dot(h2_s, wfc1[1]) + vec(1, 7))
    act_s = act_s.astype(LOW)
    x2_s = mid_s + dot(act_s, wfc2[1]) + vec(1, 8)

    unit_f, inv_f = normalise(x2_s)
    summary = (unit_f * final_gain + final_bias).astype(LOW)
    arranged = dot(summary, arrange[...]).astype(LOW)
    logits = head_bias
    spans = []
    for k in range(GROUP):
        at = 2 * CLASSES * k
        block, shift = at // LANES, at % LANES
        blocks = (at + 2 * CLASSES - 1) // LANES - block + 1
        spans.append((block, shift, blocks))
        s_k = arranged[:, k * LANES : k * LANES + GROUPS]
        wide = (HEAD_LANES // LANES + 1) * LANES
        part = dot(s_k, whead[:, block * LANES : block * LANES + wide])
        if shift:
            part = pltpu.roll(part, wide - shift, 1)
        logits = logits + part[:, :HEAD_LANES]
    column = lax.broadcasted_iota(jnp.int32, (PICKED, HEAD_LANES), 1)
    second = picked_row >= IMAGES
    low_end = jnp.where(second, CLASSES, 0)
    valid = (column >= low_end) & (column < low_end + CLASSES)
    live = picked_row < 2 * IMAGES
    target = jnp.zeros((PICKED, 1), jnp.int32)
    for i in range(IMAGES):
        target = jnp.where(picked_row == i, lab[0, i], target)
        target = jnp.where(picked_row == IMAGES + i, CLASSES + tea[0, i], target)
    hit = column == target
    logits = jnp.where(valid, logits, -3e38)
    top = jnp.max(logits, axis=-1, keepdims=True)
    e = jnp.exp(logits - top)
    total = jnp.sum(e, axis=-1, keepdims=True)
    hit_logit = jnp.sum(jnp.where(hit, logits, 0.0), axis=-1, keepdims=True)
    each = jnp.where(live, top + jnp.log(total) - hit_logit, 0.0)
    loss_sum = jnp.sum(each, axis=0, keepdims=True)
    grad_logits = jnp.where(live, (e / total - hit.astype(FULL)) * loss_scale, 0.0)
    grad_low = grad_logits.astype(LOW)
    grad_wide = jnp.concatenate([grad_low.astype(FULL), jnp.zeros((PICKED, LANES), FULL)], axis=1)

    grad_arranged = []
    for k, (block, shift, blocks) in enumerate(spans):
        turned = (pltpu.roll(grad_wide, shift, 1) if shift else grad_wide).astype(LOW)
        turned = turned[:, : blocks * LANES]
        s_k = arranged[:, k * LANES : k * LANES + GROUPS]
        grad_w = dot_tn(s_k, turned)
        for j in range(blocks):
            rows = pl.ds(HEAD_AT + block + j, GROUPS, stride=GROUP_ROWS)
            piece = grad_w[:, j * LANES : (j + 1) * LANES]
            if k and j == 0:
                piece = piece + flat[rows, :]
            flat[rows, :] = piece
        back = dot_nt(turned, whead[:, block * LANES : (block + blocks) * LANES])
        grad_arranged.append(jnp.concatenate([back, jnp.zeros((PICKED, LANES - GROUPS), FULL)], axis=1))
    parts = jnp.concatenate(exact_parts(jnp.concatenate(grad_arranged, axis=1)), axis=0)
    parts = dot_nt(parts, arrange[...])
    grad_summary = parts[:PICKED] + parts[PICKED : 2 * PICKED] + parts[2 * PICKED :]
    put_row(HEAD_BIAS_AT, col_sum(grad_low))
    put_row(FINAL_GAIN_AT, col_sum(grad_summary * unit_f))
    put_row(FINAL_BIAS_AT, col_sum(grad_summary))
    flat[GLOBAL_END:GLOBAL_ALL, :] = jnp.zeros((GLOBAL_ALL - GLOBAL_END, LANES), FULL)
    for gather in gathers:
        gather.drain()
    border = FINAL_GAIN_AT // global_rows
    gather_rows(bg, global_rows, border + 1)
    kept = (border + 1) * global_rows - FINAL_GAIN_AT
    edge[:kept, :] = flat[FINAL_GAIN_AT : FINAL_GAIN_AT + kept, :]
    plan.spend(6.0)
    scatter_g.start(0)

    dx_s = norm_back(grad_summary, final_gain, unit_f, inv_f)

    out_s = dx_s.astype(LOW)
    for c in range(4):
        put(FC2_AT, c * D, D, dot_tn(act_s[:, c * D : (c + 1) * D], out_s))
    put_row(FC2_BIAS_AT, col_sum(out_s))
    gpre_s = (dot_nt(out_s, wfc2[1]) * steep_s).astype(LOW)
    put(FC1_AT, 0, FF, dot_tn(h2_s, gpre_s))
    put_row(FC1_BIAS_AT, col_sum(gpre_s))
    gh2_s = dot_nt(gpre_s, wfc1[1])
    put_row(MID_GAIN_AT, col_sum(gh2_s * unit_m))
    put_row(MID_BIAS_AT, col_sum(gh2_s))
    gmid_s = dx_s + norm_back(gh2_s, vec(1, 5), unit_m, inv_m)
    gmid_low = gmid_s.astype(LOW)
    put(PROJ_AT, 0, D, dot_tn(att_s, gmid_low))
    put_row(PROJ_BIAS_AT, col_sum(gmid_low))
    plan.spend(1.0)
    gatt6 = stack(dot_nt(gmid_low, wproj[1]).astype(LOW))
    gprob = dot_nt(gatt6, kv[:, D:])
    gscore = (p6 * (gprob - jnp.sum(p6 * gprob, axis=-1, keepdims=True))).astype(LOW)
    gq_s = (unstack(dot(gscore, kv[:, :D])) * SCORE_SCALE).astype(LOW)
    gkeys = (dot_tn(gscore, q6) * SCORE_SCALE).astype(LOW)
    gvalues = dot_tn(p6_low, gatt6).astype(LOW)
    put_row(QUERY_BIAS_AT, col_sum(gq_s))
    put_row(VALUE_BIAS_AT, col_sum(gvalues))
    kv[:, :D] = gkeys
    kv[:, D:] = gvalues
    plan.spend(2.2)
    put(QKV_AT, 0, 3 * D, dot_tn(h_s, gq_s))
    put(QKV_AT, 0, 3 * D, dot_tn(h_c[...], kv[:, :D]), 3)
    put(QKV_AT, 0, 3 * D, dot_tn(h_c[...], kv[:, D:]), 6)
    back_s = jnp.concatenate([dot_nt(gq_s, wqkv[1, :, :D]), gmid_s], axis=1)

    back_parts = jnp.concatenate(exact_parts(back_s), axis=0)
    dx = x1

    def kv_back(i, carry):
        gain_sum, bias_sum = carry
        r = tile_rows(i)
        image_col = seg_col[r, 0:1]
        place_col = pos_col[r, 0:1]
        lane = lax.broadcasted_iota(jnp.int32, (1, PICKED), 1).astype(FULL)
        lane_image = jnp.where(lane < IMAGES, lane, lane - IMAGES)
        lane_place = jnp.where(lane < IMAGES, float(TABLE), TABLE + 1.0)
        back_pick = (
            (image_col == lane_image) & (place_col == lane_place) & (lane < 2.0 * IMAGES)
        ).astype(LOW)
        back = dot(jnp.concatenate([back_pick] * 3, axis=1), back_parts)
        grad = back[:, :D] + dot_nt(kv[r, :], wqkv[1, :, D:])
        unit = unit_c[r, :]
        dx[r, :] = back[:, D:] + norm_back(grad, vec(1, 0), unit, inv_c[r, 0:1])
        return gain_sum + col_sum(grad * unit), bias_sum + col_sum(grad)

    zero_row = jnp.zeros((1, D), FULL)
    gain_sum, bias_sum = rolled(SEQ // ROWS, kv_back, (zero_row, zero_row), 0.4)
    put_row(PRE_GAIN_AT, gain_sum)
    put_row(PRE_BIAS_AT, bias_sum)
    flat[LAYER_END:, :] = jnp.zeros((LAYER_ALL - LAYER_END, LANES), FULL)
    gather_rows(b1, layer_rows)
    plan.spend(1.5)
    scatter_1.start(0)

    def feed_back(i, carry):
        fc1_sum, fc2_sum, proj_sum, gain_sum, bias_sum = carry
        r = tile_rows(i)
        grad_out = dx[r, :]
        out_low = grad_out.astype(LOW)
        low[r, :] = out_low
        for c in range(4):
            lanes = slice(c * D, (c + 1) * D)
            slope[r, lanes] = (dot_nt(out_low, wfc2[0, lanes, :]) * slope[r, lanes].astype(FULL)).astype(LOW)
        grad_h = dot_nt(slope[r, :], wfc1[0])
        unit = unit_b[r, :]
        middle = grad_out + norm_back(grad_h, vec(0, 5), unit, inv_b[r, 0:1])
        dx[r, :] = middle
        middle_low = middle.astype(LOW)
        h2low[r, :] = middle_low
        gatt[r, :] = dot_nt(middle_low, wproj[0]).astype(LOW)
        return (
            fc1_sum + col_sum(slope[r, :]), fc2_sum + col_sum(out_low), proj_sum + col_sum(middle_low),
            gain_sum + col_sum(grad_h * unit), bias_sum + col_sum(grad_h),
        )

    h2low = kv.at[:, 0:D]
    gatt = kv.at[:, D : 2 * D]
    sums = rolled(SEQ // ROWS, feed_back, (jnp.zeros((1, FF), FULL),) + (zero_row,) * 4, 2.3)
    for at, value in zip((FC1_BIAS_AT, FC2_BIAS_AT, PROJ_BIAS_AT, MID_GAIN_AT, MID_BIAS_AT), sums):
        put_row(at, value)


    def feed_weights(c, carry):
        lanes = pl.ds(pl.multiple_of(c * D, D), D)
        put(FC2_AT, c * D, D, dot_tn(act[:, lanes], low[...]))
        put(FC1_AT, 0, FF, dot_tn(h_b[...], slope[:, lanes]), 3 * c)
        return carry

    rolled(4, feed_weights, None, 0.5)
    put(PROJ_AT, 0, D, dot_tn(attl[...], h2low[...]))
    flat[LAYER_END:, :] = jnp.zeros((LAYER_ALL - LAYER_END, LANES), FULL)
    gather_rows(b0, layer_rows, first_early)
    plan.spend(1.6)
    scatter_0.start(0)

    def attend_back(j, carry):
        r = window_rows(j)
        mine, _ = window_masks(j, r)
        for g in range(HEADS // 2):
            lanes = slice(g * LANES, (g + 1) * LANES)
            key_lanes = slice(D + g * LANES, D + (g + 1) * LANES)
            value_lanes = slice(2 * D + g * LANES, 2 * D + (g + 1) * LANES)
            q2 = both(qkv[r, lanes])
            go2 = both(gatt[r, lanes])
            keys = qkv[r, key_lanes]
            p_low = probs[j, g]
            p = p_low.astype(FULL)
            gp = dot_nt(qkv[r, value_lanes], go2)
            gs = (p * (gp - jnp.sum(p * gp, axis=0, keepdims=True))).astype(LOW)
            keep_own(mine, qkv, r, lanes, merge(dot_tn(gs, keys)) * SCORE_SCALE)
            keep_own(mine, qkv, r, key_lanes, dot(gs, q2) * SCORE_SCALE)
            keep_own(mine, qkv, r, value_lanes, dot(p_low, go2))
        return carry

    loop(WINDOWS, attend_back, None, 0.7)

    def qkv_cast(i, carry):
        query_sum, value_sum = carry
        r = tile_rows(i)
        held = seg_col[r, 0:1] < float(IMAGES)
        grads = jnp.where(held, qkv[r, :].astype(FULL), 0.0)
        qkv[r, :] = grads.astype(LOW)
        return query_sum + col_sum(grads[:, :D]), value_sum + col_sum(grads[:, 2 * D :])

    query_sum, value_sum = rolled(SEQ // ROWS, qkv_cast, (zero_row, zero_row), 0.2)
    put_row(QUERY_BIAS_AT, query_sum)
    put_row(VALUE_BIAS_AT, value_sum)

    def qkv_weights(c, carry):
        put(QKV_AT, 0, 3 * D, dot_tn(h_a[...], qkv[:, pl.ds(pl.multiple_of(c * D, D), D)]), 3 * c)
        return carry

    lax.fori_loop(0, 3, qkv_weights, 0)
    gather_rows(b0, layer_rows, 0, first_early)
    plan.spend(1.2)
    scatter_0.start(1)

    def qkv_back(i, carry):
        gain_sum, bias_sum, embed_sum = carry
        r = tile_rows(i)
        grad = dot_nt(qkv[r, :], wqkv[0])
        unit = unit_a[r, :]
        full = dx[r, :] + norm_back(grad, vec(0, 0), unit, inv_a[r, 0:1])
        dx[r, :] = full
        place = pos_col[r, 0:1]
        pixel = jnp.where(place < TABLE, full, 0.0).astype(LOW)
        low[r, :] = pixel
        return gain_sum + col_sum(grad * unit), bias_sum + col_sum(grad), embed_sum + col_sum(pixel)

    gain_sum, bias_sum, embed_sum = rolled(SEQ // ROWS, qkv_back, (zero_row,) * 3, 1.0)
    put_row(PRE_GAIN_AT, gain_sum)
    put_row(PRE_BIAS_AT, bias_sum)
    gather_rows(b0, layer_rows, *vector_blocks)
    plan.spend(0.1)
    scatter_0.start(2)

    for c in range(2):
        put(PATCH_AT, c * D, D, dot_tn(pat[:, c * D : (c + 1) * D], low[...]))
    place_col = pos_col[:, 0:1]
    onehot = onehot_of(place_col)
    high = dx[...].astype(LOW)
    rest = (dx[...] - high.astype(FULL)).astype(LOW)
    table = dot_tn(onehot, high) + dot_tn(onehot, rest)
    put(POS_AT, 0, D, table[: TABLE + 2])
    put_row(PATCH_BIAS_AT, embed_sum)
    flat[FINAL_GAIN_AT : FINAL_GAIN_AT + kept, :] = edge[:kept, :]
    gather_rows(bg, global_rows, 0, border + 1)
    plan.spend(1.5)
    scatter_g.start(1)
    plan.until()

    squares = jnp.zeros((1, 1), FULL)
    for ref in (new_l, new_g):
        used = ref[...]
        squares += jnp.sum(jnp.sum(used * used, axis=0, keepdims=True), axis=1, keepdims=True)
    row = lax.broadcasted_iota(jnp.int32, (8, LANES), 0)
    tile = jnp.where(row == 0, squares, loss_sum)
    shared[...] = add_over_slice(place, tile, tiles, tile_send, tile_recv)
    for scatter in scatters:
        scatter.drain()


def padded(rows):
    return rows + -rows % 16


def step_call(place, loss_scale, pat, pos, seg, lab, tea, lm, gm):
    vmem = pl.BlockSpec(memory_space=pltpu.VMEM)
    smem = pl.BlockSpec(memory_space=pltpu.SMEM)
    n, nz = place.n, place.nz
    rows = padded(lm.shape[0] // 2), padded(lm.shape[0] // 2), padded(gm.shape[0])

    def shape(*dims, kind=FULL):
        return pltpu.VMEM(dims, kind)

    def low(*dims):
        return pltpu.VMEM(dims, LOW)

    scratch = [low(n, 2, nz, n, r, LANES) for r in rows]
    for r in rows:
        scratch += [
            low(n, nz, n, r, LANES), low(n - 1, n, nz, r, LANES), low(n - 1, nz, r, LANES), low(nz - 1, r, LANES)
        ]
    tiles = 2 * nz + n * n
    scratch += [
        shape(LAYER_ALL, LANES), shape(gm.shape[0] + 8, LANES), shape(rows[0], LANES), low(D, GROUP * LANES),
        low(2, D, 3 * D), low(2, D, D), low(2, D, FF), low(2, FF, D),
        low(PATCH, D), low(256, D), low(GROUPS, (GROUP_ROWS + 1) * LANES),
        shape(2, 16, FF),
        shape(SEQ, LANES), shape(SEQ, LANES),
        shape(SEQ, D), shape(SEQ, LANES), low(SEQ, D),
        shape(SEQ, D), shape(SEQ, LANES), low(SEQ, D),
        low(SEQ, 3 * D), low(WINDOWS, HEADS // 2, WINDOW, 2 * WINDOW),
        low(SEQ, D), shape(SEQ, D), shape(SEQ, D),
        low(SEQ, FF), low(SEQ, FF), low(SEQ, 2 * D), low(SEQ, D), shape(SEQ, LANES),
        low(SEQ, PATCH), pltpu.SemaphoreType.DMA, shape(tiles, 8, LANES),
        pltpu.SemaphoreType.DMA((6,)),
        pltpu.SemaphoreType.DMA((3, nz + nz * n + 2 * n)), pltpu.SemaphoreType.DMA((3, 2 * n * n * nz + n * nz + nz)),
        pltpu.SemaphoreType.DMA((2,)), pltpu.SemaphoreType.DMA((2,)),
    ]
    return pl.pallas_call(
        functools.partial(step_kernel, place, loss_scale),
        out_shape=[jax.ShapeDtypeStruct(a, FULL) for a in (lm.shape, gm.shape, (8, LANES))],
        in_specs=[pl.BlockSpec(memory_space=pl.ANY)] + [vmem] * 2 + [smem] * 2 + [vmem] * 2,
        out_specs=[vmem] * 3,
        scratch_shapes=scratch,
        compiler_params=pltpu.CompilerParams(collective_id=0, has_side_effects=True, vmem_limit_bytes=VMEM_BYTES),
    )(pat, pos, seg, lab, tea, lm, gm)

def adam_kernel(total, gl, gg, lm, lo, ls, gm, go, gs, *outs):
    norm = jnp.sqrt(total[0:1, 0:1])
    factor = jnp.minimum(1.0, CLIP_NORM / norm)
    fix_one = 1.0 - BETA_ONE**STEP
    fix_two = 1.0 - BETA_TWO**STEP
    for at, (grad, master, moment, second) in ((0, (gl, lm, lo, ls)), (3, (gg, gm, go, gs))):
        clipped = grad[...] * factor
        new_moment = BETA_ONE * moment[...] + (1.0 - BETA_ONE) * clipped
        new_second = BETA_TWO * second[...] + (1.0 - BETA_TWO) * clipped * clipped
        old = master[...]
        update = new_moment / fix_one / (jnp.sqrt(new_second / fix_two) + ADAM_EPS) + WEIGHT_DECAY * old
        outs[at][...] = old - LEARN_RATE * update
        outs[at + 1][...] = new_moment
        outs[at + 2][...] = new_second
    outs[6][0, 0] = norm[0, 0]
    outs[7][0, 0] = total[1, 0]


def interleave(x):
    rows = x.shape[1] // LANES
    return x.reshape(2, rows, LANES).transpose(1, 0, 2).reshape(2 * rows, LANES)


def layers_apart(x):
    rows = x.shape[0] // 2
    return x.reshape(rows, 2, LANES).transpose(1, 0, 2).reshape(2, rows * LANES)


def shards(sizes, pat, pos, seg, lab, tea, lm, lo, ls, gm, go, gs):
    place = Place(sizes)
    count = sizes[0] * sizes[1]
    assert pat.shape[0] == 1 and lm.shape[1] * count == LAYER_ALL * LANES and gm.shape[0] * count == GLOBAL_ALL * LANES
    lm, lo, ls = interleave(lm), interleave(lo), interleave(ls)
    gm, go, gs = gm.reshape(-1, LANES), go.reshape(-1, LANES), gs.reshape(-1, LANES)
    gl, gg, total = step_call(place, 1.0 / (2 * IMAGES * count), pat[0], pos, seg, lab, tea, lm, gm)
    vmem, smem = pl.BlockSpec(memory_space=pltpu.VMEM), pl.BlockSpec(memory_space=pltpu.SMEM)
    shapes = [lm.shape] * 3 + [gm.shape] * 3 + [(1, 1)] * 2
    *new, norm, loss = pl.pallas_call(
        adam_kernel,
        out_shape=[jax.ShapeDtypeStruct(x, FULL) for x in shapes],
        out_specs=[vmem] * 6 + [smem] * 2,
        compiler_params=pltpu.CompilerParams(vmem_limit_bytes=VMEM_BYTES),
    )(total, gl, gg, lm, lo, ls, gm, go, gs)
    return tuple(layers_apart(x) for x in new[:3]) + tuple(x.reshape(-1) for x in new[3:]) + (norm.reshape(()), loss.reshape(()))


def solution(mesh):
    axes = tuple(mesh.axis_names)
    split = P(axes)
    wide = P(None, axes)
    return jax.shard_map(
        functools.partial(shards, tuple(mesh.shape[a] for a in axes)),
        mesh=mesh,
        in_specs=(split,) * 5 + (wide,) * 3 + (split,) * 3,
        out_specs=(wide,) * 3 + (split,) * 3 + (P(), P()),
        check_vma=False,
    )
```

```python
import functools

import jax
import jax.numpy as jnp
from jax import lax
from jax.experimental import pallas as pl
from jax.experimental.pallas import tpu as pltpu
from jax.sharding import PartitionSpec as P

D = 384
HEADS = 6
HEAD_DIM = 64
FF = 1536
CLASSES = 1000
PATCH = 768
TABLE = 196
IMAGES = 15
SEQ = 768
STEP = 10
LANES = 128

NORM_EPS = 1e-06
BETA_ONE = 0.9
BETA_TWO = 0.999
ADAM_EPS = 1e-08
LEARN_RATE = 0.1
WEIGHT_DECAY = 0.05
CLIP_NORM = 0.01
MASK_FILL = -1000000000.0
SCORE_SCALE = HEAD_DIM ** (-0.5)
LOW = jnp.bfloat16
FULL = jnp.float32
HIGHEST = lax.Precision.HIGHEST

QKV_AT, PROJ_AT, FC1_AT, FC2_AT = 0, 3456, 4608, 9216
PRE_GAIN_AT, PRE_BIAS_AT, QUERY_BIAS_AT, VALUE_BIAS_AT = 13824, 13827, 13830, 13833
PROJ_BIAS_AT, MID_GAIN_AT, MID_BIAS_AT, FC1_BIAS_AT, FC2_BIAS_AT = 13836, 13839, 13842, 13845, 13857
LAYER_END = 13860
PATCH_AT, POS_AT, PATCH_BIAS_AT, FINAL_GAIN_AT, FINAL_BIAS_AT = 0, 2304, 2898, 2901, 2904
HEAD_AT, HEAD_BIAS_AT, GLOBAL_END = 2907, 8907, 8923
GROUP, GROUP_ROWS, GROUPS = 8, 125, 48
HEAD_LANES = 2048
PICKED = 32
WINDOWS, WINDOW = 8, 128
ROWS = 384
LAYER_ALL, GLOBAL_ALL = 14080, 8960
VMEM_BYTES = 64 * 1024 * 1024 - 64 * 1024
MESH = pl.DeviceIdType.MESH


def dot(a, b, dims=(1, 0), precision=None):
    return lax.dot_general(
        a, b, (((dims[0],), (dims[1],)), ((), ())), precision=precision, preferred_element_type=FULL
    )


def dot_nt(a, b, precision=None):
    return dot(a, b, (1, 1), precision)


def dot_tn(a, b, precision=None):
    return dot(a, b, (0, 0), precision)


def row_mean(x):
    return jnp.sum(x, axis=-1, keepdims=True) * (1.0 / D)


def normalise(x):
    center = x - row_mean(x)
    inverse = lax.rsqrt(row_mean(center * center) + NORM_EPS)
    return center * inverse, inverse


def norm_back(grad, gain, unit, inverse):
    scaled = grad * gain
    return inverse * (scaled - row_mean(scaled) - unit * row_mean(scaled * unit))


def col_sum(x):
    return jnp.sum(x.astype(FULL), axis=0, keepdims=True)


def gelu_parts(x):
    bell = jnp.exp2(x * x * (-0.5 * 1.4426950408889634))
    base = 1.0 + (0.3275911 * 0.7071067811865476) * jnp.abs(x)
    t = pl.reciprocal(base, approx=True)
    t = t * (2.0 - base * t)
    tail = (((0.5307027145 * t - 0.7265760135) * t + 0.7107068705) * t - 0.142248368) * t + 0.127414796
    tail = tail * t * bell
    phi = jnp.where(x < 0, tail, 1.0 - tail)
    return x * phi, phi + x * bell * 0.3989422804014327


def exact_parts(x):
    high = x.astype(LOW)
    rest = x - high.astype(FULL)
    middle = rest.astype(LOW)
    return high, middle, (rest - middle.astype(FULL)).astype(LOW)


def wrap(value, size):
    return jnp.where(value >= size, value - size, value)


class Place:
    def __init__(self, sizes):
        dp, fsdp = sizes
        self.n = self.ny = self.nx = dp // 2
        self.nz = fsdp // self.nx
        assert dp == 2 * self.n and fsdp == self.n * self.nz

    def locate(self):
        dp, fsdp = lax.axis_index("dp"), lax.axis_index("fsdp")
        self.y, self.core = dp // 2, dp % 2
        self.z, self.x = fsdp // self.nx, fsdp % self.nx
        self.even = self.core == 0
        self.zs = [wrap(self.z + k, self.nz) for k in range(self.nz)]
        self.ys = [wrap(self.y + k, self.n) for k in range(self.n)]
        self.xs = [wrap(self.x + k, self.n) for k in range(self.n)]
        spans = [(p, q) for p in range(self.n) for q in range(self.n)]
        self.short = {
            (p, q): (jnp.where(self.even, self.ys[p], self.ys[q]), jnp.where(self.even, self.xs[q], self.xs[p]))
            for p, q in spans
        }

    def yx(self, p, q):
        return self.short[p, q]

    def block(self, dz, p, q):
        y, x = self.yx(p, q)
        return y, self.core, self.zs[dz], x

    def device(self, y, core, z, x):
        return y * 2 + core, z * self.nx + x

    def yx_other(self, p, q):
        return jnp.where(self.even, self.ys[q], self.ys[p]), jnp.where(self.even, self.xs[p], self.xs[q])

    def index(self, y, core, z, x):
        return ((y * 2 + core) * self.nz + z) * self.nx + x

    def meet(self):
        def there(y=0, core=0, z=0, x=0):
            return self.device(self.ys[y], 1 - self.core if core else self.core, self.zs[z], self.xs[x])

        self.other = there(core=1)
        self.zp = [there(z=k) for k in range(self.nz)]
        self.pp = [self.device(*self.block(0, k, 0)) for k in range(self.n)]
        self.qp = [self.device(*self.block(0, 0, k)) for k in range(self.n)]
        self.tall = [there(core=c, z=k) for c in range(2) for k in range(self.nz)][1:]
        self.flat = [there(y=j, x=k) for j in range(self.n) for k in range(self.n)][1:]
        barrier = pltpu.get_barrier_semaphore()
        for peer in self.tall + self.flat:
            pl.semaphore_signal(barrier, inc=1, device_id=peer, device_id_type=MESH)
        pl.semaphore_wait(barrier, len(self.tall + self.flat))


def push(src, dst, send, recv, peer):
    pltpu.make_async_remote_copy(
        src_ref=src, dst_ref=dst, send_sem=send, recv_sem=recv, device_id=peer, device_id_type=MESH
    ).start()


def landed(dst, recv):
    pltpu.make_async_copy(dst, dst, recv).wait()


class Plan:
    HOP = 2.0
    RATES = (88e3, 66e3, 600e3)

    def __init__(self):
        self.now, self.free, self.came, self.steps = 0.0, [0.0] * 3, {}, []

    def sent(self, key, way, size):
        begin = max(self.now, self.free[way])
        self.free[way] = begin + size / self.RATES[way]
        self.came[key] = max(self.came.get(key, 0.0), self.free[way] + self.HOP)

    def add(self, needs, run, name=None):
        self.steps.append((needs, run, name))

    def ready(self, step):
        return max((self.came.get(key, 1e9) for key in step[0]), default=0.0)

    def run(self, step):
        self.steps.remove(step)
        self.now = max(self.now, self.ready(step)) + 0.03
        step[1]()

    def spend(self, time):
        self.now += time
        while True:
            step = min((step for step in self.steps if self.ready(step) <= self.now), key=self.ready, default=None)
            if step is None:
                return
            self.run(step)

    def due(self, time):
        return any(self.ready(step) <= self.now + time for step in self.steps)

    def until(self, name=None):
        while self.steps and (name is None or any(step[2] == name for step in self.steps)):
            self.run(min(self.steps, key=self.ready))


class Gather:
    def __init__(self, place, plan, name, buf, send, recv):
        self.place, self.plan, self.name, self.buf, self.send, self.recv = place, plan, name, buf, send, recv
        self.from_p = place.nz
        self.from_q = self.from_p + place.nz * place.n
        self.from_core = self.from_q + place.n
        self.size = 2 * buf.shape[4] * LANES

    def sent(self, way, count, *key):
        self.plan.sent((self.name,) + key, way, count * self.size)

    def to_p(self, dz):
        a, t = self.place, self.buf.at[self.place.block(dz, 0, 0)]
        for k in range(1, a.n):
            push(t, t, self.send, self.recv.at[self.from_p + dz * a.n + a.n - k], a.pp[k])
            self.sent(0, 1, 1, dz, a.n - k)

    def to_q(self, dz, p):
        a, t = self.place, self.buf.at[self.place.block(dz, p, 0)]
        for k in range(1, a.n):
            push(t, t, self.send, self.recv.at[self.from_q + a.n - k], a.qp[k])
            self.sent(0, 1, 2, dz, p)

    def start(self):
        a, t = self.place, self.buf.at[self.place.block(0, 0, 0)]
        self.to_p(0)
        for k in range(1, a.nz):
            push(t, t, self.send, self.recv.at[a.nz - k], a.zp[k])
            self.sent(1, 1, 0, a.nz - k)
        self.to_q(0, 0)
        far = range(1, a.n)
        near = sorted(range(1, a.nz), key=lambda k: min(k, a.nz - k))
        add = self.plan.add
        for p in far:
            add([(self.name, 1, 0, p)], lambda p=p: self.p_came(0, p))
        for k in near:
            add([(self.name, 0, k)], lambda k=k: self.z_came(k))
        for k in near:
            for p in far:
                add([(self.name, 1, k, p)], lambda k=k, p=p: self.p_came(k, p))
        mine = [(self.name, 0, k) for k in near] + [(self.name, 1, k, p) for k in range(a.nz) for p in far]
        add(mine, lambda: self.to_core(0))
        for q in far:
            add([(self.name, 2, k, p) for k in range(a.nz) for p in range(a.n)], lambda q=q: self.q_came(q))
        add([(self.name, 3, q) for q in range(a.n)], self.finish, self.name)

    def z_came(self, dz):
        landed(self.buf.at[self.place.block(dz, 0, 0)], self.recv.at[dz])
        self.to_p(dz)
        self.to_q(dz, 0)

    def p_came(self, dz, p):
        landed(self.buf.at[self.place.block(dz, p, 0)], self.recv.at[self.from_p + dz * self.place.n + p])
        self.to_q(dz, p)

    def group(self, core, q):
        a = self.place
        return self.buf.at[:, 0, :, a.xs[q]] if core == 0 else self.buf.at[a.ys[q], 1]

    def to_core(self, q):
        a = self.place
        for core in range(2):

            @pl.when(a.core == core)
            def _():
                t = self.group(core, q)
                push(t, t, self.send, self.recv.at[self.from_core + q], a.other)

        self.sent(2, a.n * a.nz, 3, q)

    def q_came(self, q):
        landed(self.buf.at[:, 0, :, 0], self.recv.at[self.from_q + q])
        self.to_core(q)

    def finish(self):
        for q in range(self.place.n):
            landed(self.buf.at[:, 0, :, 0], self.recv.at[self.from_core + q])

    def drain(self):
        a = self.place
        for t in (self.buf.at[:, 0], self.buf.at[:, 0, :, pl.ds(0, a.n - 1)], self.buf.at[0, 0, :, pl.ds(0, a.n - 1)]):
            landed(t, self.send)
        landed(self.buf.at[0, 0, pl.ds(0, a.nz - 1), 0], self.send)


class Scatter:
    def __init__(self, place, plan, buf, from_core, from_q, from_p, from_z, out, send, recv, shares, turn_of):
        self.place, self.plan, self.buf, self.out, self.send, self.recv = place, plan, buf, out, send, recv
        self.core_buf, self.q_buf, self.p_buf, self.z_buf = from_core, from_q, from_p, from_z
        self.shares, self.turn_of = shares, turn_of
        n, nz = place.n, place.nz
        self.at_q = n * n * nz
        self.at_p = self.at_q + n * n * nz
        self.at_z = self.at_p + n * nz
        self.past = []
        self.far = tuple(range(1, n))
        self.order = sorted(range(1, nz), key=lambda k: -min(k, nz - k)) + [0]
        self.size = 2 * buf.shape[4] * LANES

    def when(self, turn, block, body):
        pl.when(self.turn_of(self.place.index(*block)) == turn)(body)

    def send_on(self, turn, block, src, dst, recv, peer):
        push(src, dst, self.send, recv, peer)
        self.past.append((turn, block, src))

    def sent(self, turn, way, *key):
        self.plan.sent((id(self), turn) + key, way, self.size * self.shares[turn])

    def block(self, p, q, k):
        y, x = self.place.yx(p, q)
        return y, self.place.core, self.place.zs[k], x

    def start(self, turn):
        a, name = self.place, (id(self), turn)
        for k in self.order:
            for q in self.far + (0,):
                for p in self.far + (0,):
                    y, x = a.yx_other(p, q)
                    z = a.zs[k]
                    block = y, 1 - a.core, z, x
                    recv = self.recv.at[(q * a.n + p) * a.nz + k]
                    self.when(turn, block, lambda: self.send_on(
                        turn, block, self.buf.at[block], self.core_buf.at[y, z, x], recv, a.other))
                    self.sent(turn, 2, 0, p, q, k)
        add = self.plan.add
        for k in self.order:
            for q in self.far:
                for p in self.far + (0,):
                    add([name + (0, p, q, k)], lambda p=p, q=q, k=k: self.to_q(turn, p, q, k))

            def needs(p):
                return [name + (0, p, 0, k)] + [name + (1, p, q, k) for q in self.far]

            for p in self.far:
                add(needs(p), lambda p=p, k=k: self.to_p(turn, p, k))
            here = needs(0) + [name + (2, p, k) for p in self.far]
            if k:
                add(here, lambda k=k: self.to_z(turn, k))
            else:
                add(here + [name + (3, j) for j in range(1, a.nz)], lambda: self.own(turn))

    def add(self, p, q, k, extra, out=None):
        a = self.place
        y, core, z, x = self.block(p, q, k)
        mine, theirs = self.buf.at[y, core, z, x], self.core_buf.at[y, z, x]
        landed(theirs, self.recv.at[(q * a.n + p) * a.nz + k])
        refs = [mine, theirs] + extra
        if out is None:
            add_up(refs, mine)
        else:
            out(refs)
        return mine

    def to_q(self, turn, p, q, k):
        a = self.place
        block = self.block(p, q, k)

        def body():
            mine = self.add(p, q, k, [])
            recv = self.recv.at[self.at_q + ((a.n - q) * a.n + p) * a.nz + k]
            self.send_on(turn, block, mine, self.q_buf.at[a.n - q - 1, p, a.zs[k]], recv, a.qp[q])

        self.when(turn, block, body)
        self.sent(turn, 0, 1, p, a.n - q, k)

    def q_came(self, p, k):
        a = self.place
        refs = [self.q_buf.at[q - 1, p, a.zs[k]] for q in self.far]
        for q, ref in zip(self.far, refs):
            landed(ref, self.recv.at[self.at_q + (q * a.n + p) * a.nz + k])
        return refs

    def to_p(self, turn, p, k):
        a = self.place
        block = self.block(p, 0, k)

        def body():
            mine = self.add(p, 0, k, self.q_came(p, k))
            recv = self.recv.at[self.at_p + (a.n - p) * a.nz + k]
            self.send_on(turn, block, mine, self.p_buf.at[a.n - p - 1, a.zs[k]], recv, a.pp[p])

        self.when(turn, block, body)
        self.sent(turn, 0, 2, a.n - p, k)

    def p_came(self, k):
        a = self.place
        refs = [self.p_buf.at[p - 1, a.zs[k]] for p in self.far]
        for p, ref in zip(self.far, refs):
            landed(ref, self.recv.at[self.at_p + p * a.nz + k])
        return refs

    def to_z(self, turn, k):
        a = self.place
        block = self.block(0, 0, k)

        def body():
            mine = self.add(0, 0, k, self.q_came(0, k) + self.p_came(k))
            recv = self.recv.at[self.at_z + a.nz - k]
            self.send_on(turn, block, mine, self.z_buf.at[a.nz - k - 1], recv, a.zp[k])

        self.when(turn, block, body)
        self.sent(turn, 1, 3, a.nz - k)

    def own(self, turn):
        a = self.place

        def body():
            extra = self.q_came(0, 0) + self.p_came(0)
            for k in range(1, a.nz):
                landed(self.z_buf.at[k - 1], self.recv.at[self.at_z + k])
            self.add(0, 0, 0, extra + [self.z_buf.at[k] for k in range(a.nz - 1)], self.out)

        self.when(turn, self.block(0, 0, 0), body)

    def drain(self):
        for turn, block, src in self.past:
            self.when(turn, block, lambda: landed(src, self.send))


def sum_rows(refs, r):
    value = refs[0][r, :].astype(FULL)
    for ref in refs[1:]:
        value += ref[r, :].astype(FULL)
    return value


def add_up(refs, dst):
    rows = dst.shape[0]
    step = next(v for v in (224, 144, 64, 48, 32, 16) if rows % v == 0)

    def one(t, carry):
        r = pl.ds(pl.multiple_of(t * step, step), step)
        dst[r, :] = sum_rows(refs, r).astype(LOW)
        return carry

    lax.fori_loop(0, rows // step, one, 0)


def add_over_slice(place, tile, tiles, send, recv):
    base = 0
    for turn, (peers, own) in enumerate((
        (place.tall, place.core * place.nz + place.z), (place.flat, place.y * place.n + place.x)
    )):
        mine = tiles.at[base + own]
        mine[...] = tile
        for peer in peers:
            push(mine, mine, send.at[turn], recv.at[turn], peer)
        landed(tiles.at[pl.ds(base, len(peers))], recv.at[turn])
        tile = tiles[base]
        for k in range(1, len(peers) + 1):
            tile += tiles[base + k]
        landed(tiles.at[pl.ds(base, len(peers))], send.at[turn])
        base += len(peers) + 1
    return tile


def step_kernel(
    place, loss_scale,
    pat_hbm, pos, seg, lab, tea, lm, gm,
    new_l, new_g, shared,
    b0, b1, bg, r0c, r0q, r0p, r0z, r1c, r1q, r1p, r1z, rgc, rgq, rgp, rgz, flat, edge, stage, arrange,
    wqkv, wproj, wfc1, wfc2, wpat, wpos, whead, vecs,
    pos_col, seg_col, unit_a, inv_a, h_a, unit_b, inv_b, h_b, qkv, probs, attl, x0, x1, slope, act, kv, low, inv_c,
    pat, pat_sem, tiles, sends, gather_recv, scatter_recv, tile_send, tile_recv,
):
    layer_rows, global_rows = lm.shape[0] // 2, gm.shape[0]
    place.locate()
    me = place.block(0, 0, 0)
    pat_load = pltpu.make_async_copy(pat_hbm, pat, pat_sem)
    pat_load.start()
    bg[me + (pl.ds(0, global_rows),)] = gm[...].astype(LOW)
    b0[me + (pl.ds(0, layer_rows),)] = lm[pl.ds(0, layer_rows, stride=2), :].astype(LOW)
    b1[me + (pl.ds(0, layer_rows),)] = lm[pl.ds(1, layer_rows, stride=2), :].astype(LOW)
    place.meet()
    plan = Plan()
    gathers = [
        Gather(place, plan, i, buf, sends.at[i], gather_recv.at[i]) for i, buf in enumerate((bg, b0, b1))
    ]
    gathers[0].start()
    gathers[1].start()

    def split_rows(rows):
        half = rows // 32 * 16
        return [pl.ds(at, count) for at, count in ((0, half), (half, rows - half)) if count]

    def finish_layer(n):
        def out(refs):
            for r in split_rows(layer_rows):
                new_l[pl.ds(2 * r.start + n, r.size, stride=2), :] = sum_rows(refs, r)

        return out

    def finish_global(refs):
        for r in split_rows(global_rows):
            new_g[r, :] = sum_rows(refs, r)

    def layer_turn(s):
        first, last = PRE_GAIN_AT // layer_rows, (PROJ_BIAS_AT - 1) // layer_rows
        late = (s < -(-PROJ_AT // layer_rows)).astype(jnp.int32)
        return jnp.where((s >= first) & (s <= last), 2, late)

    def global_turn(s):
        return (s < -(-FINAL_GAIN_AT // global_rows)).astype(jnp.int32)

    scatter_g = Scatter(place, plan, bg, rgc, rgq, rgp, rgz, finish_global, sends.at[5], scatter_recv.at[2],
                        (0.65, 0.4), global_turn)
    scatter_0 = Scatter(place, plan, b0, r0c, r0q, r0p, r0z, finish_layer(0), sends.at[4], scatter_recv.at[1],
                        (0.75, 0.35, 0.03), layer_turn)
    scatter_1 = Scatter(place, plan, b1, r1c, r1q, r1p, r1z, finish_layer(1), sends.at[3], scatter_recv.at[0],
                        (1.0,), lambda s: 0 * s)
    scatters = [scatter_g, scatter_0, scatter_1]
    first_early = -(-PROJ_AT // layer_rows)
    vector_blocks = PRE_GAIN_AT // layer_rows, (PROJ_BIAS_AT - 1) // layer_rows + 1

    head_of_lane = lax.broadcasted_iota(jnp.int32, (1, LANES), 1) // HEAD_DIM

    def loop(count, body, carry=None, time=0.0):
        for i in range(count):
            carry = body(i, carry)
            plan.spend(time)
        return carry

    def rolled(count, body, carry=None, time=0.0):
        traced = []

        def one(i, carry):
            assert not traced
            traced.append(i)
            carry = body(i, carry)
            for k in range(count):
                if plan.due(time):
                    pl.when(i == k)(lambda: plan.spend(time))
                else:
                    plan.spend(time)
            return carry

        return lax.fori_loop(0, count, one, 0 if carry is None else carry)

    def each_block(low_end, high_end, one):
        def body(s, carry):
            x = lax.rem(s, place.nx)
            rest = lax.div(s, place.nx)
            z, rest = lax.rem(rest, place.nz), lax.div(rest, place.nz)
            one(s, (lax.div(rest, 2), lax.rem(rest, 2), z, x))
            return carry

        lax.fori_loop(low_end, high_end, body, 0)

    def spread(buf, rows, low_end=0, high_end=2 * place.n * place.n * place.nz):
        def one(s, t):
            if rows % 8 == 0:
                flat[pl.ds(pl.multiple_of(s * rows, 8), rows), :] = buf[t + (pl.ds(0, rows),)].astype(FULL)
            else:
                stage[: buf.shape[4], :] = buf[t].astype(FULL)

                def row(i, carry):
                    flat[pl.ds(s * rows + i, 1), :] = stage[pl.ds(i, 1), :]
                    return carry

                lax.fori_loop(0, rows, row, 0)

        each_block(low_end, high_end, one)

    def gather_rows(buf, rows, low_end=0, high_end=2 * place.n * place.n * place.nz):
        def one(s, t):
            if rows % 8 == 0:
                buf[t + (pl.ds(0, rows),)] = flat[pl.ds(pl.multiple_of(s * rows, 8), rows), :].astype(LOW)
            else:

                def row(i, carry):
                    stage[pl.ds(i, 1), :] = flat[pl.ds(s * rows + i, 1), :]
                    return carry

                lax.fori_loop(0, rows, row, 0)
                buf[t] = stage[: buf.shape[4], :].astype(LOW)

        each_block(low_end, high_end, one)

    def take(dst, at, rows, width):
        count = width // LANES

        def one(c, carry):
            value = flat[pl.ds(at + c, rows, stride=count), :].astype(LOW)
            dst[:rows, pl.ds(pl.multiple_of(c * LANES, LANES), LANES)] = value
            return carry

        lax.fori_loop(0, count, one, 0)

    def take_row(at, width):
        return jnp.concatenate([flat[at + i : at + i + 1, :] for i in range(width // LANES)], axis=1)

    def put_row(at, value):
        for i in range(value.shape[1] // LANES):
            flat[at + i : at + i + 1, :] = value[:, i * LANES : (i + 1) * LANES]

    def put(at, start, width, value, first=0):
        count = width // LANES
        rows = value.shape[0]
        for i in range(value.shape[1] // LANES):
            flat[pl.ds(at + start * count + first + i, rows, stride=count), :] = value[:, i * LANES : (i + 1) * LANES]

    for i in range(SEQ // LANES):
        lanes = slice(i * LANES, (i + 1) * LANES)
        for src, dst in ((pos, pos_col), (seg, seg_col)):
            dst[lanes, :] = jnp.transpose(jnp.broadcast_to(src[0:1, lanes].astype(FULL), (LANES, LANES)))
    pos_row = pos[0:1, :]
    seg_row = seg[0:1, :]
    picked_row = lax.broadcasted_iota(jnp.int32, (PICKED, 1), 0)
    picked_image = jnp.where(picked_row < IMAGES, picked_row, picked_row - IMAGES)
    picked_image = jnp.where(picked_row < 2 * IMAGES, picked_image, -1)
    picked_place = jnp.where(picked_row < IMAGES, TABLE, TABLE + 1)
    picker = ((seg_row == picked_image) & (pos_row == picked_place)).astype(FULL)
    picker_low = picker.astype(LOW)

    arr_row = lax.broadcasted_iota(jnp.int32, (D, GROUP * LANES), 0)
    arr_lane = lax.broadcasted_iota(jnp.int32, (D, GROUP * LANES), 1)
    arrange[...] = (
        (arr_row == (arr_lane % LANES) * GROUP + arr_lane // LANES) & (arr_lane % LANES < GROUPS)
    ).astype(FULL).astype(LOW)

    plan.spend(1.0)
    plan.until(0)
    gathers[2].start()
    spread(bg, global_rows)
    plan.spend(1.2)
    take(wpat, PATCH_AT, PATCH, D)
    take(wpos, POS_AT, TABLE + 2, D)
    wpos[TABLE + 2 :, :] = jnp.zeros((wpos.shape[0] - TABLE - 2, D), LOW)

    def take_head(j, carry):
        value = flat[pl.ds(HEAD_AT + j, GROUPS, stride=GROUP_ROWS), :].astype(LOW)
        whead[:, pl.ds(pl.multiple_of(j * LANES, LANES), LANES)] = value
        return carry

    lax.fori_loop(0, GROUP_ROWS, take_head, 0)
    whead[:, GROUP_ROWS * LANES :] = jnp.zeros((GROUPS, LANES), LOW)
    patch_bias = take_row(PATCH_BIAS_AT, D)
    final_gain = take_row(FINAL_GAIN_AT, D)
    final_bias = take_row(FINAL_BIAS_AT, D)
    head_bias = take_row(HEAD_BIAS_AT, HEAD_LANES)

    row_at = (
        (PRE_GAIN_AT, D), (PRE_BIAS_AT, D), (QUERY_BIAS_AT, D), (VALUE_BIAS_AT, D), (PROJ_BIAS_AT, D),
        (MID_GAIN_AT, D), (MID_BIAS_AT, D), (FC1_BIAS_AT, FF), (FC2_BIAS_AT, D),
    )

    def take_layer(n, buf):
        spread(buf, layer_rows)
        take(wqkv.at[n], QKV_AT, D, 3 * D)
        take(wproj.at[n], PROJ_AT, D, D)
        take(wfc1.at[n], FC1_AT, D, FF)
        take(wfc2.at[n], FC2_AT, FF, D)
        for i, (at, width) in enumerate(row_at):
            vecs[n, i : i + 1, :width] = take_row(at, width)

    def vec(n, i):
        return vecs[n, i : i + 1, : row_at[i][1]]

    plan.spend(2.0)

    def tile_rows(i):
        return pl.ds(pl.multiple_of(i * ROWS, ROWS), ROWS)

    def onehot_of(place):
        iota = lax.broadcasted_iota(jnp.int32, (1, wpos.shape[0]), 1).astype(FULL)
        return (place == iota).astype(LOW)

    def embed(i, carry):
        r = tile_rows(i)
        place = pos_col[r, 0:1]
        pixel = dot(pat[r, :], wpat[...]) + patch_bias
        stream = dot(onehot_of(place), wpos[...]) + jnp.where(place < TABLE, pixel, 0.0)
        x0[r, :] = stream
        unit, inverse = normalise(stream)
        unit_a[r, :] = unit
        inv_a[r, :] = jnp.broadcast_to(inverse, (ROWS, LANES))
        return carry

    pat_load.wait()
    rolled(SEQ // ROWS, embed, None, 0.9)
    plan.until(1)
    take_layer(0, b0)
    plan.spend(1.8)
    qkv_bias = jnp.concatenate([vec(0, 2), jnp.zeros((1, D), FULL), vec(0, 3)], axis=1)

    def project(i, carry):
        r = tile_rows(i)
        h = (unit_a[r, :] * vec(0, 0) + vec(0, 1)).astype(LOW)
        h_a[r, :] = h
        qkv[r, :] = (dot(h, wqkv[0]) + qkv_bias).astype(LOW)
        return carry

    rolled(SEQ // ROWS, project, None, 0.6)

    def window_rows(j):
        return pl.ds(min(102 * j // 16 * 16, SEQ - WINDOW), WINDOW)

    def both(x):
        zero = jnp.zeros_like(x)
        return jnp.concatenate([jnp.where(head_of_lane == 0, x, zero), jnp.where(head_of_lane == 1, x, zero)], axis=0)

    def merge(x):
        return jnp.where(head_of_lane == 0, x[:WINDOW], x[WINDOW:])

    attl[...] = jnp.zeros_like(attl)

    def window_masks(j, r):
        own = seg_col[r, :]
        first = 2.0 * j
        mine = (own >= first) & (own < first + 2.0)
        other = jnp.transpose(jnp.where(mine, own, -1.0))
        pair = jnp.concatenate([own, own], axis=1) == jnp.concatenate([other, other], axis=1)
        return mine, pair

    def keep_own(mine, ref, r, lanes, value):
        ref[r, lanes] = jnp.where(mine, value, ref[r, lanes].astype(FULL)).astype(LOW)

    def attend(j, carry):
        r = window_rows(j)
        mine, pair = window_masks(j, r)
        for g in range(HEADS // 2):
            lanes = slice(g * LANES, (g + 1) * LANES)
            q2 = both(qkv[r, lanes])
            keys = qkv[r, D + g * LANES : D + (g + 1) * LANES]
            values = qkv[r, 2 * D + g * LANES : 2 * D + (g + 1) * LANES]
            scores = jnp.where(pair, dot_nt(keys, q2) * SCORE_SCALE, MASK_FILL)
            e = jnp.exp(scores - jnp.max(scores, axis=0, keepdims=True))
            p = jnp.where(pair, e * (1.0 / jnp.sum(e, axis=0, keepdims=True)), 0.0).astype(LOW)
            probs[j, g] = p
            keep_own(mine, attl, r, lanes, merge(dot_tn(p, values)))
        return carry

    loop(WINDOWS, attend, None, 0.28)

    def feed(i, carry):
        r = tile_rows(i)
        middle = x0[r, :] + dot(attl[r, :], wproj[0]) + vec(0, 4)
        unit, inverse = normalise(middle)
        unit_b[r, :] = unit
        inv_b[r, :] = jnp.broadcast_to(inverse, (ROWS, LANES))
        h = (unit * vec(0, 5) + vec(0, 6)).astype(LOW)
        h_b[r, :] = h
        for c in range(4):
            lanes = slice(c * D, (c + 1) * D)
            value, steep = gelu_parts(dot(h, wfc1[0, :, lanes]) + vecs[0, 7:8, lanes])
            act[r, lanes] = value.astype(LOW)
            slope[r, lanes] = steep.astype(LOW)
        x1[r, :] = middle + dot(act[r, :], wfc2[0]) + vec(0, 8)
        return carry

    rolled(SEQ // ROWS, feed, None, 4.0)

    plan.until(2)
    take_layer(1, b1)
    plan.spend(1.5)
    unit_c = x0
    h_c = low

    def kv_rows(i, carry):
        r = tile_rows(i)
        unit, inverse = normalise(x1[r, :])
        unit_c[r, :] = unit
        inv_c[r, :] = jnp.broadcast_to(inverse, (ROWS, LANES))
        h = (unit * vec(1, 0) + vec(1, 1)).astype(LOW)
        h_c[r, :] = h
        bias = jnp.concatenate([jnp.zeros((1, D), FULL), vec(1, 3)], axis=1)
        kv[r, :] = (dot(h, wqkv[1, :, D:]) + bias).astype(LOW)
        return carry

    rolled(SEQ // ROWS, kv_rows, None, 0.6)

    h_s = dot(picker_low, h_c[...]).astype(LOW)
    x_s = sum(dot(picker_low, part) for part in exact_parts(x1[...]))
    q_s = (dot(h_s, wqkv[1, :, :D]) + vec(1, 2)).astype(LOW)
    stack_rows = lax.broadcasted_iota(jnp.int32, (HEADS * PICKED, 1), 0)
    stack_lanes = lax.broadcasted_iota(jnp.int32, (1, D), 1)
    own_head = (stack_rows // PICKED) == (stack_lanes // HEAD_DIM)

    def stack(x):
        tall = jnp.concatenate([x.astype(FULL)] * HEADS, axis=0)
        return jnp.where(own_head, tall, 0.0).astype(LOW)

    def unstack(x):
        x = jnp.where(own_head, x, 0.0)
        total = x[:PICKED]
        for h in range(1, HEADS):
            total += x[h * PICKED : (h + 1) * PICKED]
        return total

    q6 = stack(q_s)
    image6 = jnp.concatenate([picked_image] * HEADS, axis=0)
    mask6 = image6 == seg_row
    scores = jnp.where(mask6, dot_nt(q6, kv[:, :D]) * SCORE_SCALE, MASK_FILL)
    e = jnp.exp(scores - jnp.max(scores, axis=-1, keepdims=True))
    p6 = e / jnp.sum(e, axis=-1, keepdims=True)
    p6_low = p6.astype(LOW)
    att_s = unstack(dot(p6_low, kv[:, D:])).astype(LOW)
    mid_s = x_s + dot(att_s, wproj[1]) + vec(1, 4)
    unit_m, inv_m = normalise(mid_s)
    h2_s = (unit_m * vec(1, 5) + vec(1, 6)).astype(LOW)
    act_s, steep_s = gelu_parts(dot(h2_s, wfc1[1]) + vec(1, 7))
    act_s = act_s.astype(LOW)
    x2_s = mid_s + dot(act_s, wfc2[1]) + vec(1, 8)

    unit_f, inv_f = normalise(x2_s)
    summary = (unit_f * final_gain + final_bias).astype(LOW)
    arranged = dot(summary, arrange[...]).astype(LOW)
    logits = head_bias
    spans = []
    for k in range(GROUP):
        at = 2 * CLASSES * k
        block, shift = at // LANES, at % LANES
        blocks = (at + 2 * CLASSES - 1) // LANES - block + 1
        spans.append((block, shift, blocks))
        s_k = arranged[:, k * LANES : k * LANES + GROUPS]
        wide = (HEAD_LANES // LANES + 1) * LANES
        part = dot(s_k, whead[:, block * LANES : block * LANES + wide])
        if shift:
            part = pltpu.roll(part, wide - shift, 1)
        logits = logits + part[:, :HEAD_LANES]
    column = lax.broadcasted_iota(jnp.int32, (PICKED, HEAD_LANES), 1)
    second = picked_row >= IMAGES
    low_end = jnp.where(second, CLASSES, 0)
    valid = (column >= low_end) & (column < low_end + CLASSES)
    live = picked_row < 2 * IMAGES
    target = jnp.zeros((PICKED, 1), jnp.int32)
    for i in range(IMAGES):
        target = jnp.where(picked_row == i, lab[0, i], target)
        target = jnp.where(picked_row == IMAGES + i, CLASSES + tea[0, i], target)
    hit = column == target
    logits = jnp.where(valid, logits, -3e38)
    top = jnp.max(logits, axis=-1, keepdims=True)
    e = jnp.exp(logits - top)
    total = jnp.sum(e, axis=-1, keepdims=True)
    hit_logit = jnp.sum(jnp.where(hit, logits, 0.0), axis=-1, keepdims=True)
    each = jnp.where(live, top + jnp.log(total) - hit_logit, 0.0)
    loss_sum = jnp.sum(each, axis=0, keepdims=True)
    grad_logits = jnp.where(live, (e / total - hit.astype(FULL)) * loss_scale, 0.0)
    grad_low = grad_logits.astype(LOW)
    grad_wide = jnp.concatenate([grad_low.astype(FULL), jnp.zeros((PICKED, LANES), FULL)], axis=1)

    grad_arranged = []
    for k, (block, shift, blocks) in enumerate(spans):
        turned = (pltpu.roll(grad_wide, shift, 1) if shift else grad_wide).astype(LOW)
        turned = turned[:, : blocks * LANES]
        s_k = arranged[:, k * LANES : k * LANES + GROUPS]
        grad_w = dot_tn(s_k, turned)
        for j in range(blocks):
            rows = pl.ds(HEAD_AT + block + j, GROUPS, stride=GROUP_ROWS)
            piece = grad_w[:, j * LANES : (j + 1) * LANES]
            if k and j == 0:
                piece = piece + flat[rows, :]
            flat[rows, :] = piece
        back = dot_nt(turned, whead[:, block * LANES : (block + blocks) * LANES])
        grad_arranged.append(jnp.concatenate([back, jnp.zeros((PICKED, LANES - GROUPS), FULL)], axis=1))
    parts = jnp.concatenate(exact_parts(jnp.concatenate(grad_arranged, axis=1)), axis=0)
    parts = dot_nt(parts, arrange[...])
    grad_summary = parts[:PICKED] + parts[PICKED : 2 * PICKED] + parts[2 * PICKED :]
    put_row(HEAD_BIAS_AT, col_sum(grad_low))
    put_row(FINAL_GAIN_AT, col_sum(grad_summary * unit_f))
    put_row(FINAL_BIAS_AT, col_sum(grad_summary))
    flat[GLOBAL_END:GLOBAL_ALL, :] = jnp.zeros((GLOBAL_ALL - GLOBAL_END, LANES), FULL)
    for gather in gathers:
        gather.drain()
    border = FINAL_GAIN_AT // global_rows
    gather_rows(bg, global_rows, border + 1)
    kept = (border + 1) * global_rows - FINAL_GAIN_AT
    edge[:kept, :] = flat[FINAL_GAIN_AT : FINAL_GAIN_AT + kept, :]
    plan.spend(6.0)
    scatter_g.start(0)

    dx_s = norm_back(grad_summary, final_gain, unit_f, inv_f)

    out_s = dx_s.astype(LOW)
    for c in range(4):
        put(FC2_AT, c * D, D, dot_tn(act_s[:, c * D : (c + 1) * D], out_s))
    put_row(FC2_BIAS_AT, col_sum(out_s))
    gpre_s = (dot_nt(out_s, wfc2[1]) * steep_s).astype(LOW)
    put(FC1_AT, 0, FF, dot_tn(h2_s, gpre_s))
    put_row(FC1_BIAS_AT, col_sum(gpre_s))
    gh2_s = dot_nt(gpre_s, wfc1[1])
    put_row(MID_GAIN_AT, col_sum(gh2_s * unit_m))
    put_row(MID_BIAS_AT, col_sum(gh2_s))
    gmid_s = dx_s + norm_back(gh2_s, vec(1, 5), unit_m, inv_m)
    gmid_low = gmid_s.astype(LOW)
    put(PROJ_AT, 0, D, dot_tn(att_s, gmid_low))
    put_row(PROJ_BIAS_AT, col_sum(gmid_low))
    plan.spend(1.0)
    gatt6 = stack(dot_nt(gmid_low, wproj[1]).astype(LOW))
    gprob = dot_nt(gatt6, kv[:, D:])
    gscore = (p6 * (gprob - jnp.sum(p6 * gprob, axis=-1, keepdims=True))).astype(LOW)
    gq_s = (unstack(dot(gscore, kv[:, :D])) * SCORE_SCALE).astype(LOW)
    gkeys = (dot_tn(gscore, q6) * SCORE_SCALE).astype(LOW)
    gvalues = dot_tn(p6_low, gatt6).astype(LOW)
    put_row(QUERY_BIAS_AT, col_sum(gq_s))
    put_row(VALUE_BIAS_AT, col_sum(gvalues))
    kv[:, :D] = gkeys
    kv[:, D:] = gvalues
    plan.spend(2.2)
    put(QKV_AT, 0, 3 * D, dot_tn(h_s, gq_s))
    put(QKV_AT, 0, 3 * D, dot_tn(h_c[...], kv[:, :D]), 3)
    put(QKV_AT, 0, 3 * D, dot_tn(h_c[...], kv[:, D:]), 6)
    back_s = jnp.concatenate([dot_nt(gq_s, wqkv[1, :, :D]), gmid_s], axis=1)

    back_parts = jnp.concatenate(exact_parts(back_s), axis=0)
    dx = x1

    def kv_back(i, carry):
        gain_sum, bias_sum = carry
        r = tile_rows(i)
        image_col = seg_col[r, 0:1]
        place_col = pos_col[r, 0:1]
        lane = lax.broadcasted_iota(jnp.int32, (1, PICKED), 1).astype(FULL)
        lane_image = jnp.where(lane < IMAGES, lane, lane - IMAGES)
        lane_place = jnp.where(lane < IMAGES, float(TABLE), TABLE + 1.0)
        back_pick = (
            (image_col == lane_image) & (place_col == lane_place) & (lane < 2.0 * IMAGES)
        ).astype(LOW)
        back = dot(jnp.concatenate([back_pick] * 3, axis=1), back_parts)
        grad = back[:, :D] + dot_nt(kv[r, :], wqkv[1, :, D:])
        unit = unit_c[r, :]
        dx[r, :] = back[:, D:] + norm_back(grad, vec(1, 0), unit, inv_c[r, 0:1])
        return gain_sum + col_sum(grad * unit), bias_sum + col_sum(grad)

    zero_row = jnp.zeros((1, D), FULL)
    gain_sum, bias_sum = rolled(SEQ // ROWS, kv_back, (zero_row, zero_row), 0.4)
    put_row(PRE_GAIN_AT, gain_sum)
    put_row(PRE_BIAS_AT, bias_sum)
    flat[LAYER_END:, :] = jnp.zeros((LAYER_ALL - LAYER_END, LANES), FULL)
    gather_rows(b1, layer_rows)
    plan.spend(1.5)
    scatter_1.start(0)

    def feed_back(i, carry):
        fc1_sum, fc2_sum, proj_sum, gain_sum, bias_sum = carry
        r = tile_rows(i)
        grad_out = dx[r, :]
        out_low = grad_out.astype(LOW)
        low[r, :] = out_low
        for c in range(4):
            lanes = slice(c * D, (c + 1) * D)
            slope[r, lanes] = (dot_nt(out_low, wfc2[0, lanes, :]) * slope[r, lanes].astype(FULL)).astype(LOW)
        grad_h = dot_nt(slope[r, :], wfc1[0])
        unit = unit_b[r, :]
        middle = grad_out + norm_back(grad_h, vec(0, 5), unit, inv_b[r, 0:1])
        dx[r, :] = middle
        middle_low = middle.astype(LOW)
        h2low[r, :] = middle_low
        gatt[r, :] = dot_nt(middle_low, wproj[0]).astype(LOW)
        return (
            fc1_sum + col_sum(slope[r, :]), fc2_sum + col_sum(out_low), proj_sum + col_sum(middle_low),
            gain_sum + col_sum(grad_h * unit), bias_sum + col_sum(grad_h),
        )

    h2low = kv.at[:, 0:D]
    gatt = kv.at[:, D : 2 * D]
    sums = rolled(SEQ // ROWS, feed_back, (jnp.zeros((1, FF), FULL),) + (zero_row,) * 4, 2.3)
    for at, value in zip((FC1_BIAS_AT, FC2_BIAS_AT, PROJ_BIAS_AT, MID_GAIN_AT, MID_BIAS_AT), sums):
        put_row(at, value)


    def feed_weights(c, carry):
        lanes = pl.ds(pl.multiple_of(c * D, D), D)
        put(FC2_AT, c * D, D, dot_tn(act[:, lanes], low[...]))
        put(FC1_AT, 0, FF, dot_tn(h_b[...], slope[:, lanes]), 3 * c)
        return carry

    rolled(4, feed_weights, None, 0.5)
    put(PROJ_AT, 0, D, dot_tn(attl[...], h2low[...]))
    flat[LAYER_END:, :] = jnp.zeros((LAYER_ALL - LAYER_END, LANES), FULL)
    gather_rows(b0, layer_rows, first_early)
    plan.spend(1.6)
    scatter_0.start(0)

    def attend_back(j, carry):
        r = window_rows(j)
        mine, _ = window_masks(j, r)
        for g in range(HEADS // 2):
            lanes = slice(g * LANES, (g + 1) * LANES)
            key_lanes = slice(D + g * LANES, D + (g + 1) * LANES)
            value_lanes = slice(2 * D + g * LANES, 2 * D + (g + 1) * LANES)
            q2 = both(qkv[r, lanes])
            go2 = both(gatt[r, lanes])
            keys = qkv[r, key_lanes]
            p_low = probs[j, g]
            p = p_low.astype(FULL)
            gp = dot_nt(qkv[r, value_lanes], go2)
            gs = (p * (gp - jnp.sum(p * gp, axis=0, keepdims=True))).astype(LOW)
            keep_own(mine, qkv, r, lanes, merge(dot_tn(gs, keys)) * SCORE_SCALE)
            keep_own(mine, qkv, r, key_lanes, dot(gs, q2) * SCORE_SCALE)
            keep_own(mine, qkv, r, value_lanes, dot(p_low, go2))
        return carry

    loop(WINDOWS, attend_back, None, 0.7)

    def qkv_cast(i, carry):
        query_sum, value_sum = carry
        r = tile_rows(i)
        held = seg_col[r, 0:1] < float(IMAGES)
        grads = jnp.where(held, qkv[r, :].astype(FULL), 0.0)
        qkv[r, :] = grads.astype(LOW)
        return query_sum + col_sum(grads[:, :D]), value_sum + col_sum(grads[:, 2 * D :])

    query_sum, value_sum = rolled(SEQ // ROWS, qkv_cast, (zero_row, zero_row), 0.2)
    put_row(QUERY_BIAS_AT, query_sum)
    put_row(VALUE_BIAS_AT, value_sum)

    def qkv_weights(c, carry):
        put(QKV_AT, 0, 3 * D, dot_tn(h_a[...], qkv[:, pl.ds(pl.multiple_of(c * D, D), D)]), 3 * c)
        return carry

    lax.fori_loop(0, 3, qkv_weights, 0)
    gather_rows(b0, layer_rows, 0, first_early)
    plan.spend(1.2)
    scatter_0.start(1)

    def qkv_back(i, carry):
        gain_sum, bias_sum, embed_sum = carry
        r = tile_rows(i)
        grad = dot_nt(qkv[r, :], wqkv[0])
        unit = unit_a[r, :]
        full = dx[r, :] + norm_back(grad, vec(0, 0), unit, inv_a[r, 0:1])
        dx[r, :] = full
        place = pos_col[r, 0:1]
        pixel = jnp.where(place < TABLE, full, 0.0).astype(LOW)
        low[r, :] = pixel
        return gain_sum + col_sum(grad * unit), bias_sum + col_sum(grad), embed_sum + col_sum(pixel)

    gain_sum, bias_sum, embed_sum = rolled(SEQ // ROWS, qkv_back, (zero_row,) * 3, 1.0)
    put_row(PRE_GAIN_AT, gain_sum)
    put_row(PRE_BIAS_AT, bias_sum)
    gather_rows(b0, layer_rows, *vector_blocks)
    plan.spend(0.1)
    scatter_0.start(2)

    for c in range(2):
        put(PATCH_AT, c * D, D, dot_tn(pat[:, c * D : (c + 1) * D], low[...]))
    place_col = pos_col[:, 0:1]
    onehot = onehot_of(place_col)
    high = dx[...].astype(LOW)
    rest = (dx[...] - high.astype(FULL)).astype(LOW)
    table = dot_tn(onehot, high) + dot_tn(onehot, rest)
    put(POS_AT, 0, D, table[: TABLE + 2])
    put_row(PATCH_BIAS_AT, embed_sum)
    flat[FINAL_GAIN_AT : FINAL_GAIN_AT + kept, :] = edge[:kept, :]
    gather_rows(bg, global_rows, 0, border + 1)
    plan.spend(1.5)
    scatter_g.start(1)
    plan.until()

    squares = jnp.zeros((1, 1), FULL)
    for ref in (new_l, new_g):
        used = ref[...]
        squares += jnp.sum(jnp.sum(used * used, axis=0, keepdims=True), axis=1, keepdims=True)
    row = lax.broadcasted_iota(jnp.int32, (8, LANES), 0)
    tile = jnp.where(row == 0, squares, loss_sum)
    shared[...] = add_over_slice(place, tile, tiles, tile_send, tile_recv)
    for scatter in scatters:
        scatter.drain()


def padded(rows):
    return rows + -rows % 16


def step_call(place, loss_scale, pat, pos, seg, lab, tea, lm, gm):
    vmem = pl.BlockSpec(memory_space=pltpu.VMEM)
    smem = pl.BlockSpec(memory_space=pltpu.SMEM)
    n, nz = place.n, place.nz
    rows = padded(lm.shape[0] // 2), padded(lm.shape[0] // 2), padded(gm.shape[0])

    def shape(*dims, kind=FULL):
        return pltpu.VMEM(dims, kind)

    def low(*dims):
        return pltpu.VMEM(dims, LOW)

    scratch = [low(n, 2, nz, n, r, LANES) for r in rows]
    for r in rows:
        scratch += [
            low(n, nz, n, r, LANES), low(n - 1, n, nz, r, LANES), low(n - 1, nz, r, LANES), low(nz - 1, r, LANES)
        ]
    tiles = 2 * nz + n * n
    scratch += [
        shape(LAYER_ALL, LANES), shape(gm.shape[0] + 8, LANES), shape(rows[0], LANES), low(D, GROUP * LANES),
        low(2, D, 3 * D), low(2, D, D), low(2, D, FF), low(2, FF, D),
        low(PATCH, D), low(256, D), low(GROUPS, (GROUP_ROWS + 1) * LANES),
        shape(2, 16, FF),
        shape(SEQ, LANES), shape(SEQ, LANES),
        shape(SEQ, D), shape(SEQ, LANES), low(SEQ, D),
        shape(SEQ, D), shape(SEQ, LANES), low(SEQ, D),
        low(SEQ, 3 * D), low(WINDOWS, HEADS // 2, WINDOW, 2 * WINDOW),
        low(SEQ, D), shape(SEQ, D), shape(SEQ, D),
        low(SEQ, FF), low(SEQ, FF), low(SEQ, 2 * D), low(SEQ, D), shape(SEQ, LANES),
        low(SEQ, PATCH), pltpu.SemaphoreType.DMA, shape(tiles, 8, LANES),
        pltpu.SemaphoreType.DMA((6,)),
        pltpu.SemaphoreType.DMA((3, nz + nz * n + 2 * n)), pltpu.SemaphoreType.DMA((3, 2 * n * n * nz + n * nz + nz)),
        pltpu.SemaphoreType.DMA((2,)), pltpu.SemaphoreType.DMA((2,)),
    ]
    return pl.pallas_call(
        functools.partial(step_kernel, place, loss_scale),
        out_shape=[jax.ShapeDtypeStruct(a, FULL) for a in (lm.shape, gm.shape, (8, LANES))],
        in_specs=[pl.BlockSpec(memory_space=pl.ANY)] + [vmem] * 2 + [smem] * 2 + [vmem] * 2,
        out_specs=[vmem] * 3,
        scratch_shapes=scratch,
        compiler_params=pltpu.CompilerParams(collective_id=0, has_side_effects=True, vmem_limit_bytes=VMEM_BYTES),
    )(pat, pos, seg, lab, tea, lm, gm)

def adam_kernel(total, gl, gg, lm, lo, ls, gm, go, gs, *outs):
    norm = jnp.sqrt(total[0:1, 0:1])
    factor = jnp.minimum(1.0, CLIP_NORM / norm)
    fix_one = 1.0 - BETA_ONE**STEP
    fix_two = 1.0 - BETA_TWO**STEP
    for at, (grad, master, moment, second) in ((0, (gl, lm, lo, ls)), (3, (gg, gm, go, gs))):
        clipped = grad[...] * factor
        new_moment = BETA_ONE * moment[...] + (1.0 - BETA_ONE) * clipped
        new_second = BETA_TWO * second[...] + (1.0 - BETA_TWO) * clipped * clipped
        old = master[...]
        update = new_moment / fix_one / (jnp.sqrt(new_second / fix_two) + ADAM_EPS) + WEIGHT_DECAY * old
        outs[at][...] = old - LEARN_RATE * update
        outs[at + 1][...] = new_moment
        outs[at + 2][...] = new_second
    outs[6][0, 0] = norm[0, 0]
    outs[7][0, 0] = total[1, 0]


def interleave(x):
    rows = x.shape[1] // LANES
    return x.reshape(2, rows, LANES).transpose(1, 0, 2).reshape(2 * rows, LANES)


def layers_apart(x):
    rows = x.shape[0] // 2
    return x.reshape(rows, 2, LANES).transpose(1, 0, 2).reshape(2, rows * LANES)


def shards(sizes, pat, pos, seg, lab, tea, lm, lo, ls, gm, go, gs):
    place = Place(sizes)
    count = sizes[0] * sizes[1]
    assert pat.shape[0] == 1 and lm.shape[1] * count == LAYER_ALL * LANES and gm.shape[0] * count == GLOBAL_ALL * LANES
    lm, lo, ls = interleave(lm), interleave(lo), interleave(ls)
    gm, go, gs = gm.reshape(-1, LANES), go.reshape(-1, LANES), gs.reshape(-1, LANES)
    gl, gg, total = step_call(place, 1.0 / (2 * IMAGES * count), pat[0], pos, seg, lab, tea, lm, gm)
    vmem, smem = pl.BlockSpec(memory_space=pltpu.VMEM), pl.BlockSpec(memory_space=pltpu.SMEM)
    shapes = [lm.shape] * 3 + [gm.shape] * 3 + [(1, 1)] * 2
    *new, norm, loss = pl.pallas_call(
        adam_kernel,
        out_shape=[jax.ShapeDtypeStruct(x, FULL) for x in shapes],
        out_specs=[vmem] * 6 + [smem] * 2,
        compiler_params=pltpu.CompilerParams(vmem_limit_bytes=VMEM_BYTES),
    )(total, gl, gg, lm, lo, ls, gm, go, gs)
    return tuple(layers_apart(x) for x in new[:3]) + tuple(x.reshape(-1) for x in new[3:]) + (norm.reshape(()), loss.reshape(()))


def solution(mesh):
    axes = tuple(mesh.axis_names)
    split = P(axes)
    wide = P(None, axes)
    return jax.shard_map(
        functools.partial(shards, tuple(mesh.shape[a] for a in axes)),
        mesh=mesh,
        in_specs=(split,) * 5 + (wide,) * 3 + (split,) * 3,
        out_specs=(wide,) * 3 + (split,) * 3 + (P(), P()),
        check_vma=False,
    )
```
